32 devices in a mesh: seq: 16 (over z, y, x), wt: 2 (over core).
Axes of the slice: x: 2, y: 2, z: 4, core: 2. Of those that a mesh axis runs over, the one named last changes fastest.
Arguments:
- x_in: bfloat16 [8192, 1024], P(('seq', 'wt')), may hold values from -6 to 6
- cotangent: bfloat16 [8192, 1024], P(('seq', 'wt')), may hold values from -6 to 6
- seq_lengths: int32 [4], replicated, may hold values from 1 to 4096, 8192 in all
- weights: float32 [4480, 4096], P(('seq', 'wt')), may hold values from -0.125 to 0.125
- momentum: float32 [4480, 4096], P(('seq', 'wt')), may hold values from -512 to 512
- left_stat: float32 [4480, 4096], P(('seq', 'wt')), may hold values from -524288 to 2097152
- right_stat: float32 [4480, 4096], P(('seq', 'wt')), may hold values from -524288 to 2097152
- left_root: float32 [4480, 4096], P(('seq', 'wt')), may hold values from -0.03716272 to 0.14865089
- right_root: float32 [4480, 4096], P(('seq', 'wt')), may hold values from -0.03716272 to 0.14865089
- vectors: float32 [5, 1024], replicated, may hold values from -2 to 2
- vector_sq: float32 [5, 1024], replicated, may hold values from 8192 to 32768
Outputs:
- out_act: bfloat16 [8192, 1024], P(('seq', 'wt'))
- in_grad: float32 [8192, 1024], P(('seq', 'wt'))
- new_weights: float32 [4480, 4096], P(('seq', 'wt'))
- weight_copy: bfloat16 [4480, 4096], P(('seq', 'wt'))
- new_momentum: float32 [4480, 4096], P(('seq', 'wt'))
- new_left: float32 [4480, 4096], P(('seq', 'wt'))
- new_right: float32 [4480, 4096], P(('seq', 'wt'))
- vector_grads: float32 [5, 1024], replicated
- new_vector_sq: float32 [5, 1024], replicated
- new_vectors: float32 [5, 1024], replicated
The draws below stay inside these ranges and needn't reach their ends.
Inputs may be any that keep to these rules, and one draw needn't show every extreme that they name: `seq_lengths`: the longest of the 4 lengths is exactly 4096.
All inputs are finite; a program needn't handle non-finite values.
Results may differ from the reference program's by a relative error of at most 0.011.
Values may be sent and summed in bfloat16 or wider, within the bound.
No kernel may reach another device: no remote copies, remote signals or barrier semaphores. Data moves between devices by JAX's collectives and lax.ppermute only.
A program may use at most 576 MiB of HBM per device.

```python
import math
from functools import partial
import jax
import jax.numpy as jnp
import numpy as np
from jax import lax

D = 1024
FF = 4608
SEQS = 4
BS = 64
TOKENS = 8192
BLOCKS = 4480


def dominant_blocks(key, diag_scale):
    diag_key, size_key, sign_key = jax.random.split(key, 3)
    diagonal = jnp.exp(jax.random.uniform(diag_key, (BLOCKS, BS), jnp.float32, 0.0, math.log(4.0)))
    magnitude = jax.random.uniform(size_key, (BLOCKS, BS, BS), jnp.float32, 0.5, 1.0) * (0.95 / BS)
    sign_values = jnp.where(jax.random.bernoulli(sign_key, 0.5, (BLOCKS, BS, BS)), 1.0, -1.0).astype(jnp.float32)
    upper_part = jnp.triu(magnitude * sign_values, 1)
    identity = jnp.eye(BS, dtype=jnp.float32)
    blocks = diag_scale * (upper_part + jnp.swapaxes(upper_part, 1, 2) + diagonal[:, :, None] * identity)
    return blocks.reshape(BLOCKS, BS * BS)


def draw_weights(key, part):
    key = jax.random.fold_in(key, 11)
    per_block = BS * BS
    up_end = (4 * D * D + 2 * D * FF) // per_block
    block_ids = jnp.arange(BLOCKS, dtype=jnp.int32)
    block_scale = jnp.where(block_ids >= up_end, FF ** (-0.5), D ** (-0.5)).astype(jnp.float32)
    normal_draw = jnp.clip(jax.random.normal(key, (BLOCKS, BS * BS), jnp.float32), -4.0, 4.0)
    return normal_draw * block_scale[:, None]


def draw_left_stat(key, part):
    key = jax.random.fold_in(key, 12)
    return dominant_blocks(key, float(BS * TOKENS))


def draw_right_stat(key, part):
    key = jax.random.fold_in(key, 13)
    return dominant_blocks(key, float(BS * TOKENS))


def draw_left_root(key, part):
    key = jax.random.fold_in(key, 14)
    return dominant_blocks(key, float(BS * TOKENS) ** (-0.25))


def draw_right_root(key, part):
    key = jax.random.fold_in(key, 15)
    return dominant_blocks(key, float(BS * TOKENS) ** (-0.25))


def draw_vectors(key, part):
    key = jax.random.fold_in(key, 16)
    gain_key, tap_key = jax.random.split(key)
    gain_rows = 1.0 + 0.1 * jnp.clip(jax.random.normal(gain_key, (2, D), jnp.float32), -4.0, 4.0)
    tap_rows = 0.5 * jnp.clip(jax.random.normal(tap_key, (3, D), jnp.float32), -4.0, 4.0)
    return jnp.concatenate([gain_rows, tap_rows], axis=0)


def block_levels(rng, extent, cuts, least, largest):
    level = 1.0
    for dim, parts in cuts:
        heights = jax.random.uniform(jax.random.fold_in(jax.random.fold_in(rng, 6), dim), (parts,), jnp.float32, least / len(cuts), largest / len(cuts))
        level = level * jnp.repeat(jnp.exp(heights), extent[dim] // parts).reshape((-1,) + (1,) * (len(extent) - 1 - dim))
    return level


def length_profile(number_of, total, reach, lean):
    weights = [(1 << 20) // math.isqrt(standing ** lean) + 1 for standing in range(2, number_of + 1)]
    surplus, holding = total - reach - (number_of - 1), [1] * (number_of - 1)
    while surplus > 0:
        candidates = [i for i in range(number_of - 1) if holding[i] < reach]
        mass, remaining = sum([weights[i] for i in candidates]), surplus
        for i in candidates:
            more = min(reach - holding[i], max(1, remaining * weights[i] // mass), surplus)
            holding[i] = holding[i] + more
            surplus = surplus - more
    return np.array([reach] + holding)


def ragged_sizes(rng, number_of, total, bound, skew):
    if number_of == 2:
        one = jax.random.randint(rng, (), max(1, total - bound), min(bound, total - 1) + 1)
        return jnp.stack([one, total - one])
    tallies = jnp.asarray(length_profile(number_of, total, bound, skew), jnp.int32)
    couples = (number_of - 1) // 2
    donor, sink = tallies[1:1 + 2 * couples:2], tallies[2:2 + 2 * couples:2]
    margin = jnp.minimum(donor - 1, bound - sink)
    moved = jax.random.randint(jax.random.fold_in(rng, 1), (couples,), 0, 1 << 20) % (margin + 1)
    tallies = tallies.at[1:1 + 2 * couples:2].set(donor - moved).at[2:2 + 2 * couples:2].set(sink + moved)
    return tallies[jax.random.permutation(jax.random.fold_in(rng, 2), number_of)]


def normal_values(stream_key, shape, spread, bound, shards=(), held_as=jnp.bfloat16):
    gain = block_levels(stream_key, shape, shards, -0.22, 0.18) if shards else 1.0
    drawn = jax.random.normal(stream_key, shape, jnp.float32) * spread * gain
    return jnp.minimum(jnp.maximum(drawn, -bound), bound).astype(held_as)


def setup_inputs(seed: int = 0) -> dict:
    keys = jax.random.split(jax.random.key(seed), 12)
    return {
        "x_in": normal_values(keys[0], (TOKENS, D), 1.0, 6.0, ((0, 32),)),
        "cotangent": normal_values(keys[1], (TOKENS, D), 1.0, 6.0, ((0, 32),)),
        "seq_lengths": ragged_sizes(keys[2], SEQS, TOKENS, TOKENS // 2, 0).astype(jnp.int32),
        "weights": draw_weights(jax.random.fold_in(keys[11], 71), 0),
        "momentum": normal_values(keys[4], (BLOCKS, BS * BS), (TOKENS ** 0.5), 512.0, ((0, 32),), jnp.float32),
        "left_stat": draw_left_stat(jax.random.fold_in(keys[11], 71), 0),
        "right_stat": draw_right_stat(jax.random.fold_in(keys[11], 71), 0),
        "left_root": draw_left_root(jax.random.fold_in(keys[11], 71), 0),
        "right_root": draw_right_root(jax.random.fold_in(keys[11], 71), 0),
        "vectors": draw_vectors(jax.random.fold_in(keys[11], 71), 0),
        "vector_sq": jnp.clip(jnp.exp(jax.random.uniform(keys[10], (5, D), jnp.float32, math.log(8192.0), math.log(32768.0))), 8192.0, 32768.0),
    }


@jax.custom_vjp
def low(v):
    return lax.optimization_barrier(v.astype(jnp.bfloat16)).astype(jnp.float32)

@jax.custom_vjp
def low_back(v):
    return v

def low_keep(v):
    return (low(v), None)

def low_pass(kept, grad):
    return (grad,)

def back_keep(v):
    return (v, None)

def back_low(kept, grad):
    return (low(grad),)
low.defvjp(low_keep, low_pass)
low_back.defvjp(back_keep, back_low)
NORM_EPS = 1e-05
MEAN_EPS = 1e-06
DECAY = 0.5
MOMENT = 0.9
RATE = 0.01
VEC_RATE = 0.25
HIGHEST = lax.Precision.HIGHEST

def unpack_blocks(blocks, row_count, col_count):
    return blocks.reshape(row_count // BS, col_count // BS, BS, BS).transpose(0, 2, 1, 3).reshape(row_count, col_count)

def block_bounds():
    per_block = BS * BS
    in_end = 3 * D * D // per_block
    out_end = in_end + D * D // per_block
    gate_end = out_end + D * FF // per_block
    up_end = gate_end + D * FF // per_block
    return (in_end, out_end, gate_end, up_end)

def matrices(blocks):
    in_end, out_end, gate_end, up_end = block_bounds()
    w_in = unpack_blocks(blocks[:in_end], D, 3 * D)
    w_out = unpack_blocks(blocks[in_end:out_end], D, D)
    w_gate = unpack_blocks(blocks[out_end:gate_end], D, FF)
    w_up = unpack_blocks(blocks[gate_end:up_end], D, FF)
    w_down = unpack_blocks(blocks[up_end:], FF, D)
    return (w_in, w_out, w_gate, w_up, w_down)

def product(left_side, right_side):
    return jnp.dot(left_side, right_side, precision=HIGHEST, preferred_element_type=jnp.float32)

def rms_scale(values):
    return lax.rsqrt(lax.optimization_barrier(jnp.mean(values * values, axis=-1, keepdims=True)) + NORM_EPS)

def keep_masks(places, seq_lengths):
    ends = jnp.cumsum(seq_lengths).astype(jnp.int32)
    starts = lax.optimization_barrier(jnp.max(jnp.where(ends[None, :] <= places[:, None], ends[None, :], 0), axis=1))
    keep_one = (places - 1 >= starts).astype(jnp.float32)[:, None]
    keep_two = (places - 2 >= starts).astype(jnp.float32)[:, None]
    return (keep_one, keep_two)

def layer_block(weight_set, vector_rows, carried, inputs):
    w_in, w_out, w_gate, w_up, w_down = weight_set
    hidden_in, keep_one, keep_two = inputs
    normed = low(hidden_in * rms_scale(hidden_in) * vector_rows[0])
    mixed = low_back(product(normed, w_in))
    input_gate = mixed[:, :D]
    output_gate = mixed[:, D:2 * D]
    values = mixed[:, 2 * D:]
    driven = input_gate * values
    extended = jnp.concatenate([carried, driven], axis=0)
    conv_out = vector_rows[4] * driven + vector_rows[3] * keep_one * extended[1:-1] + vector_rows[2] * keep_two * extended[:-2]
    gated_out = low(output_gate * conv_out)
    branch = low_back(product(gated_out, w_out))
    middle = hidden_in + branch
    normed_two = low(middle * rms_scale(middle) * vector_rows[1])
    gate_ff = low_back(product(normed_two, w_gate))
    up_ff = low_back(product(normed_two, w_up))
    activated = low(jax.nn.silu(gate_ff) * up_ff)
    result = middle + product(activated, w_down)
    return (extended[-2:], result)

def forward_pass(blocks, vector_rows, activations, keep_one, keep_two):
    weight_set = matrices(low(blocks))
    block_rows = min(4096, TOKENS)
    block_count = TOKENS // block_rows
    pieces = (activations.reshape(block_count, block_rows, D), keep_one.reshape(block_count, block_rows, 1), keep_two.reshape(block_count, block_rows, 1))
    block_step = jax.checkpoint(partial(layer_block, weight_set, vector_rows))
    last_state, outputs = lax.scan(block_step, jnp.zeros((2, D), jnp.float32), pieces)
    return outputs.reshape(TOKENS, D)

def reference(x_in, cotangent, seq_lengths, weights, momentum, left_stat, right_stat, left_root, right_root, vectors, vector_sq):
    weights = weights.reshape(BLOCKS, BS, BS)
    momentum = momentum.reshape(BLOCKS, BS, BS)
    left_stat = left_stat.reshape(BLOCKS, BS, BS)
    right_stat = right_stat.reshape(BLOCKS, BS, BS)
    left_root = left_root.reshape(BLOCKS, BS, BS)
    right_root = right_root.reshape(BLOCKS, BS, BS)
    places = jnp.arange(TOKENS, dtype=jnp.int32)
    keep_one, keep_two = keep_masks(places, seq_lengths)

    def wrapped(blocks, vector_rows, activations):
        return forward_pass(blocks, vector_rows, activations, keep_one, keep_two)
    result, pullback = jax.vjp(wrapped, weights, vectors, x_in.astype(jnp.float32))
    summed, vector_grads, in_grad = pullback(cotangent.astype(jnp.float32))
    new_left = DECAY * left_stat + (1.0 - DECAY) * jnp.einsum('kij,klj->kil', summed, summed, precision=HIGHEST)
    new_right = DECAY * right_stat + (1.0 - DECAY) * jnp.einsum('kji,kjl->kil', summed, summed, precision=HIGHEST)
    new_momentum = MOMENT * momentum + summed
    precond = jnp.einsum('kij,kjl->kil', left_root, new_momentum, precision=HIGHEST)
    precond = jnp.einsum('kij,kjl->kil', precond, right_root, precision=HIGHEST)
    square = lax.optimization_barrier(jnp.sum(precond * precond, axis=(1, 2)))
    in_end, out_end, gate_end, up_end = block_bounds()
    block_ids = jnp.arange(BLOCKS, dtype=jnp.int32)
    kind_index = (block_ids >= in_end).astype(jnp.int32) + (block_ids >= out_end).astype(jnp.int32) + (block_ids >= gate_end).astype(jnp.int32) + (block_ids >= up_end).astype(jnp.int32)
    one_hot = (kind_index[:, None] == jnp.arange(5, dtype=jnp.int32)[None, :]).astype(jnp.float32)
    kind_sum = lax.optimization_barrier(jnp.sum(one_hot * square[:, None], axis=0))
    kind_total = lax.optimization_barrier(jnp.sum(one_hot, axis=0)) * (BS * BS)
    kind_scale = lax.rsqrt(kind_sum / kind_total + MEAN_EPS)
    block_scale = lax.optimization_barrier(jnp.sum(one_hot * kind_scale[None, :], axis=1))
    new_weights = weights - RATE * block_scale[:, None, None] * precond
    weight_copy = new_weights.astype(jnp.bfloat16)
    new_vector_sq = DECAY * vector_sq + (1.0 - DECAY) * vector_grads * vector_grads
    new_vectors = vectors - VEC_RATE * vector_grads * lax.rsqrt(new_vector_sq)
    flat = (BLOCKS, BS * BS)
    return (result.astype(jnp.bfloat16), in_grad, new_weights.reshape(flat), weight_copy.reshape(flat), new_momentum.reshape(flat), new_left.reshape(flat), new_right.reshape(flat), vector_grads, new_vector_sq, new_vectors)
```

```python
import jax
import jax.numpy as jnp
from jax import lax
from jax.sharding import PartitionSpec as P

D = 1024
FF = 4608
BS = 64
BLOCKS = 4480


NORM_EPS = 1e-05
MEAN_EPS = 1e-06
DECAY = 0.5
MOMENT = 0.9
RATE = 0.01
VEC_RATE = 0.25
HIGHEST = lax.Precision.HIGHEST


def from_behind(block, axis, distance):
    devices = range(lax.axis_size(axis))
    route = [(i - distance, i) for i in devices if i - distance in devices]
    return lax.ppermute(block, axis, route)


def unpack_blocks(blocks, row_count, col_count):
    return (
        blocks.reshape(row_count // BS, col_count // BS, BS, BS)
        .transpose(0, 2, 1, 3)
        .reshape(row_count, col_count)
    )


def pack_blocks(matrix):
    row_count, col_count = matrix.shape
    return (
        matrix.reshape(row_count // BS, BS, col_count // BS, BS)
        .transpose(0, 2, 1, 3)
        .reshape(-1, BS * BS)
    )


def block_bounds():
    per_block = BS * BS
    in_end = 3 * D * D // per_block
    out_end = in_end + D * D // per_block
    gate_end = out_end + D * FF // per_block
    up_end = gate_end + D * FF // per_block
    return (in_end, out_end, gate_end, up_end)


def matrices(blocks):
    in_end, out_end, gate_end, up_end = block_bounds()
    w_in = unpack_blocks(blocks[:in_end], D, 3 * D)
    w_out = unpack_blocks(blocks[in_end:out_end], D, D)
    w_gate = unpack_blocks(blocks[out_end:gate_end], D, FF)
    w_up = unpack_blocks(blocks[gate_end:up_end], D, FF)
    w_down = unpack_blocks(blocks[up_end:], FF, D)
    return (w_in, w_out, w_gate, w_up, w_down)


def matmul(left_side, right_side):
    return jnp.dot(left_side, right_side, preferred_element_type=jnp.float32)


def matmul_tn(left_side, right_side):
    return lax.dot_general(
        left_side, right_side, (((0,), (0,)), ((), ())), preferred_element_type=jnp.float32
    )


def matmul_nt(left_side, right_side):
    return lax.dot_general(
        left_side, right_side, (((1,), (1,)), ((), ())), preferred_element_type=jnp.float32
    )


def rms_scale(values):
    return lax.rsqrt(jnp.mean(values * values, axis=-1, keepdims=True) + NORM_EPS)


def norm_back(values, row_scale, norm_gain, grad_normed):
    gain_grad = jnp.sum(grad_normed * values * row_scale, axis=0)
    weighted = grad_normed * norm_gain
    grad_values = row_scale * weighted - values * row_scale**3 * jnp.mean(
        weighted * values, axis=-1, keepdims=True
    )
    return (gain_grad, grad_values)


def keep_masks(places, seq_lengths):
    ends = jnp.cumsum(seq_lengths)
    starts = jnp.max(jnp.where(ends[None, :] <= places[:, None], ends[None, :], 0), axis=1)
    keep_one = (places - 1 >= starts).astype(jnp.float32)[:, None]
    keep_two = (places - 2 >= starts).astype(jnp.float32)[:, None]
    return (keep_one, keep_two)


def weight_grads(operands):
    (
        normed,
        grad_mixed,
        gated_out,
        grad_branch,
        normed_two,
        grad_gate,
        grad_up,
        activated,
        cotangent,
    ) = operands
    return jnp.concatenate(
        [
            pack_blocks(matmul_tn(normed, grad_mixed)),
            pack_blocks(matmul_tn(gated_out, grad_branch)),
            pack_blocks(matmul_tn(normed_two, grad_gate)),
            pack_blocks(matmul_tn(normed_two, grad_up)),
            pack_blocks(matmul_tn(activated, cotangent)),
        ],
        axis=0,
    )


def shards_any(
    x_in,
    cotangent,
    seq_lengths,
    weights,
    momentum,
    left_stat,
    right_stat,
    left_root,
    right_root,
    vectors,
    vector_sq,
):
    gathered = lax.all_gather(weights.astype(jnp.bfloat16), ("seq", "wt"), axis=0, tiled=True)
    w_in, w_out, w_gate, w_up, w_down = matrices(gathered)
    row_count = x_in.shape[0]
    places = lax.axis_index(("seq", "wt")) * row_count + jnp.arange(row_count, dtype=jnp.int32)
    keep_one, keep_two = keep_masks(places, seq_lengths)
    hidden_in = x_in.astype(jnp.float32)
    scale_one = rms_scale(hidden_in)
    normed = (hidden_in * scale_one * vectors[0]).astype(jnp.bfloat16)
    mixed = matmul(normed, w_in)
    input_gate = mixed[:, :D]
    output_gate = mixed[:, D : 2 * D]
    values = mixed[:, 2 * D :]
    driven = input_gate * values
    carried = from_behind(driven[-2:], ("seq", "wt"), 1)
    extended = jnp.concatenate([carried, driven], axis=0)
    conv_out = (
        vectors[4] * driven
        + vectors[3] * keep_one * extended[1:-1]
        + vectors[2] * keep_two * extended[:-2]
    )
    gated_out = (output_gate * conv_out).astype(jnp.bfloat16)
    middle = hidden_in + matmul(gated_out, w_out)
    scale_two = rms_scale(middle)
    normed_two = (middle * scale_two * vectors[1]).astype(jnp.bfloat16)
    gate_ff = matmul(normed_two, w_gate)
    up_ff = matmul(normed_two, w_up)
    sigmoid_gate = jax.nn.sigmoid(gate_ff)
    silu_value = gate_ff * sigmoid_gate
    activated = (silu_value * up_ff).astype(jnp.bfloat16)
    out_act = (middle + matmul(activated, w_down)).astype(jnp.bfloat16)
    grad_act = matmul_nt(cotangent, w_down)
    grad_gate = (grad_act * up_ff * sigmoid_gate * (1.0 + gate_ff * (1.0 - sigmoid_gate))).astype(
        jnp.bfloat16
    )
    grad_up = (grad_act * silu_value).astype(jnp.bfloat16)
    grad_normed_two = matmul_nt(grad_gate, w_gate) + matmul_nt(grad_up, w_up)
    gain_two_grad, middle_term = norm_back(middle, scale_two, vectors[1], grad_normed_two)
    grad_middle = cotangent.astype(jnp.float32) + middle_term
    grad_branch = grad_middle.astype(jnp.bfloat16)
    grad_gated = matmul_nt(grad_branch, w_out)
    grad_output_gate = grad_gated * conv_out
    grad_conv = grad_gated * output_gate
    early_one = keep_one * grad_conv
    early_two = keep_two * grad_conv
    tap_zero = jnp.sum(early_two * extended[:-2], axis=0)
    tap_first = jnp.sum(early_one * extended[1:-1], axis=0)
    tap_second = jnp.sum(grad_conv * driven, axis=0)
    sent_back = jnp.stack(
        [vectors[2] * early_two[0], vectors[3] * early_one[0] + vectors[2] * early_two[1]], axis=0
    )
    from_after = from_behind(sent_back, ("seq", "wt"), -1)
    zero_rows = jnp.zeros((2, D), jnp.float32)
    grad_driven = vectors[4] * grad_conv
    grad_driven = grad_driven + vectors[3] * jnp.concatenate([early_one[1:], zero_rows[:1]], axis=0)
    grad_driven = grad_driven + vectors[2] * jnp.concatenate([early_two[2:], zero_rows], axis=0)
    grad_driven = grad_driven + jnp.concatenate(
        [jnp.zeros((row_count - 2, D), jnp.float32), from_after], axis=0
    )
    grad_mixed = jnp.concatenate(
        [grad_driven * values, grad_output_gate, grad_driven * input_gate], axis=1
    ).astype(jnp.bfloat16)
    grad_normed = matmul_nt(grad_mixed, w_in)
    gain_one_grad, input_term = norm_back(hidden_in, scale_one, vectors[0], grad_normed)
    in_grad = grad_middle + input_term
    paired = (
        lax.all_gather(normed, "wt", axis=0, tiled=True),
        lax.all_gather(grad_mixed, "wt", axis=0, tiled=True),
        lax.all_gather(gated_out, "wt", axis=0, tiled=True),
        lax.all_gather(grad_branch, "wt", axis=0, tiled=True),
        lax.all_gather(normed_two, "wt", axis=0, tiled=True),
        lax.all_gather(grad_gate, "wt", axis=0, tiled=True),
        lax.all_gather(grad_up, "wt", axis=0, tiled=True),
        lax.all_gather(activated, "wt", axis=0, tiled=True),
        lax.all_gather(cotangent, "wt", axis=0, tiled=True),
    )
    pair_grads = weight_grads(paired)
    seq_count = lax.axis_size("seq")
    core_count = lax.axis_size("wt")
    owned_count = pair_grads.shape[0] // (seq_count * core_count)
    arranged = pair_grads.reshape(seq_count, core_count, owned_count, BS * BS)
    mine = lax.dynamic_index_in_dim(arranged, lax.axis_index("wt"), 1, keepdims=False).reshape(
        seq_count * owned_count, BS * BS
    )
    summed_flat = lax.psum_scatter(mine, "seq", scatter_dimension=0, tiled=True)
    vector_part = jnp.stack([gain_one_grad, gain_two_grad, tap_zero, tap_first, tap_second], axis=0)
    local_count = summed_flat.shape[0]
    summed = summed_flat.reshape(local_count, BS, BS)
    left_blocks = left_stat.reshape(local_count, BS, BS)
    right_blocks = right_stat.reshape(local_count, BS, BS)
    momentum_blocks = momentum.reshape(local_count, BS, BS)
    left_factor = left_root.reshape(local_count, BS, BS)
    right_factor = right_root.reshape(local_count, BS, BS)
    new_left = DECAY * left_blocks + (1.0 - DECAY) * jnp.einsum(
        "kij,klj->kil", summed, summed, precision=HIGHEST
    )
    new_right = DECAY * right_blocks + (1.0 - DECAY) * jnp.einsum(
        "kji,kjl->kil", summed, summed, precision=HIGHEST
    )
    new_momentum = MOMENT * momentum_blocks + summed
    precond = jnp.einsum("kij,kjl->kil", left_factor, new_momentum, precision=HIGHEST)
    precond = jnp.einsum("kij,kjl->kil", precond, right_factor, precision=HIGHEST)
    precond_flat = precond.reshape(local_count, BS * BS)
    square = jnp.sum(precond_flat * precond_flat, axis=1)
    in_end, out_end, gate_end, up_end = block_bounds()
    block_ids = lax.axis_index(("seq", "wt")) * local_count + jnp.arange(
        local_count, dtype=jnp.int32
    )
    kind_index = (
        (block_ids >= in_end).astype(jnp.int32)
        + (block_ids >= out_end).astype(jnp.int32)
        + (block_ids >= gate_end).astype(jnp.int32)
        + (block_ids >= up_end).astype(jnp.int32)
    )
    one_hot = (kind_index[:, None] == jnp.arange(5, dtype=jnp.int32)[None, :]).astype(jnp.float32)
    kind_part = jnp.sum(one_hot * square[:, None], axis=0)
    vector_grads, kind_sum = lax.psum((vector_part, kind_part), ("seq", "wt"))
    kind_total = jnp.array(
        [in_end, out_end - in_end, gate_end - out_end, up_end - gate_end, BLOCKS - up_end],
        jnp.float32,
    ) * (BS * BS)
    kind_scale = lax.rsqrt(kind_sum / kind_total + MEAN_EPS)
    block_scale = jnp.sum(one_hot * kind_scale[None, :], axis=1)
    new_weights = weights - RATE * block_scale[:, None] * precond_flat
    weight_copy = new_weights.astype(jnp.bfloat16)
    new_vector_sq = DECAY * vector_sq + (1.0 - DECAY) * vector_grads * vector_grads
    new_vectors = vectors - VEC_RATE * vector_grads * lax.rsqrt(new_vector_sq)
    flat_shape = (local_count, BS * BS)
    return (
        out_act,
        in_grad,
        new_weights,
        weight_copy,
        new_momentum.reshape(flat_shape),
        new_left.reshape(flat_shape),
        new_right.reshape(flat_shape),
        vector_grads,
        new_vector_sq,
        new_vectors,
    )


Z, Y, X = 4, 2, 2
CHIPS, CORES = Z * Y * X, 2
PLANE = Y * X
HALF = BS // 2
SWAP = [(0, 1), (1, 0)]


def chip(z, y, x):
    return (z * Y + y) * X + x


def plane_route(pairs):
    return [(chip(a, y, x), chip(b, y, x)) for a, b in pairs for y in range(Y) for x in range(X)]


ACROSS_X = [(i, i ^ 1) for i in range(CHIPS)]
ACROSS_Y = [(i, i ^ 2) for i in range(CHIPS)]


def send(block, route):
    return lax.ppermute(block, "seq", route)


def to_sibling(block):
    return lax.ppermute(block, "wt", SWAP)


def quad_bounds():
    return tuple(b // 4 for b in block_bounds())


def col_quads(blocks):
    n = blocks.shape[0] // 4
    return (
        blocks.reshape(n, 4, BS, 2, HALF).transpose(3, 0, 2, 1, 4).reshape(2, n, BS, 4 * HALF)
    )


def row_quads(blocks):
    n = blocks.shape[0] // 4
    return (
        blocks.reshape(n, 2, 2, 2, HALF, BS)
        .transpose(3, 0, 1, 4, 2, 5)
        .reshape(2, n, BS, 2 * BS)
    )


def col_blocks(quads):
    n = quads.shape[1]
    return quads.reshape(2, n, BS, 4, HALF).transpose(1, 3, 2, 0, 4).reshape(4 * n, BS, BS)


def row_blocks(quads):
    n = quads.shape[1]
    return quads.reshape(2, n, 2, HALF, 2, BS).transpose(1, 2, 4, 0, 3, 5).reshape(4 * n, BS, BS)


def col_matrix(quads, rows):
    n = quads.shape[0] // rows
    return quads.reshape(rows, n, BS, 128).transpose(0, 2, 1, 3).reshape(rows * BS, n * 128)


def row_matrix(quads, rows):
    n = 2 * quads.shape[0] // rows
    return quads.reshape(rows, n, HALF, 128).transpose(0, 2, 1, 3).reshape(rows * HALF, n * 128)


def matrix_col(matrix):
    rows, n = matrix.shape[0] // BS, matrix.shape[1] // 128
    return matrix.reshape(rows, BS, n, 128).transpose(0, 2, 1, 3).reshape(rows * n, BS, 128)


def matrix_row(matrix):
    rows, n = matrix.shape[0] // HALF, matrix.shape[1] // 128
    return matrix.reshape(rows, HALF, n, 128).transpose(0, 2, 1, 3).reshape(rows * n // 2, BS, 128)


def gather_plane(block, place_x, place_y):
    n = block.shape[0]
    h = n // 2
    from_x = send(block, ACROSS_X)
    from_y = send(block, ACROSS_Y)
    far = jnp.concatenate([send(from_y[:h], ACROSS_X), send(from_x[h:], ACROSS_Y)], axis=0)
    low = jnp.where(place_x == 0, block, from_x)
    high = jnp.where(place_x == 0, from_x, block)
    far_low = jnp.where(place_x == 0, from_y, far)
    far_high = jnp.where(place_x == 0, far, from_y)
    near = jnp.stack([low, high])
    other = jnp.stack([far_low, far_high])
    return jnp.concatenate(
        [jnp.where(place_y == 0, near, other), jnp.where(place_y == 0, other, near)], axis=0
    )


def pick(place, options):
    out = options[0]
    for i, option in enumerate(options[1:], 1):
        out = jnp.where(place == i, option, out)
    return out


def gather_weights(own, z, y, x):
    one = send(own, plane_route([(0, 2), (3, 1)]))
    two = send(
        jnp.where((z == 0) | (z == 3), own, one), plane_route([(0, 1), (2, 3), (3, 2), (1, 0)])
    )
    three = send(own, plane_route([(1, 2), (2, 1)]))
    four = send(own, plane_route([(1, 0), (2, 3)]))
    five = send(three, plane_route([(1, 0), (2, 3)]))
    slots = [
        own,
        pick(z, [two, two, one, two]),
        pick(z, [four, three, three, five]),
        pick(z, [five, one, two, four]),
    ]
    full = [gather_plane(block, x, y).reshape(-1, BS, 128) for block in slots]
    return [
        pick(z, [full[0], full[1], full[1], full[1]]),
        pick(z, [full[2], full[0], full[2], full[2]]),
        pick(z, [full[3], full[2], full[0], full[3]]),
        pick(z, [full[1], full[3], full[3], full[0]]),
    ]


def add(a, b):
    return (a.astype(jnp.float32) + b.astype(jnp.float32)).astype(jnp.bfloat16)


def take(array, index, axis):
    return lax.dynamic_index_in_dim(array, index, axis, keepdims=False)


def scatter_plane(grads, x, y):
    grads = grads.reshape(Y, X, -1, BS, 128)
    h = grads.shape[2] // 2
    first, second = grads[:, :, :h], grads[:, :, h:]
    got_x = send(take(first, 1 - x, 1), ACROSS_X)
    got_y = send(take(second, 1 - y, 0), ACROSS_Y)
    first = add(take(first, x, 1), got_x)
    second = add(take(second, y, 0), got_y)
    got_y = send(take(first, 1 - y, 0), ACROSS_Y)
    got_x = send(take(second, 1 - x, 0), ACROSS_X)
    first = add(take(first, y, 0), got_y)
    second = add(take(second, x, 0), got_x)
    return jnp.concatenate([first, second], axis=0)


REDUCE = (
    ([(3, 2), (1, 0)], [(2, 0)]),
    ([(3, 2), (0, 1)], [(2, 1)]),
    ([(0, 1), (3, 2)], [(1, 2)]),
    ([(0, 1), (2, 3)], [(1, 3)]),
)


def reduce_to_plane(part, plane):
    first, second = REDUCE[plane]
    part = add(part, send(part, plane_route(first)))
    return part.astype(jnp.float32) + send(part, plane_route(second)).astype(jnp.float32)


def shards(
    x_in,
    cotangent,
    seq_lengths,
    weights,
    momentum,
    left_stat,
    right_stat,
    left_root,
    right_root,
    vectors,
    vector_sq,
):
    core = lax.axis_index("wt")
    place = lax.axis_index("seq")
    z, y, x = place // PLANE, (place // X) % Y, place % X
    first_core = core == 0
    rows = x_in.shape[0]
    local_count = weights.shape[0]
    quad_count = local_count // 4
    in_end, out_end, gate_end, up_end = quad_bounds()

    blocks = weights.astype(jnp.bfloat16).reshape(local_count, BS, BS)
    quad_ids = (place * CORES + core) * quad_count + jnp.arange(quad_count, dtype=jnp.int32)
    by_row = ((quad_ids >= in_end) & (quad_ids < out_end)) | (quad_ids >= up_end)
    by_row = by_row[None, :, None, None]
    halves = jnp.where(by_row, row_quads(blocks), col_quads(blocks))
    kept = take(halves, core, 0)
    got = to_sibling(take(halves, 1 - core, 0))
    own = jnp.concatenate(
        [jnp.where(first_core, kept, got), jnp.where(first_core, got, kept)], axis=0
    )
    q0, q1, q2, q3 = gather_weights(own, z, y, x)
    per_plane = q0.shape[0]
    w_in = col_matrix(q0[:in_end], 16)
    w_out = row_matrix(q0[in_end:out_end], 16)
    w_gate = col_matrix(
        jnp.concatenate([q0[out_end:], q1[: gate_end - per_plane]], axis=0), 16
    )
    w_up = col_matrix(
        jnp.concatenate([q1[gate_end - per_plane :], q2[: up_end - 2 * per_plane]], axis=0), 16
    )
    w_down = row_matrix(jnp.concatenate([q2[up_end - 2 * per_plane :], q3], axis=0), 72)

    both_x = jnp.concatenate([x_in, to_sibling(x_in)], axis=0)
    both_cot = jnp.concatenate([cotangent, to_sibling(cotangent)], axis=0)
    starts = jnp.stack([place * CORES + core, place * CORES + 1 - core]) * rows
    places = (starts[:, None] + jnp.arange(rows, dtype=jnp.int32)[None, :]).reshape(-1)
    keep_one, keep_two = keep_masks(places, seq_lengths)
    keep_one = keep_one.reshape(2, rows, 1)
    keep_two = keep_two.reshape(2, rows, 1)
    taps = take(vectors[2:].reshape(3, 16, 2, HALF), core, 2).reshape(3, D // 2)

    def exchange_sum(partial):
        return partial[:rows] + to_sibling(partial[rows:])

    hidden_both = both_x.astype(jnp.float32)
    scale_both = rms_scale(hidden_both)
    normed = (hidden_both * scale_both * vectors[0]).astype(jnp.bfloat16)
    hidden_in, scale_one = hidden_both[:rows], scale_both[:rows]
    mixed = matmul(normed, w_in).reshape(2, rows, 3, D // 2)
    input_gate, output_gate, values = mixed[:, :, 0], mixed[:, :, 1], mixed[:, :, 2]
    driven = input_gate * values
    ends = driven[:, -2:]
    carried = lax.ppermute(
        jnp.where(first_core, ends[1], ends[0]), "seq", [(i, i + 1) for i in range(CHIPS - 1)]
    )
    halos = jnp.stack(
        [jnp.where(first_core, carried, ends[1]), jnp.where(first_core, ends[0], carried)]
    )
    extended = jnp.concatenate([halos, driven], axis=1)
    conv_out = (
        taps[2] * driven
        + taps[1] * keep_one * extended[:, 1:-1]
        + taps[0] * keep_two * extended[:, :-2]
    )
    gated_out = (output_gate * conv_out).astype(jnp.bfloat16).reshape(2 * rows, D // 2)
    middle = hidden_in + exchange_sum(matmul(gated_out, w_out))
    scale_two = rms_scale(middle)
    own_two = (middle * scale_two * vectors[1]).astype(jnp.bfloat16)
    normed_two = jnp.concatenate([own_two, to_sibling(own_two)], axis=0)
    gate_ff = matmul(normed_two, w_gate)
    up_ff = matmul(normed_two, w_up)
    sigmoid_gate = jax.nn.sigmoid(gate_ff)
    silu_value = gate_ff * sigmoid_gate
    activated = (silu_value * up_ff).astype(jnp.bfloat16)
    grad_w_down = matrix_row(matmul_tn(activated, both_cot).astype(jnp.bfloat16))
    out_act = (middle + exchange_sum(matmul(activated, w_down))).astype(jnp.bfloat16)
    grad_act = matmul_nt(both_cot, w_down)
    grad_gate = (grad_act * up_ff * sigmoid_gate * (1.0 + gate_ff * (1.0 - sigmoid_gate))).astype(
        jnp.bfloat16
    )
    grad_up = (grad_act * silu_value).astype(jnp.bfloat16)
    grad_w_up = matrix_col(matmul_tn(normed_two, grad_up).astype(jnp.bfloat16))
    grad_w_gate = matrix_col(matmul_tn(normed_two, grad_gate).astype(jnp.bfloat16))
    grad_normed_two = exchange_sum(matmul_nt(grad_gate, w_gate) + matmul_nt(grad_up, w_up))
    gain_two_grad, middle_term = norm_back(middle, scale_two, vectors[1], grad_normed_two)
    grad_middle = cotangent.astype(jnp.float32) + middle_term
    own_branch = grad_middle.astype(jnp.bfloat16)
    grad_branch = jnp.concatenate([own_branch, to_sibling(own_branch)], axis=0)
    grad_w_out = matrix_row(matmul_tn(gated_out, grad_branch).astype(jnp.bfloat16))
    grad_gated = matmul_nt(grad_branch, w_out).reshape(2, rows, D // 2)
    grad_output_gate = grad_gated * conv_out
    grad_conv = grad_gated * output_gate
    early_one = keep_one * grad_conv
    early_two = keep_two * grad_conv
    tap_zero = jnp.sum(early_two * extended[:, :-2], axis=(0, 1))
    tap_first = jnp.sum(early_one * extended[:, 1:-1], axis=(0, 1))
    tap_second = jnp.sum(grad_conv * driven, axis=(0, 1))
    heads = jnp.stack(
        [
            taps[0] * early_two[:, 0],
            taps[1] * early_one[:, 0] + taps[0] * early_two[:, 1],
        ],
        axis=1,
    )
    from_after = lax.ppermute(
        jnp.where(first_core, heads[0], heads[1]), "seq", [(i + 1, i) for i in range(CHIPS - 1)]
    )
    tails = jnp.stack(
        [jnp.where(first_core, heads[1], from_after), jnp.where(first_core, from_after, heads[0])]
    )
    zero_rows = jnp.zeros((2, 2, D // 2), jnp.float32)
    grad_driven = taps[2] * grad_conv
    grad_driven = grad_driven + taps[1] * jnp.concatenate(
        [early_one[:, 1:], zero_rows[:, :1]], axis=1
    )
    grad_driven = grad_driven + taps[0] * jnp.concatenate([early_two[:, 2:], zero_rows], axis=1)
    grad_driven = grad_driven + jnp.concatenate(
        [jnp.zeros((2, rows - 2, D // 2), jnp.float32), tails], axis=1
    )
    grad_mixed = (
        jnp.concatenate(
            [grad_driven * values, grad_output_gate, grad_driven * input_gate], axis=2
        )
        .astype(jnp.bfloat16)
        .reshape(2 * rows, 3 * D // 2)
    )
    grad_w_in = matrix_col(matmul_tn(normed, grad_mixed).astype(jnp.bfloat16))
    grad_normed = exchange_sum(matmul_nt(grad_mixed, w_in))
    gain_one_grad, input_term = norm_back(hidden_in, scale_one, vectors[0], grad_normed)
    in_grad = grad_middle + input_term

    cut_gate = per_plane - out_end
    cut_up = 2 * per_plane - gate_end
    cut_down = 3 * per_plane - up_end
    planes = [
        jnp.concatenate([grad_w_in, grad_w_out, grad_w_gate[:cut_gate]], axis=0),
        jnp.concatenate([grad_w_gate[cut_gate:], grad_w_up[:cut_up]], axis=0),
        jnp.concatenate([grad_w_up[cut_up:], grad_w_down[:cut_down]], axis=0),
        grad_w_down[cut_down:],
    ]
    totals = [None] * Z
    for plane in reversed(range(Z)):
        totals[plane] = reduce_to_plane(scatter_plane(planes[plane], x, y), plane)
    total = pick(z, totals).reshape(2, quad_count, BS, 128)
    kept = take(total, core, 0)
    got = to_sibling(take(total, 1 - core, 0))
    halves = jnp.stack([jnp.where(first_core, kept, got), jnp.where(first_core, got, kept)])
    row_flag = jnp.repeat(by_row.reshape(-1), 4)[:, None, None]
    summed = jnp.where(row_flag, row_blocks(halves), col_blocks(halves))

    tap_part = jnp.stack([tap_zero, tap_first, tap_second], axis=0).reshape(3, 16, 1, HALF)
    tap_part = jnp.where(
        jnp.arange(2).reshape(1, 1, 2, 1) == core, tap_part, 0.0
    ).reshape(3, D)
    vector_part = jnp.concatenate([gain_one_grad[None], gain_two_grad[None], tap_part], axis=0)
    left_blocks = left_stat.reshape(local_count, BS, BS)
    right_blocks = right_stat.reshape(local_count, BS, BS)
    momentum_blocks = momentum.reshape(local_count, BS, BS)
    left_factor = left_root.reshape(local_count, BS, BS)
    right_factor = right_root.reshape(local_count, BS, BS)
    new_momentum = MOMENT * momentum_blocks + summed
    precond = jnp.einsum("kij,kjl->kil", left_factor, new_momentum)
    precond = jnp.einsum("kij,kjl->kil", precond, right_factor)
    precond_flat = precond.reshape(local_count, BS * BS)
    square = jnp.sum(precond_flat * precond_flat, axis=1)
    in_end, out_end, gate_end, up_end = block_bounds()
    block_ids = (place * CORES + core) * local_count + jnp.arange(local_count, dtype=jnp.int32)
    kind_index = (
        (block_ids >= in_end).astype(jnp.int32)
        + (block_ids >= out_end).astype(jnp.int32)
        + (block_ids >= gate_end).astype(jnp.int32)
        + (block_ids >= up_end).astype(jnp.int32)
    )
    one_hot = (kind_index[:, None] == jnp.arange(5, dtype=jnp.int32)[None, :]).astype(jnp.float32)
    kind_part = jnp.sum(one_hot * square[:, None], axis=0)
    vector_grads, kind_sum = lax.psum((vector_part, kind_part), ("seq", "wt"))
    kind_total = jnp.array(
        [in_end, out_end - in_end, gate_end - out_end, up_end - gate_end, BLOCKS - up_end],
        jnp.float32,
    ) * (BS * BS)
    kind_scale = lax.rsqrt(kind_sum / kind_total + MEAN_EPS)
    block_scale = jnp.sum(one_hot * kind_scale[None, :], axis=1)
    new_weights = weights - RATE * block_scale[:, None] * precond_flat
    weight_copy = new_weights.astype(jnp.bfloat16)
    new_left = DECAY * left_blocks + (1.0 - DECAY) * jnp.einsum("kij,klj->kil", summed, summed)
    new_right = DECAY * right_blocks + (1.0 - DECAY) * jnp.einsum("kji,kjl->kil", summed, summed)
    new_vector_sq = DECAY * vector_sq + (1.0 - DECAY) * vector_grads * vector_grads
    new_vectors = vectors - VEC_RATE * vector_grads * lax.rsqrt(new_vector_sq)
    flat_shape = (local_count, BS * BS)
    return (
        out_act,
        in_grad,
        new_weights,
        weight_copy,
        new_momentum.reshape(flat_shape),
        new_left.reshape(flat_shape),
        new_right.reshape(flat_shape),
        vector_grads,
        new_vector_sq,
        new_vectors,
    )


def solution(mesh):
    body = shards if (mesh.shape["seq"], mesh.shape["wt"]) == (CHIPS, CORES) else shards_any
    return jax.shard_map(
        body,
        mesh=mesh,
        in_specs=(
            P(("seq", "wt"), None),
            P(("seq", "wt"), None),
            P(),
            P(("seq", "wt"), None),
            P(("seq", "wt"), None),
            P(("seq", "wt"), None),
            P(("seq", "wt"), None),
            P(("seq", "wt"), None),
            P(("seq", "wt"), None),
            P(),
            P(),
        ),
        out_specs=(
            P(("seq", "wt"), None),
            P(("seq", "wt"), None),
            P(("seq", "wt"), None),
            P(("seq", "wt"), None),
            P(("seq", "wt"), None),
            P(("seq", "wt"), None),
            P(("seq", "wt"), None),
            P(),
            P(),
            P(),
        ),
        check_vma=False,
    )
```

```python
import jax
import jax.numpy as jnp
from jax import lax
from jax.experimental import pallas as pl
from jax.experimental.pallas import tpu as pltpu
from jax.sharding import PartitionSpec as P

D = 1024
FF = 4608
BS = 64
BLOCKS = 4480


NORM_EPS = 1e-05
MEAN_EPS = 1e-06
DECAY = 0.5
MOMENT = 0.9
RATE = 0.01
VEC_RATE = 0.25
HIGHEST = lax.Precision.HIGHEST


def from_behind(block, axis, distance):
    devices = range(lax.axis_size(axis))
    route = [(i - distance, i) for i in devices if i - distance in devices]
    return lax.ppermute(block, axis, route)


def unpack_blocks(blocks, row_count, col_count):
    return (
        blocks.reshape(row_count // BS, col_count // BS, BS, BS)
        .transpose(0, 2, 1, 3)
        .reshape(row_count, col_count)
    )


def pack_blocks(matrix):
    row_count, col_count = matrix.shape
    return (
        matrix.reshape(row_count // BS, BS, col_count // BS, BS)
        .transpose(0, 2, 1, 3)
        .reshape(-1, BS * BS)
    )


def block_bounds():
    per_block = BS * BS
    in_end = 3 * D * D // per_block
    out_end = in_end + D * D // per_block
    gate_end = out_end + D * FF // per_block
    up_end = gate_end + D * FF // per_block
    return (in_end, out_end, gate_end, up_end)


def matrices(blocks):
    in_end, out_end, gate_end, up_end = block_bounds()
    w_in = unpack_blocks(blocks[:in_end], D, 3 * D)
    w_out = unpack_blocks(blocks[in_end:out_end], D, D)
    w_gate = unpack_blocks(blocks[out_end:gate_end], D, FF)
    w_up = unpack_blocks(blocks[gate_end:up_end], D, FF)
    w_down = unpack_blocks(blocks[up_end:], FF, D)
    return (w_in, w_out, w_gate, w_up, w_down)


def matmul(left_side, right_side):
    return jnp.dot(left_side, right_side, preferred_element_type=jnp.float32)


def matmul_tn(left_side, right_side):
    return lax.dot_general(
        left_side, right_side, (((0,), (0,)), ((), ())), preferred_element_type=jnp.float32
    )


def matmul_nt(left_side, right_side):
    return lax.dot_general(
        left_side, right_side, (((1,), (1,)), ((), ())), preferred_element_type=jnp.float32
    )


def rms_scale(values):
    return lax.rsqrt(jnp.mean(values * values, axis=-1, keepdims=True) + NORM_EPS)


def norm_back(values, row_scale, norm_gain, grad_normed):
    gain_grad = jnp.sum(grad_normed * values * row_scale, axis=0)
    weighted = grad_normed * norm_gain
    grad_values = row_scale * weighted - values * row_scale**3 * jnp.mean(
        weighted * values, axis=-1, keepdims=True
    )
    return (gain_grad, grad_values)


def keep_masks(places, seq_lengths):
    ends = jnp.cumsum(seq_lengths)
    starts = jnp.max(jnp.where(ends[None, :] <= places[:, None], ends[None, :], 0), axis=1)
    keep_one = (places - 1 >= starts).astype(jnp.float32)[:, None]
    keep_two = (places - 2 >= starts).astype(jnp.float32)[:, None]
    return (keep_one, keep_two)


def weight_grads(operands):
    (
        normed,
        grad_mixed,
        gated_out,
        grad_branch,
        normed_two,
        grad_gate,
        grad_up,
        activated,
        cotangent,
    ) = operands
    return jnp.concatenate(
        [
            pack_blocks(matmul_tn(normed, grad_mixed)),
            pack_blocks(matmul_tn(gated_out, grad_branch)),
            pack_blocks(matmul_tn(normed_two, grad_gate)),
            pack_blocks(matmul_tn(normed_two, grad_up)),
            pack_blocks(matmul_tn(activated, cotangent)),
        ],
        axis=0,
    )


def shards_any(
    x_in,
    cotangent,
    seq_lengths,
    weights,
    momentum,
    left_stat,
    right_stat,
    left_root,
    right_root,
    vectors,
    vector_sq,
):
    gathered = lax.all_gather(weights.astype(jnp.bfloat16), ("seq", "wt"), axis=0, tiled=True)
    w_in, w_out, w_gate, w_up, w_down = matrices(gathered)
    row_count = x_in.shape[0]
    places = lax.axis_index(("seq", "wt")) * row_count + jnp.arange(row_count, dtype=jnp.int32)
    keep_one, keep_two = keep_masks(places, seq_lengths)
    hidden_in = x_in.astype(jnp.float32)
    scale_one = rms_scale(hidden_in)
    normed = (hidden_in * scale_one * vectors[0]).astype(jnp.bfloat16)
    mixed = matmul(normed, w_in)
    input_gate = mixed[:, :D]
    output_gate = mixed[:, D : 2 * D]
    values = mixed[:, 2 * D :]
    driven = input_gate * values
    carried = from_behind(driven[-2:], ("seq", "wt"), 1)
    extended = jnp.concatenate([carried, driven], axis=0)
    conv_out = (
        vectors[4] * driven
        + vectors[3] * keep_one * extended[1:-1]
        + vectors[2] * keep_two * extended[:-2]
    )
    gated_out = (output_gate * conv_out).astype(jnp.bfloat16)
    middle = hidden_in + matmul(gated_out, w_out)
    scale_two = rms_scale(middle)
    normed_two = (middle * scale_two * vectors[1]).astype(jnp.bfloat16)
    gate_ff = matmul(normed_two, w_gate)
    up_ff = matmul(normed_two, w_up)
    sigmoid_gate = jax.nn.sigmoid(gate_ff)
    silu_value = gate_ff * sigmoid_gate
    activated = (silu_value * up_ff).astype(jnp.bfloat16)
    out_act = (middle + matmul(activated, w_down)).astype(jnp.bfloat16)
    grad_act = matmul_nt(cotangent, w_down)
    grad_gate = (grad_act * up_ff * sigmoid_gate * (1.0 + gate_ff * (1.0 - sigmoid_gate))).astype(
        jnp.bfloat16
    )
    grad_up = (grad_act * silu_value).astype(jnp.bfloat16)
    grad_normed_two = matmul_nt(grad_gate, w_gate) + matmul_nt(grad_up, w_up)
    gain_two_grad, middle_term = norm_back(middle, scale_two, vectors[1], grad_normed_two)
    grad_middle = cotangent.astype(jnp.float32) + middle_term
    grad_branch = grad_middle.astype(jnp.bfloat16)
    grad_gated = matmul_nt(grad_branch, w_out)
    grad_output_gate = grad_gated * conv_out
    grad_conv = grad_gated * output_gate
    early_one = keep_one * grad_conv
    early_two = keep_two * grad_conv
    tap_zero = jnp.sum(early_two * extended[:-2], axis=0)
    tap_first = jnp.sum(early_one * extended[1:-1], axis=0)
    tap_second = jnp.sum(grad_conv * driven, axis=0)
    sent_back = jnp.stack(
        [vectors[2] * early_two[0], vectors[3] * early_one[0] + vectors[2] * early_two[1]], axis=0
    )
    from_after = from_behind(sent_back, ("seq", "wt"), -1)
    zero_rows = jnp.zeros((2, D), jnp.float32)
    grad_driven = vectors[4] * grad_conv
    grad_driven = grad_driven + vectors[3] * jnp.concatenate([early_one[1:], zero_rows[:1]], axis=0)
    grad_driven = grad_driven + vectors[2] * jnp.concatenate([early_two[2:], zero_rows], axis=0)
    grad_driven = grad_driven + jnp.concatenate(
        [jnp.zeros((row_count - 2, D), jnp.float32), from_after], axis=0
    )
    grad_mixed = jnp.concatenate(
        [grad_driven * values, grad_output_gate, grad_driven * input_gate], axis=1
    ).astype(jnp.bfloat16)
    grad_normed = matmul_nt(grad_mixed, w_in)
    gain_one_grad, input_term = norm_back(hidden_in, scale_one, vectors[0], grad_normed)
    in_grad = grad_middle + input_term
    paired = (
        lax.all_gather(normed, "wt", axis=0, tiled=True),
        lax.all_gather(grad_mixed, "wt", axis=0, tiled=True),
        lax.all_gather(gated_out, "wt", axis=0, tiled=True),
        lax.all_gather(grad_branch, "wt", axis=0, tiled=True),
        lax.all_gather(normed_two, "wt", axis=0, tiled=True),
        lax.all_gather(grad_gate, "wt", axis=0, tiled=True),
        lax.all_gather(grad_up, "wt", axis=0, tiled=True),
        lax.all_gather(activated, "wt", axis=0, tiled=True),
        lax.all_gather(cotangent, "wt", axis=0, tiled=True),
    )
    pair_grads = weight_grads(paired)
    seq_count = lax.axis_size("seq")
    core_count = lax.axis_size("wt")
    owned_count = pair_grads.shape[0] // (seq_count * core_count)
    arranged = pair_grads.reshape(seq_count, core_count, owned_count, BS * BS)
    mine = lax.dynamic_index_in_dim(arranged, lax.axis_index("wt"), 1, keepdims=False).reshape(
        seq_count * owned_count, BS * BS
    )
    summed_flat = lax.psum_scatter(mine, "seq", scatter_dimension=0, tiled=True)
    vector_part = jnp.stack([gain_one_grad, gain_two_grad, tap_zero, tap_first, tap_second], axis=0)
    local_count = summed_flat.shape[0]
    summed = summed_flat.reshape(local_count, BS, BS)
    left_blocks = left_stat.reshape(local_count, BS, BS)
    right_blocks = right_stat.reshape(local_count, BS, BS)
    momentum_blocks = momentum.reshape(local_count, BS, BS)
    left_factor = left_root.reshape(local_count, BS, BS)
    right_factor = right_root.reshape(local_count, BS, BS)
    new_left = DECAY * left_blocks + (1.0 - DECAY) * jnp.einsum(
        "kij,klj->kil", summed, summed, precision=HIGHEST
    )
    new_right = DECAY * right_blocks + (1.0 - DECAY) * jnp.einsum(
        "kji,kjl->kil", summed, summed, precision=HIGHEST
    )
    new_momentum = MOMENT * momentum_blocks + summed
    precond = jnp.einsum("kij,kjl->kil", left_factor, new_momentum, precision=HIGHEST)
    precond = jnp.einsum("kij,kjl->kil", precond, right_factor, precision=HIGHEST)
    precond_flat = precond.reshape(local_count, BS * BS)
    square = jnp.sum(precond_flat * precond_flat, axis=1)
    in_end, out_end, gate_end, up_end = block_bounds()
    block_ids = lax.axis_index(("seq", "wt")) * local_count + jnp.arange(
        local_count, dtype=jnp.int32
    )
    kind_index = (
        (block_ids >= in_end).astype(jnp.int32)
        + (block_ids >= out_end).astype(jnp.int32)
        + (block_ids >= gate_end).astype(jnp.int32)
        + (block_ids >= up_end).astype(jnp.int32)
    )
    one_hot = (kind_index[:, None] == jnp.arange(5, dtype=jnp.int32)[None, :]).astype(jnp.float32)
    kind_part = jnp.sum(one_hot * square[:, None], axis=0)
    vector_grads, kind_sum = lax.psum((vector_part, kind_part), ("seq", "wt"))
    kind_total = jnp.array(
        [in_end, out_end - in_end, gate_end - out_end, up_end - gate_end, BLOCKS - up_end],
        jnp.float32,
    ) * (BS * BS)
    kind_scale = lax.rsqrt(kind_sum / kind_total + MEAN_EPS)
    block_scale = jnp.sum(one_hot * kind_scale[None, :], axis=1)
    new_weights = weights - RATE * block_scale[:, None] * precond_flat
    weight_copy = new_weights.astype(jnp.bfloat16)
    new_vector_sq = DECAY * vector_sq + (1.0 - DECAY) * vector_grads * vector_grads
    new_vectors = vectors - VEC_RATE * vector_grads * lax.rsqrt(new_vector_sq)
    flat_shape = (local_count, BS * BS)
    return (
        out_act,
        in_grad,
        new_weights,
        weight_copy,
        new_momentum.reshape(flat_shape),
        new_left.reshape(flat_shape),
        new_right.reshape(flat_shape),
        vector_grads,
        new_vector_sq,
        new_vectors,
    )


Z, Y, X = 4, 2, 2
CHIPS, CORES = Z * Y * X, 2
PLANE = Y * X
HALF = BS // 2
SWAP = [(0, 1), (1, 0)]


def chip(z, y, x):
    return (z * Y + y) * X + x


def plane_route(pairs):
    return [(chip(a, y, x), chip(b, y, x)) for a, b in pairs for y in range(Y) for x in range(X)]


ACROSS_X = [(i, i ^ 1) for i in range(CHIPS)]
ACROSS_Y = [(i, i ^ 2) for i in range(CHIPS)]


def send(block, route):
    return lax.ppermute(block, "seq", route)


def to_sibling(block):
    return lax.ppermute(block, "wt", SWAP)


def quad_bounds():
    return tuple(b // 4 for b in block_bounds())


def pick(place, options):
    out = options[0]
    for i, option in enumerate(options[1:], 1):
        out = jnp.where(place == i, option, out)
    return out


def add(a, b):
    return (a.astype(jnp.float32) + b.astype(jnp.float32)).astype(jnp.bfloat16)


def take(array, index, axis):
    return lax.dynamic_index_in_dim(array, index, axis, keepdims=False)


def scatter_plane(grads, x, y):
    grads = grads.reshape(Y, X, -1, BS, 128)
    h = grads.shape[2] // 2
    first, second = grads[:, :, :h], grads[:, :, h:]
    got_x = send(take(first, 1 - x, 1), ACROSS_X)
    got_y = send(take(second, 1 - y, 0), ACROSS_Y)
    first = add(take(first, x, 1), got_x)
    second = add(take(second, y, 0), got_y)
    got_y = send(take(first, 1 - y, 0), ACROSS_Y)
    got_x = send(take(second, 1 - x, 0), ACROSS_X)
    first = add(take(first, y, 0), got_y)
    second = add(take(second, x, 0), got_x)
    return jnp.concatenate([first, second], axis=0)


REDUCE = (
    ([(3, 2), (1, 0)], [(2, 0)]),
    ([(3, 2), (0, 1)], [(2, 1)]),
    ([(0, 1), (3, 2)], [(1, 2)]),
    ([(0, 1), (2, 3)], [(1, 3)]),
)


def reduce_to_plane(part, plane):
    first, second = REDUCE[plane]
    part = add(part, send(part, plane_route(first)))
    return part.astype(jnp.float32) + send(part, plane_route(second)).astype(jnp.float32)


QUAD = 4 * BS
LANES = 128
KINDS = 5
VMEM_LIMIT = 56 * 1024 * 1024


def busy(micros):
    return pl.CostEstimate(flops=0, bytes_accessed=int(micros * 3e6), transcendentals=0)


def lane_ids(rows):
    return lax.broadcasted_iota(jnp.int32, (rows, LANES), 1)


def strided(ref, part, start, count, stride):
    return ref[part, pl.ds(start, count, stride=stride), :]


def columns(flat_ref, cols_ref):
    for k in range(cols_ref.shape[0]):
        cols_ref[k] = flat_ref[:, pl.ds(k * LANES, LANES)]


def cols_to_wide(cols_ref, wide_ref, count):
    low = lane_ids(count) < BS
    for k in range(BS // 2):
        parts = [strided(cols_ref, k, b, count, 4) for b in range(4)]
        turned = [pltpu.roll(p, BS, 1) for p in parts]
        for t in range(2):
            a, b = 2 * t, 2 * t + 1
            even = jnp.where(low, parts[a], turned[b])
            odd = jnp.where(low, turned[a], parts[b])
            wide_ref[t, pl.ds(2 * k, count, stride=BS), :] = even
            wide_ref[t, pl.ds(2 * k + 1, count, stride=BS), :] = odd


def wide_to_cols(wide_ref, cols_ref, count):
    low = lane_ids(count) < BS
    for k in range(BS // 2):
        for t in range(2):
            even = strided(wide_ref, t, 2 * k, count, BS)
            odd = strided(wide_ref, t, 2 * k + 1, count, BS)
            a, b = 2 * t, 2 * t + 1
            cols_ref[k, pl.ds(a, count, stride=4), :] = jnp.where(
                low, even, pltpu.roll(odd, BS, 1)
            )
            cols_ref[k, pl.ds(b, count, stride=4), :] = jnp.where(
                low, pltpu.roll(even, BS, 1), odd
            )


def join(wide_ref, rows):
    return jnp.concatenate([wide_ref[0, rows, :], wide_ref[1, rows, :]], axis=1)


def cut(wide_ref, rows, value):
    wide_ref[0, rows, :] = value[:, :LANES].astype(wide_ref.dtype)
    wide_ref[1, rows, :] = value[:, LANES:].astype(wide_ref.dtype)


def cols_shape(flat):
    return (flat.shape[1] // LANES, flat.shape[0], LANES)


def kind_of(quad):
    kind = jnp.int32(0)
    for bound in quad_bounds():
        kind = kind + (quad >= bound).astype(jnp.int32)
    return kind


def is_row_kind(kind):
    return (kind == 1) | (kind == 4)


def split_weights_kernel(place_ref, flat_ref, kept_ref, sent_ref, cols_ref, col_ref, row_ref):
    count = flat_ref.shape[0] // 4
    core, first = place_ref[0], place_ref[1]
    group = lane_ids(count) // HALF
    low = group < 2
    columns(flat_ref, cols_ref)
    for k in range(BS // 2):
        parts = [strided(cols_ref, k, b, count, 4) for b in range(4)]
        rolls = [[p] + [pltpu.roll(p, s * HALF, 1) for s in (1, 2, 3)] for p in parts]
        for odd in range(2):
            r = 2 * k + odd
            for half in range(2):
                g = 2 * odd + half
                out = rolls[0][(0 - g) % 4]
                for b in range(1, 4):
                    out = jnp.where(group == b, rolls[b][(b - g) % 4], out)
                col_ref[half, pl.ds(r, count, stride=BS), :] = out
            for t in range(2):
                a, b = 2 * t, 2 * t + 1
                if odd:
                    out = jnp.where(low, rolls[a][2], parts[b])
                else:
                    out = jnp.where(low, parts[a], rolls[b][2])
                row_ref[r // HALF, pl.ds(t * HALF + r % HALF, count, stride=BS), :] = out

    def finish(q, carry):
        rows = pl.ds(pl.multiple_of(q * BS, BS), BS)
        by_row = is_row_kind(kind_of(first + q))
        for ref, half in ((kept_ref, core), (sent_ref, 1 - core)):
            value = jnp.where(by_row, row_ref[half, rows, :], col_ref[half, rows, :])
            ref[q] = value.astype(ref.dtype)
        return carry

    lax.fori_loop(0, count, finish, 0)


def whole(n):
    return [pl.BlockSpec(memory_space=pltpu.VMEM)] * n


SCALARS = pl.BlockSpec(memory_space=pltpu.SMEM)


def split_weights(core, first, weights):
    count = weights.shape[0] // 4
    quads = jax.ShapeDtypeStruct((count, BS, LANES), jnp.bfloat16)
    return pl.pallas_call(
        split_weights_kernel,
        out_shape=(quads, quads),
        in_specs=[SCALARS] + whole(1),
        out_specs=tuple(whole(2)),
        scratch_shapes=[pltpu.VMEM(cols_shape(weights), jnp.float32)]
        + [pltpu.VMEM((2, count * BS, LANES), jnp.float32)] * 2,
        compiler_params=pltpu.CompilerParams(vmem_limit_bytes=VMEM_LIMIT),
        cost_estimate=busy(8),
    )(jnp.stack([core, first]), weights)


def widen_kernel(momentum_ref, left_ref, right_ref, mom_ref, lw_ref, rw_ref, cols_ref, wide_ref):
    count = momentum_ref.shape[0] // 4
    columns(momentum_ref, cols_ref)
    cols_to_wide(cols_ref, mom_ref, count)
    for src, dst in ((left_ref, lw_ref), (right_ref, rw_ref)):
        columns(src, cols_ref)
        cols_to_wide(cols_ref, wide_ref, count)
        dst[...] = wide_ref[...].astype(dst.dtype)


def widen(momentum, left_root, right_root):
    shape = (2, momentum.shape[0] // 4 * BS, LANES)
    return pl.pallas_call(
        widen_kernel,
        out_shape=(
            jax.ShapeDtypeStruct(shape, jnp.float32),
            jax.ShapeDtypeStruct(shape, jnp.bfloat16),
            jax.ShapeDtypeStruct(shape, jnp.bfloat16),
        ),
        in_specs=whole(3),
        out_specs=tuple(whole(3)),
        scratch_shapes=[
            pltpu.VMEM(cols_shape(momentum), jnp.float32),
            pltpu.VMEM(shape, jnp.float32),
        ],
        compiler_params=pltpu.CompilerParams(vmem_limit_bytes=VMEM_LIMIT),
        cost_estimate=busy(11),
    )(momentum, left_root, right_root)


def diagonal(wide, mask):
    return jnp.where(mask, jnp.concatenate([wide] * 4, axis=0), jnp.zeros((), wide.dtype))


def diagonal_mask():
    rows = lax.broadcasted_iota(jnp.int32, (QUAD, QUAD), 0) // BS
    cols = lax.broadcasted_iota(jnp.int32, (QUAD, QUAD), 1) // BS
    return rows == cols


def wide_sum(kept, got, core, by_row):
    first = jnp.where(core == 0, kept, got)
    second = jnp.where(core == 0, got, kept)
    group = lane_ids(BS) // HALF
    tiles = []
    for t in range(2):
        pieces = (
            (first, 2 * t, 0),
            (second, 2 * t, 1),
            (first, 2 * t + 1, 2),
            (second, 2 * t + 1, 3),
        )
        out = None
        for value, source, target in pieces:
            shift = (target - source) * HALF % LANES
            moved = value if shift == 0 else pltpu.roll(value, shift, 1)
            out = moved if out is None else jnp.where(group == target, moved, out)
        rows = slice(t * HALF, (t + 1) * HALF)
        tiles.append(
            jnp.where(by_row, jnp.concatenate([first[rows], second[rows]], axis=0), out)
        )
    return jnp.concatenate(tiles, axis=1)


def step_kernel(
    place_ref, kept_ref, got_ref, mom_ref, lw_ref, rw_ref, flat_ref,
    new_mom_ref, precond_ref, wide_ref, kind_ref, cols_ref, sum_ref, step_ref,
):
    count = kept_ref.shape[0]
    core, first = place_ref[0], place_ref[1]
    mask = diagonal_mask()
    kind_ref[...] = jnp.zeros_like(kind_ref)

    def one(q, carry):
        rows = pl.ds(pl.multiple_of(q * BS, BS), BS)
        kind = kind_of(first + q)
        total = wide_sum(
            kept_ref[q].astype(jnp.float32), got_ref[q].astype(jnp.float32), core, is_row_kind(kind)
        )
        cut(sum_ref, rows, total)
        wide_ref[rows, :] = total.astype(jnp.bfloat16)
        moment = (MOMENT * join(mom_ref, rows) + total).astype(jnp.bfloat16)
        inner = jnp.dot(
            join(lw_ref, rows), diagonal(moment, mask), preferred_element_type=jnp.float32
        ).astype(jnp.bfloat16)
        step = jnp.dot(
            inner, diagonal(join(rw_ref, rows), mask), preferred_element_type=jnp.float32
        )
        cut(step_ref, rows, step)
        square = jnp.sum(step * step, axis=0, keepdims=True)
        kind_ref[pl.ds(kind, 1), :] += square[:, :LANES] + square[:, LANES:]
        return carry

    lax.fori_loop(0, count, one, 0, unroll=5)

    wide_to_cols(sum_ref, cols_ref, count)
    for k in range(cols_ref.shape[0]):
        lanes = pl.ds(k * LANES, LANES)
        new_mom_ref[:, lanes] = MOMENT * flat_ref[:, lanes] + cols_ref[k]
    wide_to_cols(step_ref, cols_ref, count)
    for k in range(cols_ref.shape[0]):
        precond_ref[:, pl.ds(k * LANES, LANES)] = cols_ref[k]


def step_blocks(core, first, kept, got, mom_wide, left_wide, right_wide, momentum):
    count = kept.shape[0]
    rows = count * BS
    flat = jax.ShapeDtypeStruct(momentum.shape, jnp.float32)
    return pl.pallas_call(
        step_kernel,
        out_shape=(
            flat,
            flat,
            jax.ShapeDtypeStruct((rows, QUAD), jnp.bfloat16),
            jax.ShapeDtypeStruct((8, LANES), jnp.float32),
        ),
        in_specs=[SCALARS] + whole(6),
        out_specs=tuple(whole(4)),
        scratch_shapes=[pltpu.VMEM(cols_shape(momentum), jnp.float32)]
        + [pltpu.VMEM((2, rows, LANES), jnp.float32)] * 2,
        compiler_params=pltpu.CompilerParams(vmem_limit_bytes=VMEM_LIMIT),
        cost_estimate=busy(13),
    )(jnp.stack([core, first]), kept, got, mom_wide, left_wide, right_wide, momentum)


def stats_kernel(
    wide_ref, left_ref, right_ref, new_left_ref, new_right_ref, cols_ref, gram_ref, turn_ref
):
    count = wide_ref.shape[0] // BS
    mask = diagonal_mask()

    def one(q, carry):
        rows = pl.ds(pl.multiple_of(q * BS, BS), BS)
        total = wide_ref[rows, :]
        gram = lax.dot_general(
            total, diagonal(total, mask), (((1,), (1,)), ((), ())),
            preferred_element_type=jnp.float32,
        )
        cut(gram_ref, rows, gram)
        turned = lax.dot_general(
            total, total, (((0,), (0,)), ((), ())), preferred_element_type=jnp.float32
        )
        turned = jnp.where(mask, turned, 0.0)
        turned = turned[:BS] + turned[BS : 2 * BS] + turned[2 * BS : 3 * BS] + turned[3 * BS :]
        cut(turn_ref, rows, turned)
        return carry

    lax.fori_loop(0, count, one, 0, unroll=5)

    pairs = ((gram_ref, left_ref, new_left_ref), (turn_ref, right_ref, new_right_ref))
    for product_ref, old_ref, new_ref in pairs:
        wide_to_cols(product_ref, cols_ref, count)
        for k in range(cols_ref.shape[0]):
            lanes = pl.ds(k * LANES, LANES)
            new_ref[:, lanes] = DECAY * old_ref[:, lanes] + (1.0 - DECAY) * cols_ref[k]


def stats_blocks(wide, left_stat, right_stat):
    flat = jax.ShapeDtypeStruct(left_stat.shape, jnp.float32)
    return pl.pallas_call(
        stats_kernel,
        out_shape=(flat, flat),
        in_specs=whole(3),
        out_specs=tuple(whole(2)),
        scratch_shapes=[pltpu.VMEM(cols_shape(left_stat), jnp.float32)]
        + [pltpu.VMEM((2, wide.shape[0], LANES), jnp.float32)] * 2,
        compiler_params=pltpu.CompilerParams(vmem_limit_bytes=VMEM_LIMIT),
        cost_estimate=busy(12),
    )(wide, left_stat, right_stat)


TILE = 256


def f32_dot(a, b, dims=((1,), (0,))):
    return lax.dot_general(a, b, (dims, ((), ())), preferred_element_type=jnp.float32)


def nt_dot(a, b):
    return f32_dot(a, b, ((1,), (1,)))


def col_tile(ref, rows, per_row, j, width=2):
    parts = [
        jnp.concatenate([ref[i * per_row + j + d] for i in range(rows)], axis=0)
        for d in range(width)
    ]
    return jnp.concatenate(parts, axis=1)


def col_rows(ref, first, rows, per_row):
    return jnp.concatenate(
        [
            jnp.concatenate([ref[(first + i) * per_row + j] for j in range(per_row)], axis=1)
            for i in range(rows)
        ],
        axis=0,
    )


def row_rows(ref, first, rows, per_row):
    return jnp.concatenate(
        [
            jnp.concatenate(
                [
                    ref[(first + i) * per_row + j, h * HALF : (h + 1) * HALF]
                    for j in range(per_row)
                    for h in range(2)
                ],
                axis=1,
            )
            for i in range(rows)
        ],
        axis=0,
    )


def row_tile(ref, rows, per_row, j):
    parts = [
        jnp.concatenate(
            [ref[i * per_row + j, h * HALF : (h + 1) * HALF] for i in range(rows)], axis=0
        )
        for h in range(2)
    ]
    return jnp.concatenate(parts, axis=1)


def put_col_tile(ref, value, rows, per_row, j, width=2):
    value = value.astype(ref.dtype)
    for i in range(rows):
        for d in range(width):
            ref[i * per_row + j + d] = value[i * BS : (i + 1) * BS, d * LANES : (d + 1) * LANES]


def put_row_rows(ref, value, first, rows, per_row):
    value = value.astype(ref.dtype)
    for i in range(rows):
        for j in range(per_row):
            for h in range(2):
                part = value[
                    i * HALF : (i + 1) * HALF, (2 * j + h) * LANES : (2 * j + h + 1) * LANES
                ]
                ref[(first + i) * per_row + j, h * HALF : (h + 1) * HALF] = part


def put_part(own_ref, other_ref, cols, value):
    rows = own_ref.shape[0]
    own_ref[:, cols] = value[:rows]
    other_ref[:, cols] = value[rows:]


def parts(rows):
    return [shape((rows // 2, D), jnp.float32)] * 2


def call(kernel, outs, ins, scratch=(), micros=0, any_in=()):
    specs = [
        pl.BlockSpec(memory_space=pl.ANY if i in any_in else pltpu.VMEM) for i in range(len(ins))
    ]
    return pl.pallas_call(
        kernel,
        out_shape=tuple(jax.ShapeDtypeStruct(o.shape, o.dtype) for o in outs),
        in_specs=specs,
        out_specs=tuple(whole(len(outs))),
        scratch_shapes=list(scratch),
        compiler_params=pltpu.CompilerParams(vmem_limit_bytes=VMEM_LIMIT),
        cost_estimate=busy(micros),
    )(*ins)


def shape(dims, dtype):
    return jax.ShapeDtypeStruct(dims, dtype)


IN_ROWS = D // BS
IN_COLS = 3 * D // 256
OUT_COLS = D // 256
FF_COLS = FF // 256
DOWN_ROWS = FF // BS
FF_HALF = FF // 2
D_HALF = D // 2


def fetch(quads_ref, first, count, into, sem):
    return pltpu.make_async_copy(quads_ref.at[pl.ds(first, count)], into, sem)


def mix_kernel(normed_ref, quads_ref, mixed_ref, w_ref, sems):
    step = 4 * IN_COLS
    copies = [
        fetch(quads_ref, g * step, step, w_ref.at[pl.ds(g * step, step)], sems.at[g])
        for g in range(IN_ROWS // 4)
    ]
    for c in copies:
        c.start()
    for c in copies:
        c.wait()

    def tile(t, carry):
        cols = pl.ds(pl.multiple_of(t * TILE, TILE), TILE)
        mixed_ref[:, cols] = f32_dot(
            normed_ref[...], col_tile(w_ref, IN_ROWS, IN_COLS, 2 * t)
        )
        return carry

    lax.fori_loop(0, IN_COLS // 2, tile, 0)


def mix(normed, quads):
    rows = normed.shape[0]
    return call(
        mix_kernel,
        [shape((rows, 3 * D_HALF), jnp.float32)],
        [normed, quads],
        [
            pltpu.VMEM((IN_ROWS * IN_COLS, BS, LANES), jnp.bfloat16),
            pltpu.SemaphoreType.DMA((IN_ROWS // 4,)),
        ],
        micros=7,
        any_in=(1,),
    )[0]


def shift_down(value, halo, distance):
    moved = pltpu.roll(value, distance, 0)
    row = lax.broadcasted_iota(jnp.int32, value.shape, 0)
    out = jnp.where(row == 0, halo[2 - distance : 3 - distance], moved)
    if distance == 2:
        out = jnp.where(row == 1, halo[1:2], out)
    return out


def shift_up(value, distance):
    count = value.shape[0]
    moved = pltpu.roll(value, count - distance, 0)
    row = lax.broadcasted_iota(jnp.int32, value.shape, 0)
    return jnp.where(row < count - distance, moved, 0.0)


def conv_kernel(
    mixed_ref, halo_ref, keep_ref, taps_ref, quads_ref,
    conv_ref, gated_ref, own_ref, other_ref,
    w_ref, sem,
):
    first = 3 * IN_ROWS * OUT_COLS
    copy = fetch(quads_ref, first, IN_ROWS * OUT_COLS, w_ref, sem)
    copy.start()
    rows = mixed_ref.shape[0] // 2
    for s in range(2):
        at = pl.ds(s * rows, rows)
        driven = mixed_ref[at, :D_HALF] * mixed_ref[at, 2 * D_HALF :]
        halo = halo_ref[s]
        conv = (
            taps_ref[2:3] * driven
            + taps_ref[1:2] * keep_ref[at, 0:1] * shift_down(driven, halo, 1)
            + taps_ref[0:1] * keep_ref[at, 1:2] * shift_down(driven, halo, 2)
        )
        conv_ref[at, :] = conv
        gated_ref[at, :] = (mixed_ref[at, D_HALF : 2 * D_HALF] * conv).astype(jnp.bfloat16)
    copy.wait()
    for j in range(OUT_COLS):
        value = f32_dot(gated_ref[...], row_tile(w_ref, IN_ROWS, OUT_COLS, j))
        put_part(own_ref, other_ref, slice(j * TILE, (j + 1) * TILE), value)


def conv_forward(mixed, halos, keep, taps, quads):
    rows = mixed.shape[0]
    return call(
        conv_kernel,
        [
            shape((rows, D_HALF), jnp.float32),
            shape((rows, D_HALF), jnp.bfloat16),
        ]
        + parts(rows),
        [mixed, halos, keep, taps, quads],
        [
            pltpu.VMEM((IN_ROWS * OUT_COLS, BS, LANES), jnp.bfloat16),
            pltpu.SemaphoreType.DMA(()),
        ],
        micros=5,
        any_in=(4,),
    )


def ff_kernel(
    normed_ref, cot_ref, quads_ref,
    act_ref, gg_ref, gu_ref, dup_ref, ddown_ref,
    gate_ref, up_ref, down_ref, turned_ref, sems,
):
    _, out_end, gate_end, up_end = quad_bounds()
    per = IN_ROWS * FF_COLS
    copies = [
        fetch(quads_ref, first, per, ref, sems.at[n])
        for n, (first, ref) in enumerate(
            ((out_end, gate_ref), (gate_end, up_ref), (up_end, down_ref))
        )
    ]
    for c in copies:
        c.start()
    turned_ref[...] = normed_ref[...].T
    for c in copies:
        c.wait()
    step = TILE // HALF

    def tile(t, carry):
        cols = pl.ds(pl.multiple_of(t * TILE, TILE), TILE)
        normed, cot = normed_ref[...], cot_ref[...]
        gate = f32_dot(normed, col_tile(gate_ref, IN_ROWS, FF_COLS, 2 * t))
        up = f32_dot(normed, col_tile(up_ref, IN_ROWS, FF_COLS, 2 * t))
        grad_act = nt_dot(cot, row_rows(down_ref, step * t, step, OUT_COLS))
        sig = jax.nn.sigmoid(gate)
        silu = gate * sig
        act = (silu * up).astype(jnp.bfloat16)
        act_ref[:, cols] = act
        gg_ref[:, cols] = (grad_act * up * sig * (1.0 + gate * (1.0 - sig))).astype(jnp.bfloat16)
        grad_up = (grad_act * silu).astype(jnp.bfloat16)
        gu_ref[:, cols] = grad_up
        put_row_rows(ddown_ref, f32_dot(act.T, cot), step * t, step, OUT_COLS)
        put_col_tile(dup_ref, f32_dot(turned_ref[...], grad_up), IN_ROWS, FF_COLS, 2 * t)
        return carry

    lax.fori_loop(0, FF_COLS // 2, tile, 0)


def ff_pass(normed, cot, quads):
    rows = normed.shape[0]
    per = IN_ROWS * FF_COLS
    wide = shape((rows, FF_HALF), jnp.bfloat16)
    grads = shape((per, BS, LANES), jnp.bfloat16)
    weights = pltpu.VMEM((per, BS, LANES), jnp.bfloat16)
    return call(
        ff_kernel,
        [wide, wide, wide, grads, grads],
        [normed, cot, quads],
        [weights] * 3
        + [pltpu.VMEM((D, rows), jnp.bfloat16), pltpu.SemaphoreType.DMA((3,))],
        micros=27,
        any_in=(2,),
    )


def ff_back_kernel(gg_ref, gu_ref, quads_ref, own_ref, other_ref, gate_ref, up_ref, sems):
    _, out_end, gate_end, _ = quad_bounds()
    step = 4 * FF_COLS
    groups = IN_ROWS // 4
    copies = []
    for g in range(groups):
        at = pl.ds(g * step, step)
        copies.append(fetch(quads_ref, out_end + g * step, step, gate_ref.at[at], sems.at[0, g]))
        copies.append(fetch(quads_ref, gate_end + g * step, step, up_ref.at[at], sems.at[1, g]))
    for c in copies:
        c.start()
    for g in range(groups):
        copies[2 * g].wait()
        copies[2 * g + 1].wait()
        value = nt_dot(gg_ref[...], col_rows(gate_ref, 4 * g, 4, FF_COLS))
        value = value + nt_dot(gu_ref[...], col_rows(up_ref, 4 * g, 4, FF_COLS))
        put_part(own_ref, other_ref, slice(g * TILE, (g + 1) * TILE), value)


def ff_back(gg, gu, quads):
    rows = gg.shape[0]
    weights = pltpu.VMEM((IN_ROWS * FF_COLS, BS, LANES), jnp.bfloat16)
    return call(
        ff_back_kernel,
        parts(rows),
        [gg, gu, quads],
        [weights, weights, pltpu.SemaphoreType.DMA((2, IN_ROWS // 4))],
        micros=16,
        any_in=(2,),
    )


def ff_rest_kernel(
    normed_ref, act_ref, gg_ref, quads_ref, dgate_ref, own_ref, other_ref, down_ref, turned_ref, sem
):
    copy = fetch(quads_ref, quad_bounds()[3], DOWN_ROWS * OUT_COLS, down_ref, sem)
    copy.start()
    turned_ref[...] = normed_ref[...].T

    def tile(t, carry):
        cols = pl.ds(pl.multiple_of(t * TILE, TILE), TILE)
        put_col_tile(dgate_ref, f32_dot(turned_ref[...], gg_ref[:, cols]), IN_ROWS, FF_COLS, 2 * t)
        return carry

    lax.fori_loop(0, FF_COLS // 2, tile, 0)
    copy.wait()
    for j in range(OUT_COLS):
        value = f32_dot(act_ref[...], row_tile(down_ref, DOWN_ROWS, OUT_COLS, j))
        put_part(own_ref, other_ref, slice(j * TILE, (j + 1) * TILE), value)


def ff_rest(normed, act, gg, quads):
    rows = normed.shape[0]
    per = IN_ROWS * FF_COLS
    return call(
        ff_rest_kernel,
        [shape((per, BS, LANES), jnp.bfloat16)] + parts(rows),
        [normed, act, gg, quads],
        [
            pltpu.VMEM((per, BS, LANES), jnp.bfloat16),
            pltpu.VMEM((D, rows), jnp.bfloat16),
            pltpu.SemaphoreType.DMA(()),
        ],
        micros=11,
        any_in=(3,),
    )


def conv_back_kernel(
    branch_ref, mixed_ref, conv_ref, gated_ref, halo_ref, keep_ref, taps_ref, quads_ref,
    dout_ref, gconv_ref, ggate_ref, heads_ref, tap_ref, w_ref, sem,
):
    first = 3 * IN_ROWS * OUT_COLS
    copy = fetch(quads_ref, first, IN_ROWS * OUT_COLS, w_ref, sem)
    copy.start()
    copy.wait()
    rows = mixed_ref.shape[0] // 2
    step = TILE // HALF
    grad = jnp.concatenate(
        [
            nt_dot(branch_ref[...], row_rows(w_ref, g * step, step, OUT_COLS))
            for g in range(IN_ROWS // step)
        ],
        axis=1,
    )
    ggate_ref[...] = (grad * conv_ref[...]).astype(jnp.bfloat16)
    gconv_ref[...] = grad * mixed_ref[:, D_HALF : 2 * D_HALF]
    taps = [jnp.zeros((1, D_HALF), jnp.float32)] * 3
    for s in range(2):
        at = pl.ds(s * rows, rows)
        driven = mixed_ref[at, :D_HALF] * mixed_ref[at, 2 * D_HALF :]
        halo = halo_ref[s]
        grad_conv = gconv_ref[at, :]
        one = keep_ref[at, 0:1] * grad_conv
        two = keep_ref[at, 1:2] * grad_conv
        terms = (two * shift_down(driven, halo, 2), one * shift_down(driven, halo, 1), grad_conv * driven)
        taps = [a + jnp.sum(b, axis=0, keepdims=True) for a, b in zip(taps, terms)]
        heads_ref[s, 0:1] = taps_ref[0:1] * two[0:1]
        heads_ref[s, 1:2] = taps_ref[1:2] * one[0:1] + taps_ref[0:1] * two[1:2]
    tap_ref[...] = jnp.concatenate(taps, axis=0)
    put_row_rows(dout_ref, f32_dot(gated_ref[...].T, branch_ref[...]), 0, IN_ROWS, OUT_COLS)


def conv_back(branch, mixed, conv, gated, halos, keep, taps, quads):
    rows = mixed.shape[0]
    return call(
        conv_back_kernel,
        [
            shape((IN_ROWS * OUT_COLS, BS, LANES), jnp.bfloat16),
            shape((rows, D_HALF), jnp.float32),
            shape((rows, D_HALF), jnp.bfloat16),
            shape((2, 2, D_HALF), jnp.float32),
            shape((3, D_HALF), jnp.float32),
        ],
        [branch, mixed, conv, gated, halos, keep, taps, quads],
        [
            pltpu.VMEM((IN_ROWS * OUT_COLS, BS, LANES), jnp.bfloat16),
            pltpu.SemaphoreType.DMA(()),
        ],
        micros=7,
        any_in=(7,),
    )


def mix_back_kernel(
    gconv_ref, ggate_ref, mixed_ref, normed_ref, tails_ref, keep_ref, taps_ref, quads_ref,
    din_ref, own_ref, other_ref, grad_ref, turned_ref, w_ref, sem,
):
    copy = fetch(quads_ref, 0, IN_ROWS * IN_COLS, w_ref, sem)
    copy.start()
    turned_ref[...] = normed_ref[...].T
    rows = mixed_ref.shape[0] // 2
    for s in range(2):
        at = pl.ds(s * rows, rows)
        grad_conv = gconv_ref[at, :]
        one = keep_ref[at, 0:1] * grad_conv
        two = keep_ref[at, 1:2] * grad_conv
        grad = (
            taps_ref[2:3] * grad_conv
            + taps_ref[1:2] * shift_up(one, 1)
            + taps_ref[0:1] * shift_up(two, 2)
        )
        row = lax.broadcasted_iota(jnp.int32, grad.shape, 0)
        tail = tails_ref[s]
        grad = grad + jnp.where(
            row == rows - 2, tail[0:1], jnp.where(row == rows - 1, tail[1:2], 0.0)
        )
        grad_ref[at, :D_HALF] = (grad * mixed_ref[at, 2 * D_HALF :]).astype(jnp.bfloat16)
        grad_ref[at, D_HALF : 2 * D_HALF] = ggate_ref[at, :]
        grad_ref[at, 2 * D_HALF :] = (grad * mixed_ref[at, :D_HALF]).astype(jnp.bfloat16)

    def tile(t, carry):
        cols = pl.ds(pl.multiple_of(t * TILE, TILE), TILE)
        put_col_tile(din_ref, f32_dot(turned_ref[...], grad_ref[:, cols]), IN_ROWS, IN_COLS, 2 * t)
        return carry

    lax.fori_loop(0, IN_COLS // 2, tile, 0)
    copy.wait()
    for g in range(IN_ROWS // 4):
        value = nt_dot(grad_ref[...], col_rows(w_ref, 4 * g, 4, IN_COLS))
        put_part(own_ref, other_ref, slice(g * TILE, (g + 1) * TILE), value)


def mix_back(gconv, ggate, mixed, normed, tails, keep, taps, quads):
    rows = mixed.shape[0]
    per = IN_ROWS * IN_COLS
    return call(
        mix_back_kernel,
        [shape((per, BS, LANES), jnp.bfloat16)] + parts(rows),
        [gconv, ggate, mixed, normed, tails, keep, taps, quads],
        [
            pltpu.VMEM((rows, 3 * D_HALF), jnp.bfloat16),
            pltpu.VMEM((D, rows), jnp.bfloat16),
            pltpu.VMEM((per, BS, LANES), jnp.bfloat16),
            pltpu.SemaphoreType.DMA(()),
        ],
        micros=10,
        any_in=(7,),
    )


def place_kernel(place_ref, near_ref, x_ref, y_ref, far_a_ref, far_b_ref, *refs):
    out_ref, sems = refs[-2:]
    plane, here, core = place_ref[0], place_ref[1], place_ref[2]
    copies = []
    for n, src in enumerate((near_ref, x_ref, y_ref)):
        there = here ^ n
        for slot in range(2):
            copies.append((src.at[slot], out_ref.at[plane, there, slot ^ core]))
    there = here ^ 3
    copies.append((far_a_ref, out_ref.at[plane, there, core]))
    copies.append((far_b_ref, out_ref.at[plane, there, 1 - core]))
    copies = [pltpu.make_async_copy(a, b, sems.at[n]) for n, (a, b) in enumerate(copies)]
    for c in copies:
        c.start()
    for c in copies:
        c.wait()


def put_plane(plane, here, core, pieces, out):
    hbm = pl.BlockSpec(memory_space=pl.ANY)
    near = pieces[0]
    given = list(pieces) + ([] if out is None else [out])
    return pl.pallas_call(
        place_kernel,
        out_shape=jax.ShapeDtypeStruct((Z, PLANE) + near.shape, near.dtype),
        in_specs=[SCALARS] + [hbm] * len(given),
        out_specs=hbm,
        scratch_shapes=[pltpu.SemaphoreType.DMA((8,))],
        input_output_aliases={} if out is None else {6: 0},
        compiler_params=pltpu.CompilerParams(vmem_limit_bytes=1024 * 1024),
        cost_estimate=busy(3),
    )(jnp.stack([plane, here, core]), *given)


UP = [(0, 1), (1, 2), (2, 3)]
DOWN = [(1, 0), (2, 1), (3, 2)]
SLOT_PLANES = ((0, 1, 2, 3), (1, 0, 2, 3), (2, 1, 0, 3), (3, 2, 1, 0))


def together(*values):
    return lax.optimization_barrier(values)


def gather_weights(own, z, here, core):
    def far(from_x, from_y):
        return send(from_y[0], ACROSS_X), send(from_x[1], ACROSS_Y)

    def near(block):
        return send(block, ACROSS_X), send(block, ACROSS_Y)

    out = None
    up, down, slots, sides, corners = [], [], [own], [], []
    for n in range(Z + 1):
        pending = []
        if n < Z - 1:
            up.append(send(up[-1] if n else own, plane_route(UP[n:])))
            down.append(send(down[-1] if n else own, plane_route(DOWN[: Z - 1 - n])))
            pending += [up, down]
        if n > 0:
            corners.append(far(*sides[n - 1]))
        if n < Z:
            sides.append(near(slots[n]))
        flat = [up[-1], down[-1]] if n < Z - 1 else []
        flat += list(corners[-1]) if n > 0 else []
        flat += list(sides[-1]) if n < Z else []
        flat = list(together(*flat))
        if n < Z:
            sides[-1] = (flat[-2], flat[-1])
            flat = flat[:-2]
        if n > 0:
            corners[-1] = (flat[-2], flat[-1])
            flat = flat[:-2]
        if n < Z - 1:
            up[-1], down[-1] = flat
        if n == 0:
            slots.append(pick(z, [down[0], up[0], up[0], up[0]]))
        elif n == 1:
            slots.append(pick(z, [down[1], down[0], up[1], up[1]]))
        elif n == 2:
            slots.append(pick(z, [down[2], down[1], down[0], up[2]]))
        if n > 0:
            plane = pick(z, [jnp.int32(row[n - 1]) for row in SLOT_PLANES])
            pieces = (slots[n - 1],) + sides[n - 1] + corners[n - 1]
            out = put_plane(plane, here, core, pieces, out)
    return out.reshape(-1, BS, LANES)


def spread_sum(value):
    for bit in (1, 2, 4, 8):
        value = value + send(value, [(i, i ^ bit) for i in range(CHIPS)])
    return value + to_sibling(value)


def shards(
    x_in,
    cotangent,
    seq_lengths,
    weights,
    momentum,
    left_stat,
    right_stat,
    left_root,
    right_root,
    vectors,
    vector_sq,
):
    core = lax.axis_index("wt").astype(jnp.int32)
    place = lax.axis_index("seq").astype(jnp.int32)
    z, here, x = place // PLANE, place % PLANE, place % X
    y = here // X
    first_core = core == 0
    rows = x_in.shape[0]
    local_count = weights.shape[0]
    quad_count = local_count // 4
    first_quad = (place * CORES + core) * quad_count

    kept, sent = split_weights(core, first_quad, weights)
    quads = gather_weights(jnp.stack([kept, to_sibling(sent)]), z, here, core)
    quads, *wide = together(quads, *widen(momentum, left_root, right_root))

    both_x = jnp.concatenate([x_in, to_sibling(x_in)], axis=0)
    both_cot = jnp.concatenate([cotangent, to_sibling(cotangent)], axis=0)
    starts = jnp.stack([place * CORES + core, place * CORES + 1 - core]) * rows
    places = (starts[:, None] + jnp.arange(rows, dtype=jnp.int32)[None, :]).reshape(-1)
    keep_one, keep_two = keep_masks(places, seq_lengths)
    lane = jnp.arange(LANES)[None, :]
    keep = jnp.where(lane == 0, keep_one, jnp.where(lane == 1, keep_two, 0.0))
    taps = take(vectors[2:].reshape(3, IN_ROWS, 2, HALF), core, 2).reshape(3, D_HALF)

    hidden_both = both_x.astype(jnp.float32)
    scale_both = rms_scale(hidden_both)
    normed = (hidden_both * scale_both * vectors[0]).astype(jnp.bfloat16)
    hidden_in, scale_one = hidden_both[:rows], scale_both[:rows]
    mixed = mix(normed, quads)
    ends = jnp.stack([mixed[rows - 2 : rows], mixed[-2:]])
    ends = ends[:, :, :D_HALF] * ends[:, :, 2 * D_HALF :]
    carried = send(jnp.where(first_core, ends[1], ends[0]), [(i, i + 1) for i in range(CHIPS - 1)])
    halos = jnp.stack(
        [jnp.where(first_core, carried, ends[1]), jnp.where(first_core, ends[0], carried)]
    )
    conv_out, gated_out, part, other = conv_forward(mixed, halos, keep, taps, quads)
    middle = hidden_in + part + to_sibling(other)
    scale_two = rms_scale(middle)
    own_two = (middle * scale_two * vectors[1]).astype(jnp.bfloat16)
    normed_two = jnp.concatenate([own_two, to_sibling(own_two)], axis=0)
    activated, grad_gate, grad_up, grad_w_up, grad_w_down = ff_pass(normed_two, both_cot, quads)
    part, other = ff_back(grad_gate, grad_up, quads)
    grad_normed_two = part + to_sibling(other)
    gain_two_grad, middle_term = norm_back(middle, scale_two, vectors[1], grad_normed_two)
    grad_middle = cotangent.astype(jnp.float32) + middle_term
    own_branch = grad_middle.astype(jnp.bfloat16)
    grad_branch = jnp.concatenate([own_branch, to_sibling(own_branch)], axis=0)
    grad_w_gate, part, other = ff_rest(normed_two, activated, grad_gate, quads)
    out_act = (middle + part + to_sibling(other)).astype(jnp.bfloat16)
    grad_w_out, grad_conv, grad_output, heads, tap_grads = conv_back(
        grad_branch, mixed, conv_out, gated_out, halos, keep, taps, quads
    )
    from_after = send(
        jnp.where(first_core, heads[0], heads[1]), [(i + 1, i) for i in range(CHIPS - 1)]
    )
    tails = jnp.stack(
        [jnp.where(first_core, heads[1], from_after), jnp.where(first_core, from_after, heads[0])]
    )
    grad_w_in, part, other = mix_back(
        grad_conv, grad_output, mixed, normed, tails, keep, taps, quads
    )
    grad_normed = part + to_sibling(other)
    gain_one_grad, input_term = norm_back(hidden_in, scale_one, vectors[0], grad_normed)
    in_grad = grad_middle + input_term

    in_end, out_end, gate_end, up_end = quad_bounds()
    per_plane = BLOCKS // 4 // Z
    cut_gate = per_plane - out_end
    cut_up = 2 * per_plane - gate_end
    cut_down = 3 * per_plane - up_end
    planes = [
        jnp.concatenate([grad_w_in, grad_w_out, grad_w_gate[:cut_gate]], axis=0),
        jnp.concatenate([grad_w_gate[cut_gate:], grad_w_up[:cut_up]], axis=0),
        jnp.concatenate([grad_w_up[cut_up:], grad_w_down[:cut_down]], axis=0),
        grad_w_down[cut_down:],
    ]
    totals = [None] * Z
    for plane in reversed(range(Z)):
        totals[plane] = reduce_to_plane(scatter_plane(planes[plane], x, y), plane)
    total = pick(z, totals).astype(jnp.bfloat16).reshape(2, quad_count, BS, LANES)
    kept = take(total, core, 0)
    got = to_sibling(take(total, 1 - core, 0))

    tap_part = jnp.where(
        jnp.arange(2).reshape(1, 1, 2, 1) == core, tap_grads.reshape(3, IN_ROWS, 1, HALF), 0.0
    ).reshape(3, D)
    vector_grads = spread_sum(
        jnp.concatenate([gain_one_grad[None], gain_two_grad[None], tap_part], axis=0)
    )
    new_vector_sq = DECAY * vector_sq + (1.0 - DECAY) * vector_grads * vector_grads
    new_vectors = vectors - VEC_RATE * vector_grads * lax.rsqrt(new_vector_sq)

    new_momentum, precond, sums, kind_part = step_blocks(
        core, first_quad, kept, got, *wide, momentum
    )
    kind_sum = jnp.sum(spread_sum(kind_part), axis=1)[:KINDS]
    new_left, new_right = stats_blocks(sums, left_stat, right_stat)
    in_end, out_end, gate_end, up_end = block_bounds()
    kind_total = jnp.array(
        [in_end, out_end - in_end, gate_end - out_end, up_end - gate_end, BLOCKS - up_end],
        jnp.float32,
    ) * (BS * BS)
    kind_scale = lax.rsqrt(kind_sum / kind_total + MEAN_EPS)
    block_kinds = kind_of(first_quad + jnp.arange(local_count, dtype=jnp.int32) // 4)
    one_hot = (block_kinds[:, None] == jnp.arange(KINDS)[None, :]).astype(jnp.float32)
    block_scale = jnp.sum(one_hot * kind_scale[None, :], axis=1)
    new_weights = weights - RATE * block_scale[:, None] * precond
    return (
        out_act,
        in_grad,
        new_weights,
        new_weights.astype(jnp.bfloat16),
        new_momentum,
        new_left,
        new_right,
        vector_grads,
        new_vector_sq,
        new_vectors,
    )


def solution(mesh):
    body = shards if (mesh.shape["seq"], mesh.shape["wt"]) == (CHIPS, CORES) else shards_any
    return jax.shard_map(
        body,
        mesh=mesh,
        in_specs=(
            P(("seq", "wt"), None),
            P(("seq", "wt"), None),
            P(),
            P(("seq", "wt"), None),
            P(("seq", "wt"), None),
            P(("seq", "wt"), None),
            P(("seq", "wt"), None),
            P(("seq", "wt"), None),
            P(("seq", "wt"), None),
            P(),
            P(),
        ),
        out_specs=(
            P(("seq", "wt"), None),
            P(("seq", "wt"), None),
            P(("seq", "wt"), None),
            P(("seq", "wt"), None),
            P(("seq", "wt"), None),
            P(("seq", "wt"), None),
            P(("seq", "wt"), None),
            P(),
            P(),
            P(),
        ),
        check_vma=False,
    )
```

```python
import functools

import jax
import jax.numpy as jnp
from jax import lax
from jax.experimental import pallas as pl
from jax.experimental.pallas import tpu as pltpu
from jax.sharding import PartitionSpec as P

D = 1024
FF = 4608
BS = 64
BLOCKS = 4480


NORM_EPS = 1e-05
MEAN_EPS = 1e-06
DECAY = 0.5
MOMENT = 0.9
RATE = 0.01
VEC_RATE = 0.25
HIGHEST = lax.Precision.HIGHEST


def from_behind(block, axis, distance):
    devices = range(lax.axis_size(axis))
    route = [(i - distance, i) for i in devices if i - distance in devices]
    return lax.ppermute(block, axis, route)


def unpack_blocks(blocks, row_count, col_count):
    return (
        blocks.reshape(row_count // BS, col_count // BS, BS, BS)
        .transpose(0, 2, 1, 3)
        .reshape(row_count, col_count)
    )


def pack_blocks(matrix):
    row_count, col_count = matrix.shape
    return (
        matrix.reshape(row_count // BS, BS, col_count // BS, BS)
        .transpose(0, 2, 1, 3)
        .reshape(-1, BS * BS)
    )


def block_bounds():
    per_block = BS * BS
    in_end = 3 * D * D // per_block
    out_end = in_end + D * D // per_block
    gate_end = out_end + D * FF // per_block
    up_end = gate_end + D * FF // per_block
    return (in_end, out_end, gate_end, up_end)


def matrices(blocks):
    in_end, out_end, gate_end, up_end = block_bounds()
    w_in = unpack_blocks(blocks[:in_end], D, 3 * D)
    w_out = unpack_blocks(blocks[in_end:out_end], D, D)
    w_gate = unpack_blocks(blocks[out_end:gate_end], D, FF)
    w_up = unpack_blocks(blocks[gate_end:up_end], D, FF)
    w_down = unpack_blocks(blocks[up_end:], FF, D)
    return (w_in, w_out, w_gate, w_up, w_down)


def matmul(left_side, right_side):
    return jnp.dot(left_side, right_side, preferred_element_type=jnp.float32)


def matmul_tn(left_side, right_side):
    return lax.dot_general(
        left_side, right_side, (((0,), (0,)), ((), ())), preferred_element_type=jnp.float32
    )


def matmul_nt(left_side, right_side):
    return lax.dot_general(
        left_side, right_side, (((1,), (1,)), ((), ())), preferred_element_type=jnp.float32
    )


def rms_scale(values):
    return lax.rsqrt(jnp.mean(values * values, axis=-1, keepdims=True) + NORM_EPS)


def norm_back(values, row_scale, norm_gain, grad_normed):
    gain_grad = jnp.sum(grad_normed * values * row_scale, axis=0)
    weighted = grad_normed * norm_gain
    grad_values = row_scale * weighted - values * row_scale**3 * jnp.mean(
        weighted * values, axis=-1, keepdims=True
    )
    return (gain_grad, grad_values)


def keep_masks(places, seq_lengths):
    ends = jnp.cumsum(seq_lengths)
    starts = jnp.max(jnp.where(ends[None, :] <= places[:, None], ends[None, :], 0), axis=1)
    keep_one = (places - 1 >= starts).astype(jnp.float32)[:, None]
    keep_two = (places - 2 >= starts).astype(jnp.float32)[:, None]
    return (keep_one, keep_two)


def weight_grads(operands):
    (
        normed,
        grad_mixed,
        gated_out,
        grad_branch,
        normed_two,
        grad_gate,
        grad_up,
        activated,
        cotangent,
    ) = operands
    return jnp.concatenate(
        [
            pack_blocks(matmul_tn(normed, grad_mixed)),
            pack_blocks(matmul_tn(gated_out, grad_branch)),
            pack_blocks(matmul_tn(normed_two, grad_gate)),
            pack_blocks(matmul_tn(normed_two, grad_up)),
            pack_blocks(matmul_tn(activated, cotangent)),
        ],
        axis=0,
    )


def shards_any(
    x_in,
    cotangent,
    seq_lengths,
    weights,
    momentum,
    left_stat,
    right_stat,
    left_root,
    right_root,
    vectors,
    vector_sq,
):
    gathered = lax.all_gather(weights.astype(jnp.bfloat16), ("seq", "wt"), axis=0, tiled=True)
    w_in, w_out, w_gate, w_up, w_down = matrices(gathered)
    row_count = x_in.shape[0]
    places = lax.axis_index(("seq", "wt")) * row_count + jnp.arange(row_count, dtype=jnp.int32)
    keep_one, keep_two = keep_masks(places, seq_lengths)
    hidden_in = x_in.astype(jnp.float32)
    scale_one = rms_scale(hidden_in)
    normed = (hidden_in * scale_one * vectors[0]).astype(jnp.bfloat16)
    mixed = matmul(normed, w_in)
    input_gate = mixed[:, :D]
    output_gate = mixed[:, D : 2 * D]
    values = mixed[:, 2 * D :]
    driven = input_gate * values
    carried = from_behind(driven[-2:], ("seq", "wt"), 1)
    extended = jnp.concatenate([carried, driven], axis=0)
    conv_out = (
        vectors[4] * driven
        + vectors[3] * keep_one * extended[1:-1]
        + vectors[2] * keep_two * extended[:-2]
    )
    gated_out = (output_gate * conv_out).astype(jnp.bfloat16)
    middle = hidden_in + matmul(gated_out, w_out)
    scale_two = rms_scale(middle)
    normed_two = (middle * scale_two * vectors[1]).astype(jnp.bfloat16)
    gate_ff = matmul(normed_two, w_gate)
    up_ff = matmul(normed_two, w_up)
    sigmoid_gate = jax.nn.sigmoid(gate_ff)
    silu_value = gate_ff * sigmoid_gate
    activated = (silu_value * up_ff).astype(jnp.bfloat16)
    out_act = (middle + matmul(activated, w_down)).astype(jnp.bfloat16)
    grad_act = matmul_nt(cotangent, w_down)
    grad_gate = (grad_act * up_ff * sigmoid_gate * (1.0 + gate_ff * (1.0 - sigmoid_gate))).astype(
        jnp.bfloat16
    )
    grad_up = (grad_act * silu_value).astype(jnp.bfloat16)
    grad_normed_two = matmul_nt(grad_gate, w_gate) + matmul_nt(grad_up, w_up)
    gain_two_grad, middle_term = norm_back(middle, scale_two, vectors[1], grad_normed_two)
    grad_middle = cotangent.astype(jnp.float32) + middle_term
    grad_branch = grad_middle.astype(jnp.bfloat16)
    grad_gated = matmul_nt(grad_branch, w_out)
    grad_output_gate = grad_gated * conv_out
    grad_conv = grad_gated * output_gate
    early_one = keep_one * grad_conv
    early_two = keep_two * grad_conv
    tap_zero = jnp.sum(early_two * extended[:-2], axis=0)
    tap_first = jnp.sum(early_one * extended[1:-1], axis=0)
    tap_second = jnp.sum(grad_conv * driven, axis=0)
    sent_back = jnp.stack(
        [vectors[2] * early_two[0], vectors[3] * early_one[0] + vectors[2] * early_two[1]], axis=0
    )
    from_after = from_behind(sent_back, ("seq", "wt"), -1)
    zero_rows = jnp.zeros((2, D), jnp.float32)
    grad_driven = vectors[4] * grad_conv
    grad_driven = grad_driven + vectors[3] * jnp.concatenate([early_one[1:], zero_rows[:1]], axis=0)
    grad_driven = grad_driven + vectors[2] * jnp.concatenate([early_two[2:], zero_rows], axis=0)
    grad_driven = grad_driven + jnp.concatenate(
        [jnp.zeros((row_count - 2, D), jnp.float32), from_after], axis=0
    )
    grad_mixed = jnp.concatenate(
        [grad_driven * values, grad_output_gate, grad_driven * input_gate], axis=1
    ).astype(jnp.bfloat16)
    grad_normed = matmul_nt(grad_mixed, w_in)
    gain_one_grad, input_term = norm_back(hidden_in, scale_one, vectors[0], grad_normed)
    in_grad = grad_middle + input_term
    paired = (
        lax.all_gather(normed, "wt", axis=0, tiled=True),
        lax.all_gather(grad_mixed, "wt", axis=0, tiled=True),
        lax.all_gather(gated_out, "wt", axis=0, tiled=True),
        lax.all_gather(grad_branch, "wt", axis=0, tiled=True),
        lax.all_gather(normed_two, "wt", axis=0, tiled=True),
        lax.all_gather(grad_gate, "wt", axis=0, tiled=True),
        lax.all_gather(grad_up, "wt", axis=0, tiled=True),
        lax.all_gather(activated, "wt", axis=0, tiled=True),
        lax.all_gather(cotangent, "wt", axis=0, tiled=True),
    )
    pair_grads = weight_grads(paired)
    seq_count = lax.axis_size("seq")
    core_count = lax.axis_size("wt")
    owned_count = pair_grads.shape[0] // (seq_count * core_count)
    arranged = pair_grads.reshape(seq_count, core_count, owned_count, BS * BS)
    mine = lax.dynamic_index_in_dim(arranged, lax.axis_index("wt"), 1, keepdims=False).reshape(
        seq_count * owned_count, BS * BS
    )
    summed_flat = lax.psum_scatter(mine, "seq", scatter_dimension=0, tiled=True)
    vector_part = jnp.stack([gain_one_grad, gain_two_grad, tap_zero, tap_first, tap_second], axis=0)
    local_count = summed_flat.shape[0]
    summed = summed_flat.reshape(local_count, BS, BS)
    left_blocks = left_stat.reshape(local_count, BS, BS)
    right_blocks = right_stat.reshape(local_count, BS, BS)
    momentum_blocks = momentum.reshape(local_count, BS, BS)
    left_factor = left_root.reshape(local_count, BS, BS)
    right_factor = right_root.reshape(local_count, BS, BS)
    new_left = DECAY * left_blocks + (1.0 - DECAY) * jnp.einsum(
        "kij,klj->kil", summed, summed, precision=HIGHEST
    )
    new_right = DECAY * right_blocks + (1.0 - DECAY) * jnp.einsum(
        "kji,kjl->kil", summed, summed, precision=HIGHEST
    )
    new_momentum = MOMENT * momentum_blocks + summed
    precond = jnp.einsum("kij,kjl->kil", left_factor, new_momentum, precision=HIGHEST)
    precond = jnp.einsum("kij,kjl->kil", precond, right_factor, precision=HIGHEST)
    precond_flat = precond.reshape(local_count, BS * BS)
    square = jnp.sum(precond_flat * precond_flat, axis=1)
    in_end, out_end, gate_end, up_end = block_bounds()
    block_ids = lax.axis_index(("seq", "wt")) * local_count + jnp.arange(
        local_count, dtype=jnp.int32
    )
    kind_index = (
        (block_ids >= in_end).astype(jnp.int32)
        + (block_ids >= out_end).astype(jnp.int32)
        + (block_ids >= gate_end).astype(jnp.int32)
        + (block_ids >= up_end).astype(jnp.int32)
    )
    one_hot = (kind_index[:, None] == jnp.arange(5, dtype=jnp.int32)[None, :]).astype(jnp.float32)
    kind_part = jnp.sum(one_hot * square[:, None], axis=0)
    vector_grads, kind_sum = lax.psum((vector_part, kind_part), ("seq", "wt"))
    kind_total = jnp.array(
        [in_end, out_end - in_end, gate_end - out_end, up_end - gate_end, BLOCKS - up_end],
        jnp.float32,
    ) * (BS * BS)
    kind_scale = lax.rsqrt(kind_sum / kind_total + MEAN_EPS)
    block_scale = jnp.sum(one_hot * kind_scale[None, :], axis=1)
    new_weights = weights - RATE * block_scale[:, None] * precond_flat
    weight_copy = new_weights.astype(jnp.bfloat16)
    new_vector_sq = DECAY * vector_sq + (1.0 - DECAY) * vector_grads * vector_grads
    new_vectors = vectors - VEC_RATE * vector_grads * lax.rsqrt(new_vector_sq)
    flat_shape = (local_count, BS * BS)
    return (
        out_act,
        in_grad,
        new_weights,
        weight_copy,
        new_momentum.reshape(flat_shape),
        new_left.reshape(flat_shape),
        new_right.reshape(flat_shape),
        vector_grads,
        new_vector_sq,
        new_vectors,
    )


Z, Y, X = 4, 2, 2
CHIPS, CORES = Z * Y * X, 2
PLANE = Y * X
HALF = BS // 2
SWAP = [(0, 1), (1, 0)]


def chip(z, y, x):
    return (z * Y + y) * X + x


def plane_route(pairs):
    return [(chip(a, y, x), chip(b, y, x)) for a, b in pairs for y in range(Y) for x in range(X)]


ACROSS_X = [(i, i ^ 1) for i in range(CHIPS)]
ACROSS_Y = [(i, i ^ 2) for i in range(CHIPS)]


def send(block, route):
    return lax.ppermute(block, "seq", route)


def to_sibling(block):
    return lax.ppermute(block, "wt", SWAP)


def quad_bounds():
    return tuple(b // 4 for b in block_bounds())


def pick(place, options):
    out = options[0]
    for i, option in enumerate(options[1:], 1):
        out = jnp.where(place == i, option, out)
    return out


def take(array, index, axis):
    return lax.dynamic_index_in_dim(array, index, axis, keepdims=False)


QUAD = 4 * BS
LANES = 128
KINDS = 5
VMEM_LIMIT = 24 * 1024 * 1024
VMEM_ALL = 62 * 1024 * 1024


def busy(micros):
    return pl.CostEstimate(flops=0, bytes_accessed=int(micros * 3e6), transcendentals=0)


def lane_ids(rows):
    return lax.broadcasted_iota(jnp.int32, (rows, LANES), 1)


def strided(ref, part, start, count, stride):
    return ref[part, pl.ds(start, count, stride=stride), :]


def columns(flat_ref, cols_ref):
    for k in range(cols_ref.shape[0]):
        cols_ref[k] = flat_ref[:, pl.ds(k * LANES, LANES)]


def cols_to_wide(cols_ref, wide_ref, count):
    low = lane_ids(count) < BS
    for k in range(BS // 2):
        parts = [strided(cols_ref, k, b, count, 4) for b in range(4)]
        turned = [pltpu.roll(p, BS, 1) for p in parts]
        for t in range(2):
            a, b = 2 * t, 2 * t + 1
            even = jnp.where(low, parts[a], turned[b])
            odd = jnp.where(low, turned[a], parts[b])
            wide_ref[t, pl.ds(2 * k, count, stride=BS), :] = even
            wide_ref[t, pl.ds(2 * k + 1, count, stride=BS), :] = odd


def wide_to_cols(wide_ref, cols_ref, count):
    low = lane_ids(count) < BS
    for k in range(BS // 2):
        for t in range(2):
            even = strided(wide_ref, t, 2 * k, count, BS)
            odd = strided(wide_ref, t, 2 * k + 1, count, BS)
            a, b = 2 * t, 2 * t + 1
            cols_ref[k, pl.ds(a, count, stride=4), :] = jnp.where(
                low, even, pltpu.roll(odd, BS, 1)
            )
            cols_ref[k, pl.ds(b, count, stride=4), :] = jnp.where(
                low, pltpu.roll(even, BS, 1), odd
            )


def join(wide_ref, rows):
    return jnp.concatenate([wide_ref[0, rows, :], wide_ref[1, rows, :]], axis=1)


def cut(wide_ref, rows, value):
    wide_ref[0, rows, :] = value[:, :LANES].astype(wide_ref.dtype)
    wide_ref[1, rows, :] = value[:, LANES:].astype(wide_ref.dtype)


def cols_shape(flat):
    return (flat.shape[1] // LANES, flat.shape[0], LANES)


def kind_of(quad):
    kind = jnp.int32(0)
    for bound in quad_bounds():
        kind = kind + (quad >= bound).astype(jnp.int32)
    return kind


def is_row_kind(kind):
    return (kind == 1) | (kind == 4)


def split_weights_kernel(place_ref, flat_ref, kept_ref, sent_ref, cols_ref, col_ref, row_ref):
    count = flat_ref.shape[0] // 4
    core, first = place_ref[0], place_ref[1]
    group = lane_ids(count) // HALF
    low = group < 2
    columns(flat_ref, cols_ref)
    for k in range(BS // 2):
        parts = [strided(cols_ref, k, b, count, 4) for b in range(4)]
        rolls = [[p] + [pltpu.roll(p, s * HALF, 1) for s in (1, 2, 3)] for p in parts]
        for odd in range(2):
            r = 2 * k + odd
            for half in range(2):
                g = 2 * odd + half
                out = rolls[0][(0 - g) % 4]
                for b in range(1, 4):
                    out = jnp.where(group == b, rolls[b][(b - g) % 4], out)
                col_ref[half, pl.ds(r, count, stride=BS), :] = out
            for t in range(2):
                a, b = 2 * t, 2 * t + 1
                if odd:
                    out = jnp.where(low, rolls[a][2], parts[b])
                else:
                    out = jnp.where(low, parts[a], rolls[b][2])
                row_ref[r // HALF, pl.ds(t * HALF + r % HALF, count, stride=BS), :] = out

    def finish(q, carry):
        rows = pl.ds(pl.multiple_of(q * BS, BS), BS)
        by_row = is_row_kind(kind_of(first + q))
        for ref, half in ((kept_ref, core), (sent_ref, 1 - core)):
            value = jnp.where(by_row, row_ref[half, rows, :], col_ref[half, rows, :])
            ref[q] = value.astype(ref.dtype)
        return carry

    lax.fori_loop(0, count, finish, 0)


def whole(n):
    return [pl.BlockSpec(memory_space=pltpu.VMEM)] * n


SCALARS = pl.BlockSpec(memory_space=pltpu.SMEM)


def split_weights(core, first, weights):
    count = weights.shape[0] // 4
    quads = jax.ShapeDtypeStruct((count, BS, LANES), jnp.bfloat16)
    return pl.pallas_call(
        split_weights_kernel,
        out_shape=(quads, quads),
        in_specs=[SCALARS] + whole(1),
        out_specs=tuple(whole(2)),
        scratch_shapes=[pltpu.VMEM(cols_shape(weights), jnp.float32)]
        + [pltpu.VMEM((2, count * BS, LANES), jnp.float32)] * 2,
        compiler_params=pltpu.CompilerParams(vmem_limit_bytes=VMEM_LIMIT),
        cost_estimate=busy(8),
    )(jnp.stack([core, first]), weights)


def widen_kernel(momentum_ref, left_ref, right_ref, mom_ref, lw_ref, rw_ref, cols_ref, wide_ref):
    count = momentum_ref.shape[0] // 4
    columns(momentum_ref, cols_ref)
    cols_to_wide(cols_ref, mom_ref, count)
    for src, dst in ((left_ref, lw_ref), (right_ref, rw_ref)):
        columns(src, cols_ref)
        cols_to_wide(cols_ref, wide_ref, count)
        dst[...] = wide_ref[...].astype(dst.dtype)


def widen(momentum, left_root, right_root):
    shape = (2, momentum.shape[0] // 4 * BS, LANES)
    return pl.pallas_call(
        widen_kernel,
        out_shape=(
            jax.ShapeDtypeStruct(shape, jnp.float32),
            jax.ShapeDtypeStruct(shape, jnp.bfloat16),
            jax.ShapeDtypeStruct(shape, jnp.bfloat16),
        ),
        in_specs=whole(3),
        out_specs=tuple(whole(3)),
        scratch_shapes=[
            pltpu.VMEM(cols_shape(momentum), jnp.float32),
            pltpu.VMEM(shape, jnp.float32),
        ],
        compiler_params=pltpu.CompilerParams(vmem_limit_bytes=VMEM_LIMIT),
        cost_estimate=busy(11),
    )(momentum, left_root, right_root)


def diagonal(wide, mask):
    return jnp.where(mask, jnp.concatenate([wide] * 4, axis=0), jnp.zeros((), wide.dtype))


def diagonal_mask():
    rows = lax.broadcasted_iota(jnp.int32, (QUAD, QUAD), 0) // BS
    cols = lax.broadcasted_iota(jnp.int32, (QUAD, QUAD), 1) // BS
    return rows == cols


def wide_sum(kept, got, core, by_row):
    first = jnp.where(core == 0, kept, got)
    second = jnp.where(core == 0, got, kept)
    group = lane_ids(BS) // HALF
    tiles = []
    for t in range(2):
        pieces = (
            (first, 2 * t, 0),
            (second, 2 * t, 1),
            (first, 2 * t + 1, 2),
            (second, 2 * t + 1, 3),
        )
        out = None
        for value, source, target in pieces:
            shift = (target - source) * HALF % LANES
            moved = value if shift == 0 else pltpu.roll(value, shift, 1)
            out = moved if out is None else jnp.where(group == target, moved, out)
        rows = slice(t * HALF, (t + 1) * HALF)
        tiles.append(
            jnp.where(by_row, jnp.concatenate([first[rows], second[rows]], axis=0), out)
        )
    return jnp.concatenate(tiles, axis=1)


def step_kernel(
    place_ref, kept_ref, got_ref, mom_ref, lw_ref, rw_ref, flat_ref,
    new_mom_ref, precond_ref, wide_ref, kind_ref, cols_ref, sum_ref, step_ref,
):
    count = kept_ref.shape[0]
    core, first = place_ref[0], place_ref[1]
    mask = diagonal_mask()
    kind_ref[...] = jnp.zeros_like(kind_ref)

    def one(q, carry):
        rows = pl.ds(pl.multiple_of(q * BS, BS), BS)
        kind = kind_of(first + q)
        total = wide_sum(
            kept_ref[q].astype(jnp.float32), got_ref[q].astype(jnp.float32), core, is_row_kind(kind)
        )
        cut(sum_ref, rows, total)
        wide_ref[rows, :] = total.astype(jnp.bfloat16)
        moment = (MOMENT * join(mom_ref, rows) + total).astype(jnp.bfloat16)
        inner = jnp.dot(
            join(lw_ref, rows), diagonal(moment, mask), preferred_element_type=jnp.float32
        ).astype(jnp.bfloat16)
        step = jnp.dot(
            inner, diagonal(join(rw_ref, rows), mask), preferred_element_type=jnp.float32
        )
        cut(step_ref, rows, step)
        square = jnp.sum(step * step, axis=0, keepdims=True)
        kind_ref[pl.ds(kind, 1), :] += square[:, :LANES] + square[:, LANES:]
        return carry

    lax.fori_loop(0, count, one, 0, unroll=5)

    wide_to_cols(sum_ref, cols_ref, count)
    for k in range(cols_ref.shape[0]):
        lanes = pl.ds(k * LANES, LANES)
        new_mom_ref[:, lanes] = MOMENT * flat_ref[:, lanes] + cols_ref[k]
    wide_to_cols(step_ref, cols_ref, count)
    for k in range(cols_ref.shape[0]):
        precond_ref[:, pl.ds(k * LANES, LANES)] = cols_ref[k]


def step_blocks(core, first, kept, got, mom_wide, left_wide, right_wide, momentum):
    count = kept.shape[0]
    rows = count * BS
    flat = jax.ShapeDtypeStruct(momentum.shape, jnp.float32)
    return pl.pallas_call(
        step_kernel,
        out_shape=(
            flat,
            flat,
            jax.ShapeDtypeStruct((rows, QUAD), jnp.bfloat16),
            jax.ShapeDtypeStruct((8, LANES), jnp.float32),
        ),
        in_specs=[SCALARS] + whole(6),
        out_specs=tuple(whole(4)),
        scratch_shapes=[pltpu.VMEM(cols_shape(momentum), jnp.float32)]
        + [pltpu.VMEM((2, rows, LANES), jnp.float32)] * 2,
        compiler_params=pltpu.CompilerParams(vmem_limit_bytes=VMEM_LIMIT),
        cost_estimate=busy(13),
    )(jnp.stack([core, first]), kept, got, mom_wide, left_wide, right_wide, momentum)


def stat_kernel(turned, wide_ref, old_ref, new_ref, cols_ref, gram_ref):
    count = wide_ref.shape[0] // BS
    mask = diagonal_mask()

    def one(q, carry):
        rows = pl.ds(pl.multiple_of(q * BS, BS), BS)
        total = wide_ref[rows, :]
        if turned:
            gram = lax.dot_general(
                total, total, (((0,), (0,)), ((), ())), preferred_element_type=jnp.float32
            )
            gram = jnp.where(mask, gram, 0.0)
            gram = gram[:BS] + gram[BS : 2 * BS] + gram[2 * BS : 3 * BS] + gram[3 * BS :]
        else:
            gram = lax.dot_general(
                total, diagonal(total, mask), (((1,), (1,)), ((), ())),
                preferred_element_type=jnp.float32,
            )
        cut(gram_ref, rows, gram)
        return carry

    lax.fori_loop(0, count, one, 0, unroll=5)
    wide_to_cols(gram_ref, cols_ref, count)
    for k in range(cols_ref.shape[0]):
        lanes = pl.ds(k * LANES, LANES)
        new_ref[:, lanes] = DECAY * old_ref[:, lanes] + (1.0 - DECAY) * cols_ref[k]


def stat_blocks(wide, stat, turned):
    return pl.pallas_call(
        functools.partial(stat_kernel, turned),
        out_shape=jax.ShapeDtypeStruct(stat.shape, jnp.float32),
        in_specs=whole(2),
        out_specs=whole(1)[0],
        scratch_shapes=[
            pltpu.VMEM(cols_shape(stat), jnp.float32),
            pltpu.VMEM((2, wide.shape[0], LANES), jnp.float32),
        ],
        compiler_params=pltpu.CompilerParams(vmem_limit_bytes=VMEM_LIMIT),
        cost_estimate=busy(6),
    )(wide, stat)


TILE = 768
QUADS_WIDE = TILE // LANES
OUT_TILE = 256


def f32_dot(a, b, dims=((1,), (0,))):
    return lax.dot_general(a, b, (dims, ((), ())), preferred_element_type=jnp.float32)


def nt_dot(a, b):
    return f32_dot(a, b, ((1,), (1,)))


def col_tile(ref, rows, per_row, j, width=2):
    parts = [
        jnp.concatenate([ref[i * per_row + j + d] for i in range(rows)], axis=0)
        for d in range(width)
    ]
    return jnp.concatenate(parts, axis=1)


def col_rows(ref, first, rows, per_row):
    return jnp.concatenate(
        [
            jnp.concatenate([ref[(first + i) * per_row + j] for j in range(per_row)], axis=1)
            for i in range(rows)
        ],
        axis=0,
    )


def row_rows(ref, first, rows, per_row):
    return jnp.concatenate(
        [
            jnp.concatenate(
                [
                    ref[(first + i) * per_row + j, h * HALF : (h + 1) * HALF]
                    for j in range(per_row)
                    for h in range(2)
                ],
                axis=1,
            )
            for i in range(rows)
        ],
        axis=0,
    )


def row_tile(ref, rows, per_row, j):
    parts = [
        jnp.concatenate(
            [ref[i * per_row + j, h * HALF : (h + 1) * HALF] for i in range(rows)], axis=0
        )
        for h in range(2)
    ]
    return jnp.concatenate(parts, axis=1)


def put_col_tile(ref, value, rows, per_row, j, width=2):
    value = value.astype(ref.dtype)
    for i in range(rows):
        for d in range(width):
            ref[i * per_row + j + d] = value[i * BS : (i + 1) * BS, d * LANES : (d + 1) * LANES]


def put_row_rows(ref, value, first, rows, per_row):
    value = value.astype(ref.dtype)
    for i in range(rows):
        for j in range(per_row):
            for h in range(2):
                part = value[
                    i * HALF : (i + 1) * HALF, (2 * j + h) * LANES : (2 * j + h + 1) * LANES
                ]
                ref[(first + i) * per_row + j, h * HALF : (h + 1) * HALF] = part


def put_part(own_ref, other_ref, cols, value):
    rows = own_ref.shape[0]
    own_ref[:, cols] = value[:rows]
    other_ref[:, cols] = value[rows:]


def parts(rows):
    return [shape((rows // 2, D), jnp.float32)] * 2


def call(kernel, outs, ins, scratch=(), micros=0, any_in=(), any_out=(), limit=VMEM_ALL):
    def specs(count, far):
        return [
            pl.BlockSpec(memory_space=pltpu.HBM if i in far else pltpu.VMEM) for i in range(count)
        ]

    return pl.pallas_call(
        kernel,
        out_shape=tuple(jax.ShapeDtypeStruct(o.shape, o.dtype) for o in outs),
        in_specs=specs(len(ins), any_in),
        out_specs=tuple(specs(len(outs), any_out)),
        scratch_shapes=list(scratch),
        compiler_params=pltpu.CompilerParams(vmem_limit_bytes=limit),
        cost_estimate=busy(micros),
    )(*ins)


def shape(dims, dtype):
    return jax.ShapeDtypeStruct(dims, dtype)


IN_ROWS = D // BS
IN_COLS = 3 * D // 256
OUT_COLS = D // 256
FF_COLS = FF // 256
DOWN_ROWS = FF // BS
FF_HALF = FF // 2
D_HALF = D // 2


def fetch(quads_ref, first, count, into, sem):
    return pltpu.make_async_copy(quads_ref.at[pl.ds(first, count)], into, sem)


def mix_kernel(normed_ref, quads_ref, mixed_ref, w_ref, sems):
    step = 4 * IN_COLS
    copies = [
        fetch(quads_ref, g * step, step, w_ref.at[pl.ds(g * step, step)], sems.at[g])
        for g in range(IN_ROWS // 4)
    ]
    for c in copies:
        c.start()
    for c in copies:
        c.wait()

    def tile(t, carry):
        cols = pl.ds(pl.multiple_of(t * TILE, TILE), TILE)
        mixed_ref[:, cols] = f32_dot(
            normed_ref[...], col_tile(w_ref, IN_ROWS, IN_COLS, QUADS_WIDE * t, QUADS_WIDE)
        )
        return carry

    lax.fori_loop(0, IN_COLS // QUADS_WIDE, tile, 0)


def mix(normed, quads):
    rows = normed.shape[0]
    return call(
        mix_kernel,
        [shape((rows, 3 * D_HALF), jnp.float32)],
        [normed, quads],
        [
            pltpu.VMEM((IN_ROWS * IN_COLS, BS, LANES), jnp.bfloat16),
            pltpu.SemaphoreType.DMA((IN_ROWS // 4,)),
        ],
        micros=7,
        any_in=(1,),
    )[0]


def shift_down(value, halo, distance):
    moved = pltpu.roll(value, distance, 0)
    row = lax.broadcasted_iota(jnp.int32, value.shape, 0)
    out = jnp.where(row == 0, halo[2 - distance : 3 - distance], moved)
    if distance == 2:
        out = jnp.where(row == 1, halo[1:2], out)
    return out


def shift_up(value, distance):
    count = value.shape[0]
    moved = pltpu.roll(value, count - distance, 0)
    row = lax.broadcasted_iota(jnp.int32, value.shape, 0)
    return jnp.where(row < count - distance, moved, 0.0)


def conv_kernel(
    mixed_ref, halo_ref, keep_ref, taps_ref, quads_ref,
    conv_ref, gated_ref, own_ref, other_ref,
    w_ref, sem,
):
    first = 3 * IN_ROWS * OUT_COLS
    copy = fetch(quads_ref, first, IN_ROWS * OUT_COLS, w_ref, sem)
    copy.start()
    rows = mixed_ref.shape[0] // 2
    for s in range(2):
        at = pl.ds(s * rows, rows)
        driven = mixed_ref[at, :D_HALF] * mixed_ref[at, 2 * D_HALF :]
        halo = halo_ref[s]
        conv = (
            taps_ref[2:3] * driven
            + taps_ref[1:2] * keep_ref[at, 0:1] * shift_down(driven, halo, 1)
            + taps_ref[0:1] * keep_ref[at, 1:2] * shift_down(driven, halo, 2)
        )
        conv_ref[at, :] = conv
        gated_ref[at, :] = (mixed_ref[at, D_HALF : 2 * D_HALF] * conv).astype(jnp.bfloat16)
    copy.wait()
    for j in range(OUT_COLS):
        value = f32_dot(gated_ref[...], row_tile(w_ref, IN_ROWS, OUT_COLS, j))
        put_part(own_ref, other_ref, slice(j * OUT_TILE, (j + 1) * OUT_TILE), value)


def conv_forward(mixed, halos, keep, taps, quads):
    rows = mixed.shape[0]
    return call(
        conv_kernel,
        [
            shape((rows, D_HALF), jnp.float32),
            shape((rows, D_HALF), jnp.bfloat16),
        ]
        + parts(rows),
        [mixed, halos, keep, taps, quads],
        [
            pltpu.VMEM((IN_ROWS * OUT_COLS, BS, LANES), jnp.bfloat16),
            pltpu.SemaphoreType.DMA(()),
        ],
        micros=5,
        any_in=(4,),
    )


def ff_kernel(
    normed_ref, cot_ref, quads_ref, act_ref, gg_ref, gu_ref, gate_ref, up_ref, down_ref, sems
):
    _, out_end, gate_end, up_end = quad_bounds()
    per = IN_ROWS * FF_COLS
    copies = [
        fetch(quads_ref, first, per, ref, sems.at[n])
        for n, (first, ref) in enumerate(
            ((out_end, gate_ref), (gate_end, up_ref), (up_end, down_ref))
        )
    ]
    for c in copies:
        c.start()
    step = TILE // HALF

    def tile(t, wait):
        cols = pl.ds(pl.multiple_of(t * TILE, TILE), TILE)
        if wait:
            copies[0].wait()
        gate = f32_dot(
            normed_ref[...], col_tile(gate_ref, IN_ROWS, FF_COLS, QUADS_WIDE * t, QUADS_WIDE)
        )
        if wait:
            copies[1].wait()
        up = f32_dot(
            normed_ref[...], col_tile(up_ref, IN_ROWS, FF_COLS, QUADS_WIDE * t, QUADS_WIDE)
        )
        if wait:
            copies[2].wait()
        grad_act = nt_dot(cot_ref[...], row_rows(down_ref, step * t, step, OUT_COLS))
        sig = jax.nn.sigmoid(gate)
        silu = gate * sig
        act_ref[:, cols] = (silu * up).astype(jnp.bfloat16)
        gg_ref[:, cols] = (grad_act * up * sig * (1.0 + gate * (1.0 - sig))).astype(jnp.bfloat16)
        gu_ref[:, cols] = (grad_act * silu).astype(jnp.bfloat16)

    tile(0, True)

    def later(t, carry):
        tile(t, False)
        return carry

    lax.fori_loop(1, FF_HALF // TILE, later, 0)


def ff_pass(normed, cot, quads):
    rows = normed.shape[0]
    wide = shape((rows, FF_HALF), jnp.bfloat16)
    weights = pltpu.VMEM((IN_ROWS * FF_COLS, BS, LANES), jnp.bfloat16)
    return call(
        ff_kernel,
        [wide] * 3,
        [normed, cot, quads],
        [weights] * 3 + [pltpu.SemaphoreType.DMA((3,))],
        micros=15,
        any_in=(2,),
    )


BACK_ROWS = 8


def ff_back_kernel(gg_ref, gu_ref, quads_ref, own_ref, other_ref, gate_ref, up_ref, sems):
    _, out_end, gate_end, _ = quad_bounds()
    step = BACK_ROWS * FF_COLS
    groups = IN_ROWS // BACK_ROWS
    copies = []
    for g in range(groups):
        at = pl.ds(g * step, step)
        copies.append(fetch(quads_ref, out_end + g * step, step, gate_ref.at[at], sems.at[0, g]))
        copies.append(fetch(quads_ref, gate_end + g * step, step, up_ref.at[at], sems.at[1, g]))
    for c in copies:
        c.start()
    for g in range(groups):
        copies[2 * g].wait()
        value = nt_dot(gg_ref[...], col_rows(gate_ref, BACK_ROWS * g, BACK_ROWS, FF_COLS))
        copies[2 * g + 1].wait()
        value = value + nt_dot(
            gu_ref[...], col_rows(up_ref, BACK_ROWS * g, BACK_ROWS, FF_COLS)
        )
        put_part(own_ref, other_ref, slice(g * BACK_ROWS * BS, (g + 1) * BACK_ROWS * BS), value)


def ff_back(gg, gu, quads):
    rows = gg.shape[0]
    weights = pltpu.VMEM((IN_ROWS * FF_COLS, BS, LANES), jnp.bfloat16)
    return call(
        ff_back_kernel,
        parts(rows),
        [gg, gu, quads],
        [weights, weights, pltpu.SemaphoreType.DMA((2, IN_ROWS // BACK_ROWS))],
        micros=11,
        any_in=(2,),
    )


def down_grad_kernel(normed_ref, act_ref, gg_ref, cot_ref, ddown_ref, dgate_ref):
    step = TILE // HALF

    def tile(t, carry):
        cols = pl.ds(pl.multiple_of(t * TILE, TILE), TILE)
        put_row_rows(
            ddown_ref, f32_dot(act_ref[:, cols].T, cot_ref[...]), step * t, step, OUT_COLS
        )
        return carry

    lax.fori_loop(0, FF_HALF // TILE, tile, 0)
    turned = normed_ref[:, : 2 * BS].T
    ahead = dgate_ref.shape[0] - FF_COLS
    first = f32_dot(turned[:BS], gg_ref[...]).astype(jnp.bfloat16)
    second = f32_dot(turned[BS:], gg_ref[:, : ahead * LANES]).astype(jnp.bfloat16)
    for j in range(FF_COLS):
        dgate_ref[j] = first[:, j * LANES : (j + 1) * LANES]
    for j in range(ahead):
        dgate_ref[FF_COLS + j] = second[:, j * LANES : (j + 1) * LANES]


PER_PLANE = BLOCKS // 4 // Z


def down_grad(normed, act, gg, cot):
    return call(
        down_grad_kernel,
        [
            shape((DOWN_ROWS * OUT_COLS, BS, LANES), jnp.bfloat16),
            shape((PER_PLANE - quad_bounds()[1], BS, LANES), jnp.bfloat16),
        ],
        [normed, act, gg, cot],
        micros=6,
    )


def ff_rest_kernel(
    normed_ref, act_ref, gg_ref, gu_ref, ddown_ref, quads_ref,
    grads_ref, own_ref, other_ref,
    dgate_ref, dup_ref, down_ref, turned_ref, sems,
):
    _, out_end, gate_end, up_end = quad_bounds()
    per = IN_ROWS * FF_COLS
    ahead = PER_PLANE - out_end
    behind = 3 * PER_PLANE - up_end
    weights = fetch(quads_ref, up_end, DOWN_ROWS * OUT_COLS, down_ref, sems.at[0])
    weights.start()
    moves = [
        pltpu.make_async_copy(
            ddown_ref,
            grads_ref.at[pl.ds(2 * per - ahead, behind)],
            sems.at[1],
        ),
        pltpu.make_async_copy(
            dgate_ref.at[pl.ds(ahead, per - ahead)],
            grads_ref.at[pl.ds(0, per - ahead)],
            sems.at[2],
        ),
        pltpu.make_async_copy(dup_ref, grads_ref.at[pl.ds(per - ahead, per)], sems.at[3]),
    ]
    moves[0].start()
    turned_ref[...] = normed_ref[...].T

    def weight_grad(grad_ref, out_ref):
        def tile(t, carry):
            cols = pl.ds(pl.multiple_of(t * TILE, TILE), TILE)
            put_col_tile(
                out_ref,
                f32_dot(turned_ref[...], grad_ref[:, cols]),
                IN_ROWS,
                FF_COLS,
                QUADS_WIDE * t,
                QUADS_WIDE,
            )
            return carry

        lax.fori_loop(0, FF_HALF // TILE, tile, 0)

    weight_grad(gg_ref, dgate_ref)
    moves[1].start()
    weight_grad(gu_ref, dup_ref)
    moves[2].start()
    weights.wait()
    for j in range(OUT_COLS):
        value = f32_dot(act_ref[...], row_tile(down_ref, DOWN_ROWS, OUT_COLS, j))
        put_part(own_ref, other_ref, slice(j * OUT_TILE, (j + 1) * OUT_TILE), value)
    for move in moves:
        move.wait()


def ff_rest(normed, act, gg, gu, ddown, quads):
    rows = normed.shape[0]
    weights = pltpu.VMEM((IN_ROWS * FF_COLS, BS, LANES), jnp.bfloat16)
    return call(
        ff_rest_kernel,
        [shape((2 * PER_PLANE, BS, LANES), jnp.bfloat16)] + parts(rows),
        [normed, act, gg, gu, ddown[: 3 * PER_PLANE - quad_bounds()[3]], quads],
        [weights] * 3 + [pltpu.VMEM((D, rows), jnp.bfloat16), pltpu.SemaphoreType.DMA((4,))],
        micros=17,
        any_in=(5,),
        any_out=(0,),
    )


def conv_back_kernel(
    branch_ref, mixed_ref, conv_ref, gated_ref, halo_ref, keep_ref, taps_ref, quads_ref,
    dout_ref, gconv_ref, ggate_ref, heads_ref, tap_ref, w_ref, sem,
):
    first = 3 * IN_ROWS * OUT_COLS
    copy = fetch(quads_ref, first, IN_ROWS * OUT_COLS, w_ref, sem)
    copy.start()
    copy.wait()
    rows = mixed_ref.shape[0] // 2
    step = 2 * BS // HALF * 2
    grad = jnp.concatenate(
        [
            nt_dot(branch_ref[...], row_rows(w_ref, g * step, step, OUT_COLS))
            for g in range(IN_ROWS // step)
        ],
        axis=1,
    )
    ggate_ref[...] = (grad * conv_ref[...]).astype(jnp.bfloat16)
    gconv_ref[...] = grad * mixed_ref[:, D_HALF : 2 * D_HALF]
    taps = [jnp.zeros((1, D_HALF), jnp.float32)] * 3
    for s in range(2):
        at = pl.ds(s * rows, rows)
        driven = mixed_ref[at, :D_HALF] * mixed_ref[at, 2 * D_HALF :]
        halo = halo_ref[s]
        grad_conv = gconv_ref[at, :]
        one = keep_ref[at, 0:1] * grad_conv
        two = keep_ref[at, 1:2] * grad_conv
        terms = (two * shift_down(driven, halo, 2), one * shift_down(driven, halo, 1), grad_conv * driven)
        taps = [a + jnp.sum(b, axis=0, keepdims=True) for a, b in zip(taps, terms)]
        heads_ref[s, 0:1] = taps_ref[0:1] * two[0:1]
        heads_ref[s, 1:2] = taps_ref[1:2] * one[0:1] + taps_ref[0:1] * two[1:2]
    tap_ref[...] = jnp.concatenate(taps, axis=0)
    put_row_rows(dout_ref, f32_dot(gated_ref[...].T, branch_ref[...]), 0, IN_ROWS, OUT_COLS)


def conv_back(branch, mixed, conv, gated, halos, keep, taps, quads):
    rows = mixed.shape[0]
    return call(
        conv_back_kernel,
        [
            shape((IN_ROWS * OUT_COLS, BS, LANES), jnp.bfloat16),
            shape((rows, D_HALF), jnp.float32),
            shape((rows, D_HALF), jnp.bfloat16),
            shape((2, 2, D_HALF), jnp.float32),
            shape((3, D_HALF), jnp.float32),
        ],
        [branch, mixed, conv, gated, halos, keep, taps, quads],
        [
            pltpu.VMEM((IN_ROWS * OUT_COLS, BS, LANES), jnp.bfloat16),
            pltpu.SemaphoreType.DMA(()),
        ],
        micros=7,
        any_in=(7,),
    )


def mix_back_kernel(
    gconv_ref, ggate_ref, mixed_ref, normed_ref, tails_ref, keep_ref, taps_ref,
    dout_ref, dgate_ref, ddown_ref,
    grads_ref, grad_ref, din_ref, turned_ref, sems,
):
    behind = 3 * PER_PLANE - quad_bounds()[3]
    moves = []
    at = IN_ROWS * IN_COLS
    pieces = (dout_ref, dgate_ref, ddown_ref.at[pl.ds(behind, PER_PLANE)])
    for n, piece in enumerate(pieces):
        count = piece.shape[0]
        moves.append(pltpu.make_async_copy(piece, grads_ref.at[pl.ds(at, count)], sems.at[n]))
        at += count
    for move in moves:
        move.start()
    turned_ref[...] = normed_ref[...].T
    rows = mixed_ref.shape[0] // 2
    for s in range(2):
        at = pl.ds(s * rows, rows)
        grad_conv = gconv_ref[at, :]
        one = keep_ref[at, 0:1] * grad_conv
        two = keep_ref[at, 1:2] * grad_conv
        grad = (
            taps_ref[2:3] * grad_conv
            + taps_ref[1:2] * shift_up(one, 1)
            + taps_ref[0:1] * shift_up(two, 2)
        )
        row = lax.broadcasted_iota(jnp.int32, grad.shape, 0)
        tail = tails_ref[s]
        grad = grad + jnp.where(
            row == rows - 2, tail[0:1], jnp.where(row == rows - 1, tail[1:2], 0.0)
        )
        grad_ref[at, :D_HALF] = (grad * mixed_ref[at, 2 * D_HALF :]).astype(jnp.bfloat16)
        grad_ref[at, D_HALF : 2 * D_HALF] = ggate_ref[at, :]
        grad_ref[at, 2 * D_HALF :] = (grad * mixed_ref[at, :D_HALF]).astype(jnp.bfloat16)

    def tile(t, carry):
        cols = pl.ds(pl.multiple_of(t * TILE, TILE), TILE)
        put_col_tile(
            din_ref,
            f32_dot(turned_ref[...], grad_ref[:, cols]),
            IN_ROWS,
            IN_COLS,
            QUADS_WIDE * t,
            QUADS_WIDE,
        )
        return carry

    lax.fori_loop(0, IN_COLS // QUADS_WIDE, tile, 0)
    last = pltpu.make_async_copy(
        din_ref, grads_ref.at[pl.ds(0, IN_ROWS * IN_COLS)], sems.at[len(moves)]
    )
    last.start()
    for move in moves:
        move.wait()
    last.wait()


def mix_back(gconv, ggate, mixed, normed, tails, keep, taps, dout, dgate, ddown):
    rows = mixed.shape[0]
    return call(
        mix_back_kernel,
        [
            shape((2 * PER_PLANE, BS, LANES), jnp.bfloat16),
            shape((rows, 3 * D_HALF), jnp.bfloat16),
        ],
        [gconv, ggate, mixed, normed, tails, keep, taps, dout, dgate, ddown],
        [
            pltpu.VMEM((IN_ROWS * IN_COLS, BS, LANES), jnp.bfloat16),
            pltpu.VMEM((D, rows), jnp.bfloat16),
            pltpu.SemaphoreType.DMA((4,)),
        ],
        micros=9,
        any_out=(0,),
    )


def mix_rest_kernel(grad_ref, quads_ref, own_ref, other_ref, w_ref, sem):
    copy = fetch(quads_ref, 0, IN_ROWS * IN_COLS, w_ref, sem)
    copy.start()
    copy.wait()
    for g in range(IN_ROWS // BACK_ROWS):
        value = nt_dot(grad_ref[...], col_rows(w_ref, BACK_ROWS * g, BACK_ROWS, IN_COLS))
        put_part(own_ref, other_ref, slice(g * BACK_ROWS * BS, (g + 1) * BACK_ROWS * BS), value)


def mix_rest(grad, quads):
    rows = grad.shape[0]
    return call(
        mix_rest_kernel,
        parts(rows),
        [grad, quads],
        [
            pltpu.VMEM((IN_ROWS * IN_COLS, BS, LANES), jnp.bfloat16),
            pltpu.SemaphoreType.DMA(()),
        ],
        micros=5,
        any_in=(1,),
    )


def through(pairs, stage_ref, sems):
    ins = [
        pltpu.make_async_copy(src, stage_ref.at[n], sems.at[0, n])
        for n, (src, _) in enumerate(pairs)
    ]
    outs = [
        pltpu.make_async_copy(stage_ref.at[n], dst, sems.at[1, n])
        for n, (_, dst) in enumerate(pairs)
    ]
    for c in ins:
        c.start()
    for c, d in zip(ins, outs):
        c.wait()
        d.start()
    for d in outs:
        d.wait()


def place_kernel(place_ref, *refs):
    out_ref, stage_ref, sems = refs[-3:]
    plane, here, core = place_ref[0], place_ref[1], place_ref[2]
    pairs = []
    for n, src in enumerate(refs[:4]):
        for slot in range(2):
            pairs.append((src.at[slot], out_ref.at[plane, here ^ n, slot ^ core]))
    through(pairs, stage_ref, sems)


def put_plane(plane, here, core, pieces, out):
    hbm = pl.BlockSpec(memory_space=pltpu.HBM)
    near = pieces[0]
    given = list(pieces) + ([] if out is None else [out])
    return pl.pallas_call(
        place_kernel,
        out_shape=jax.ShapeDtypeStruct((Z, PLANE) + near.shape, near.dtype),
        in_specs=[SCALARS] + [hbm] * len(given),
        out_specs=hbm,
        scratch_shapes=[
            pltpu.VMEM((8,) + near.shape[1:], near.dtype),
            pltpu.SemaphoreType.DMA((2, 8)),
        ],
        input_output_aliases={} if out is None else {5: 0},
        compiler_params=pltpu.CompilerParams(vmem_limit_bytes=VMEM_ALL),
        cost_estimate=busy(3),
    )(jnp.stack([plane, here, core]), *given)


def pieces_kernel(place_ref, near_ref, far_ref, zero_ref, two_ref, stage_ref, sems):
    z, here = place_ref[0], place_ref[1]
    count = zero_ref.shape[1]
    places = (
        ((near_ref, 0), (far_ref, PER_PLANE)),
        ((far_ref, 0), (near_ref, 0)),
        ((far_ref, PER_PLANE), (near_ref, PER_PLANE)),
        ((near_ref, PER_PLANE), (far_ref, 0)),
    )
    for plane, sources in enumerate(places):

        @pl.when(z == plane)
        def _(sources=sources):
            pairs = []
            for (src, first), dst in zip(sources, (zero_ref, two_ref)):
                for k in range(PLANE):
                    at = pl.ds(first + (here ^ k) * count, count)
                    pairs.append((src.at[at], dst.at[k]))
            through(pairs, stage_ref, sems)


def take_pieces(z, here, near, far):
    hbm = pl.BlockSpec(memory_space=pltpu.HBM)
    out = jax.ShapeDtypeStruct((PLANE, PER_PLANE // PLANE, BS, LANES), near.dtype)
    return pl.pallas_call(
        pieces_kernel,
        out_shape=(out, out),
        in_specs=[SCALARS, hbm, hbm],
        out_specs=(hbm, hbm),
        scratch_shapes=[
            pltpu.VMEM((2 * PLANE,) + out.shape[1:], near.dtype),
            pltpu.SemaphoreType.DMA((2, 2 * PLANE)),
        ],
        compiler_params=pltpu.CompilerParams(vmem_limit_bytes=VMEM_ALL),
        cost_estimate=busy(5),
    )(jnp.stack([z, here]), near, far)


UP = [(0, 1), (1, 2), (2, 3)]
DOWN = [(1, 0), (2, 1), (3, 2)]
SLOT_PLANES = ((0, 1, 2, 3), (1, 2, 0, 3), (2, 1, 3, 0), (3, 2, 1, 0))
INNER = [(1, 0), (2, 3), (0, 1), (3, 2)]


def reverse(pairs):
    return [(b, a) for a, b in pairs]


def together(*values):
    return lax.optimization_barrier(values)


def over_z(block, pairs):
    return send(block, plane_route(pairs))


def over_x(block):
    return send(block, ACROSS_X)


def over_y(block):
    return send(block, ACROSS_Y)


def gather_weights(own, z, here, core, beside):
    edge = (z == 0) | (z == Z - 1)
    up, down, x0, y0 = together(over_z(own, UP), over_z(own, DOWN), over_x(own), over_y(own))
    one = jnp.where(z < 2, down, up)
    up_two, down_two, x1, y1, beside = together(
        over_z(up, UP[1:]), over_z(down, DOWN[:2]), over_x(one), over_y(one), beside
    )
    two = pick(z, [down_two, up, down, up_two])
    ends, x2, y2, f0, f1 = together(
        over_z(jnp.where(z == 2, up_two, down_two), [UP[2], DOWN[0]]),
        over_x(two),
        over_y(two),
        over_x(y0),
        over_y(x1),
    )
    three = pick(z, [ends, down_two, up_two, ends])

    def put(slot, pieces, out):
        plane = pick(z, [jnp.int32(row[slot]) for row in SLOT_PLANES])
        return put_plane(plane, here, core, pieces, out)

    out = put(1, (one, x1, y1, f1), put(0, (own, x0, y0, f0), None))
    x3, y3, f2, out = together(
        over_x(three), over_y(three), over_z(jnp.where(edge, f0, f1), INNER), out
    )
    out = put(2, (two, x2, y2, f2), out)
    f3 = jnp.stack([over_x(y3[0]), over_y(x3[1])])
    f3, out = together(f3, out)
    out = put(3, (three, x3, y3, f3), out)
    return out.reshape(-1, BS, LANES), beside


def total(*values):
    out = values[0].astype(jnp.float32)
    for value in values[1:]:
        out = out + value.astype(jnp.float32)
    return out


def low_total(*values):
    return total(*values).astype(jnp.bfloat16)


def reduce_grads(near, far, z, here):
    count = PER_PLANE // PLANE
    half = count // 2
    edge = (z == 0) | (z == Z - 1)

    def cut(array, plane_part, k, first=0, size=count):
        start = plane_part * PER_PLANE + (here ^ k) * count + first
        return lax.dynamic_slice_in_dim(array, start, size, axis=0)

    part_three = (z < 2).astype(jnp.int32)
    part_one = z % 2
    got_a = over_x(cut(near, part_three, 3, 0, half))
    got_b = over_y(cut(near, part_three, 3, half, half))
    zero, two = take_pieces(z, here, near, far)
    got_a, got_b, zero, two = together(got_a, got_b, zero, two)
    x3 = jnp.concatenate(
        [cut(near, part_three, 1, 0, half), low_total(cut(near, part_three, 1, half, half), got_b)]
    )
    y3 = jnp.concatenate(
        [low_total(cut(near, part_three, 2, 0, half), got_a), cut(near, part_three, 2, half, half)]
    )
    got_x, got_y, got_z = together(over_x(x3), over_y(y3), over_z(two[3], reverse(INNER)))
    three = low_total(cut(near, part_three, 0), got_x, got_y)
    nothing = jnp.zeros_like(got_z)
    f0 = low_total(zero[3], jnp.where(edge, got_z, nothing))
    f1 = low_total(cut(far, part_one, 3), jnp.where(edge, nothing, got_z))
    got_f0, got_f1, got_x, got_y, got_z = together(
        over_x(f0), over_y(f1), over_x(two[1]), over_y(two[2]), over_z(three, [(3, 2), (0, 1)])
    )
    y0 = low_total(zero[2], got_f0)
    x1 = low_total(cut(far, part_one, 1), got_f1)
    two = low_total(two[0], got_x, got_y)
    three = low_total(three, got_z)
    got_x, got_y, got_up, got_down = together(
        over_x(x1),
        over_y(cut(far, part_one, 2)),
        over_z(jnp.where(z == 3, two, three), reverse(UP[1:])),
        over_z(jnp.where(z == 0, two, three), reverse(DOWN[:2])),
    )
    one = low_total(cut(far, part_one, 0), got_x, got_y, jnp.where(z == 1, got_down, got_up))
    two = low_total(two, jnp.where(z == 1, got_up, got_down))
    got = together(
        over_x(zero[1]),
        over_y(y0),
        over_z(jnp.where(z == 1, two, one), reverse(UP)),
        over_z(jnp.where(z == 2, two, one), reverse(DOWN)),
    )
    return low_total(zero[0], *got)


def phase(value, bits):
    a, b = bits
    got = [send(value, [(i, i ^ bit) for i in range(CHIPS)]) for bit in (a, b, a | b)]
    return got


def close(value, got):
    return (value + got[0]) + (got[1] + got[2])


def spread_sum(value, beside=(None, None)):
    beside = list(beside)
    for n, bits in enumerate(((1, 2), (4, 8))):
        got, beside[n] = together(phase(value, bits), beside[n])
        value = close(value, got)
    return value + to_sibling(value), beside


def shards(
    x_in,
    cotangent,
    seq_lengths,
    weights,
    momentum,
    left_stat,
    right_stat,
    left_root,
    right_root,
    vectors,
    vector_sq,
):
    core = lax.axis_index("wt").astype(jnp.int32)
    place = lax.axis_index("seq").astype(jnp.int32)
    z, here = place // PLANE, place % PLANE
    first_core = core == 0
    rows = x_in.shape[0]
    local_count = weights.shape[0]
    quad_count = local_count // 4
    first_quad = (place * CORES + core) * quad_count

    kept, sent = split_weights(core, first_quad, weights)
    quads, wide = gather_weights(
        jnp.stack([kept, to_sibling(sent)]), z, here, core, widen(momentum, left_root, right_root)
    )

    both_x = jnp.concatenate([x_in, to_sibling(x_in)], axis=0)
    both_cot = jnp.concatenate([cotangent, to_sibling(cotangent)], axis=0)
    starts = jnp.stack([place * CORES + core, place * CORES + 1 - core]) * rows
    places = (starts[:, None] + jnp.arange(rows, dtype=jnp.int32)[None, :]).reshape(-1)
    keep_one, keep_two = keep_masks(places, seq_lengths)
    lane = jnp.arange(LANES)[None, :]
    keep = jnp.where(lane == 0, keep_one, jnp.where(lane == 1, keep_two, 0.0))
    taps = take(vectors[2:].reshape(3, IN_ROWS, 2, HALF), core, 2).reshape(3, D_HALF)

    hidden_both = both_x.astype(jnp.float32)
    scale_both = rms_scale(hidden_both)
    normed = (hidden_both * scale_both * vectors[0]).astype(jnp.bfloat16)
    hidden_in, scale_one = hidden_both[:rows], scale_both[:rows]
    mixed = mix(normed, quads)
    ends = jnp.stack([mixed[rows - 2 : rows], mixed[-2:]])
    ends = ends[:, :, :D_HALF] * ends[:, :, 2 * D_HALF :]
    carried = send(jnp.where(first_core, ends[1], ends[0]), [(i, i + 1) for i in range(CHIPS - 1)])
    halos = jnp.stack(
        [jnp.where(first_core, carried, ends[1]), jnp.where(first_core, ends[0], carried)]
    )
    conv_out, gated_out, part, other = conv_forward(mixed, halos, keep, taps, quads)
    middle = hidden_in + part + to_sibling(other)
    scale_two = rms_scale(middle)
    own_two = (middle * scale_two * vectors[1]).astype(jnp.bfloat16)
    normed_two = jnp.concatenate([own_two, to_sibling(own_two)], axis=0)
    activated, grad_gate, grad_up = ff_pass(normed_two, both_cot, quads)
    part, other = ff_back(grad_gate, grad_up, quads)
    grad_w_down, grad_w_gate = down_grad(normed_two, activated, grad_gate, both_cot)
    grad_normed_two = part + to_sibling(other)
    gain_two_grad, middle_term = norm_back(middle, scale_two, vectors[1], grad_normed_two)
    grad_middle = cotangent.astype(jnp.float32) + middle_term
    own_branch = grad_middle.astype(jnp.bfloat16)
    grad_branch = jnp.concatenate([own_branch, to_sibling(own_branch)], axis=0)
    grad_w_out, grad_conv, grad_output, heads, tap_grads = conv_back(
        grad_branch, mixed, conv_out, gated_out, halos, keep, taps, quads
    )
    from_after = send(
        jnp.where(first_core, heads[0], heads[1]), [(i + 1, i) for i in range(CHIPS - 1)]
    )
    tails = jnp.stack(
        [jnp.where(first_core, heads[1], from_after), jnp.where(first_core, from_after, heads[0])]
    )
    near_grads, grad_mixed = mix_back(
        grad_conv, grad_output, mixed, normed, tails, keep, taps, grad_w_out, grad_w_gate, grad_w_down
    )
    near_grads, grad_w_down = together(near_grads, grad_w_down)
    far_grads, part, other = ff_rest(
        normed_two, activated, grad_gate, grad_up, grad_w_down, quads
    )
    out_act = (middle + part + to_sibling(other)).astype(jnp.bfloat16)
    part, other = mix_rest(grad_mixed, quads)
    grad_normed = part + to_sibling(other)
    gain_one_grad, input_term = norm_back(hidden_in, scale_one, vectors[0], grad_normed)
    in_grad = grad_middle + input_term

    summed = reduce_grads(near_grads, far_grads, z, here).reshape(2, quad_count, BS, LANES)
    kept = take(summed, core, 0)
    got = to_sibling(take(summed, 1 - core, 0))

    tap_part = jnp.where(
        jnp.arange(2).reshape(1, 1, 2, 1) == core, tap_grads.reshape(3, IN_ROWS, 1, HALF), 0.0
    ).reshape(3, D)
    vector_grads, _ = spread_sum(
        jnp.concatenate([gain_one_grad[None], gain_two_grad[None], tap_part], axis=0)
    )
    new_vector_sq = DECAY * vector_sq + (1.0 - DECAY) * vector_grads * vector_grads
    new_vectors = vectors - VEC_RATE * vector_grads * lax.rsqrt(new_vector_sq)

    new_momentum, precond, sums, kind_part = step_blocks(
        core, first_quad, kept, got, *wide, momentum
    )
    kind_sum, (new_left, new_right) = spread_sum(
        kind_part, (stat_blocks(sums, left_stat, False), stat_blocks(sums, right_stat, True))
    )
    kind_sum = jnp.sum(kind_sum, axis=1)[:KINDS]
    in_end, out_end, gate_end, up_end = block_bounds()
    kind_total = jnp.array(
        [in_end, out_end - in_end, gate_end - out_end, up_end - gate_end, BLOCKS - up_end],
        jnp.float32,
    ) * (BS * BS)
    kind_scale = lax.rsqrt(kind_sum / kind_total + MEAN_EPS)
    block_kinds = kind_of(first_quad + jnp.arange(local_count, dtype=jnp.int32) // 4)
    one_hot = (block_kinds[:, None] == jnp.arange(KINDS)[None, :]).astype(jnp.float32)
    block_scale = jnp.sum(one_hot * kind_scale[None, :], axis=1)
    new_weights = weights - RATE * block_scale[:, None] * precond
    return (
        out_act,
        in_grad,
        new_weights,
        new_weights.astype(jnp.bfloat16),
        new_momentum,
        new_left,
        new_right,
        vector_grads,
        new_vector_sq,
        new_vectors,
    )


def solution(mesh):
    body = shards if (mesh.shape["seq"], mesh.shape["wt"]) == (CHIPS, CORES) else shards_any
    return jax.shard_map(
        body,
        mesh=mesh,
        in_specs=(
            P(("seq", "wt"), None),
            P(("seq", "wt"), None),
            P(),
            P(("seq", "wt"), None),
            P(("seq", "wt"), None),
            P(("seq", "wt"), None),
            P(("seq", "wt"), None),
            P(("seq", "wt"), None),
            P(("seq", "wt"), None),
            P(),
            P(),
        ),
        out_specs=(
            P(("seq", "wt"), None),
            P(("seq", "wt"), None),
            P(("seq", "wt"), None),
            P(("seq", "wt"), None),
            P(("seq", "wt"), None),
            P(("seq", "wt"), None),
            P(("seq", "wt"), None),
            P(),
            P(),
            P(),
        ),
        check_vma=False,
    )
```

```python
import functools

import jax
import jax.numpy as jnp
from jax import lax
from jax.experimental import pallas as pl
from jax.experimental.pallas import tpu as pltpu
from jax.sharding import PartitionSpec as P

D = 1024
FF = 4608
BS = 64
BLOCKS = 4480


NORM_EPS = 1e-05
MEAN_EPS = 1e-06
DECAY = 0.5
MOMENT = 0.9
RATE = 0.01
VEC_RATE = 0.25
HIGHEST = lax.Precision.HIGHEST


def from_behind(block, axis, distance):
    devices = range(lax.axis_size(axis))
    route = [(i - distance, i) for i in devices if i - distance in devices]
    return lax.ppermute(block, axis, route)


def unpack_blocks(blocks, row_count, col_count):
    return (
        blocks.reshape(row_count // BS, col_count // BS, BS, BS)
        .transpose(0, 2, 1, 3)
        .reshape(row_count, col_count)
    )


def pack_blocks(matrix):
    row_count, col_count = matrix.shape
    return (
        matrix.reshape(row_count // BS, BS, col_count // BS, BS)
        .transpose(0, 2, 1, 3)
        .reshape(-1, BS * BS)
    )


def block_bounds():
    per_block = BS * BS
    in_end = 3 * D * D // per_block
    out_end = in_end + D * D // per_block
    gate_end = out_end + D * FF // per_block
    up_end = gate_end + D * FF // per_block
    return (in_end, out_end, gate_end, up_end)


def matrices(blocks):
    in_end, out_end, gate_end, up_end = block_bounds()
    w_in = unpack_blocks(blocks[:in_end], D, 3 * D)
    w_out = unpack_blocks(blocks[in_end:out_end], D, D)
    w_gate = unpack_blocks(blocks[out_end:gate_end], D, FF)
    w_up = unpack_blocks(blocks[gate_end:up_end], D, FF)
    w_down = unpack_blocks(blocks[up_end:], FF, D)
    return (w_in, w_out, w_gate, w_up, w_down)


def matmul(left_side, right_side):
    return jnp.dot(left_side, right_side, preferred_element_type=jnp.float32)


def matmul_tn(left_side, right_side):
    return lax.dot_general(
        left_side, right_side, (((0,), (0,)), ((), ())), preferred_element_type=jnp.float32
    )


def matmul_nt(left_side, right_side):
    return lax.dot_general(
        left_side, right_side, (((1,), (1,)), ((), ())), preferred_element_type=jnp.float32
    )


def rms_scale(values):
    return lax.rsqrt(jnp.mean(values * values, axis=-1, keepdims=True) + NORM_EPS)


def norm_back(values, row_scale, norm_gain, grad_normed):
    gain_grad = jnp.sum(grad_normed * values * row_scale, axis=0)
    weighted = grad_normed * norm_gain
    grad_values = row_scale * weighted - values * row_scale**3 * jnp.mean(
        weighted * values, axis=-1, keepdims=True
    )
    return (gain_grad, grad_values)


def keep_masks(places, seq_lengths):
    ends = jnp.cumsum(seq_lengths)
    starts = jnp.max(jnp.where(ends[None, :] <= places[:, None], ends[None, :], 0), axis=1)
    keep_one = (places - 1 >= starts).astype(jnp.float32)[:, None]
    keep_two = (places - 2 >= starts).astype(jnp.float32)[:, None]
    return (keep_one, keep_two)


def weight_grads(operands):
    (
        normed,
        grad_mixed,
        gated_out,
        grad_branch,
        normed_two,
        grad_gate,
        grad_up,
        activated,
        cotangent,
    ) = operands
    return jnp.concatenate(
        [
            pack_blocks(matmul_tn(normed, grad_mixed)),
            pack_blocks(matmul_tn(gated_out, grad_branch)),
            pack_blocks(matmul_tn(normed_two, grad_gate)),
            pack_blocks(matmul_tn(normed_two, grad_up)),
            pack_blocks(matmul_tn(activated, cotangent)),
        ],
        axis=0,
    )


def shards_any(
    x_in,
    cotangent,
    seq_lengths,
    weights,
    momentum,
    left_stat,
    right_stat,
    left_root,
    right_root,
    vectors,
    vector_sq,
):
    gathered = lax.all_gather(weights.astype(jnp.bfloat16), ("seq", "wt"), axis=0, tiled=True)
    w_in, w_out, w_gate, w_up, w_down = matrices(gathered)
    row_count = x_in.shape[0]
    places = lax.axis_index(("seq", "wt")) * row_count + jnp.arange(row_count, dtype=jnp.int32)
    keep_one, keep_two = keep_masks(places, seq_lengths)
    hidden_in = x_in.astype(jnp.float32)
    scale_one = rms_scale(hidden_in)
    normed = (hidden_in * scale_one * vectors[0]).astype(jnp.bfloat16)
    mixed = matmul(normed, w_in)
    input_gate = mixed[:, :D]
    output_gate = mixed[:, D : 2 * D]
    values = mixed[:, 2 * D :]
    driven = input_gate * values
    carried = from_behind(driven[-2:], ("seq", "wt"), 1)
    extended = jnp.concatenate([carried, driven], axis=0)
    conv_out = (
        vectors[4] * driven
        + vectors[3] * keep_one * extended[1:-1]
        + vectors[2] * keep_two * extended[:-2]
    )
    gated_out = (output_gate * conv_out).astype(jnp.bfloat16)
    middle = hidden_in + matmul(gated_out, w_out)
    scale_two = rms_scale(middle)
    normed_two = (middle * scale_two * vectors[1]).astype(jnp.bfloat16)
    gate_ff = matmul(normed_two, w_gate)
    up_ff = matmul(normed_two, w_up)
    sigmoid_gate = jax.nn.sigmoid(gate_ff)
    silu_value = gate_ff * sigmoid_gate
    activated = (silu_value * up_ff).astype(jnp.bfloat16)
    out_act = (middle + matmul(activated, w_down)).astype(jnp.bfloat16)
    grad_act = matmul_nt(cotangent, w_down)
    grad_gate = (grad_act * up_ff * sigmoid_gate * (1.0 + gate_ff * (1.0 - sigmoid_gate))).astype(
        jnp.bfloat16
    )
    grad_up = (grad_act * silu_value).astype(jnp.bfloat16)
    grad_normed_two = matmul_nt(grad_gate, w_gate) + matmul_nt(grad_up, w_up)
    gain_two_grad, middle_term = norm_back(middle, scale_two, vectors[1], grad_normed_two)
    grad_middle = cotangent.astype(jnp.float32) + middle_term
    grad_branch = grad_middle.astype(jnp.bfloat16)
    grad_gated = matmul_nt(grad_branch, w_out)
    grad_output_gate = grad_gated * conv_out
    grad_conv = grad_gated * output_gate
    early_one = keep_one * grad_conv
    early_two = keep_two * grad_conv
    tap_zero = jnp.sum(early_two * extended[:-2], axis=0)
    tap_first = jnp.sum(early_one * extended[1:-1], axis=0)
    tap_second = jnp.sum(grad_conv * driven, axis=0)
    sent_back = jnp.stack(
        [vectors[2] * early_two[0], vectors[3] * early_one[0] + vectors[2] * early_two[1]], axis=0
    )
    from_after = from_behind(sent_back, ("seq", "wt"), -1)
    zero_rows = jnp.zeros((2, D), jnp.float32)
    grad_driven = vectors[4] * grad_conv
    grad_driven = grad_driven + vectors[3] * jnp.concatenate([early_one[1:], zero_rows[:1]], axis=0)
    grad_driven = grad_driven + vectors[2] * jnp.concatenate([early_two[2:], zero_rows], axis=0)
    grad_driven = grad_driven + jnp.concatenate(
        [jnp.zeros((row_count - 2, D), jnp.float32), from_after], axis=0
    )
    grad_mixed = jnp.concatenate(
        [grad_driven * values, grad_output_gate, grad_driven * input_gate], axis=1
    ).astype(jnp.bfloat16)
    grad_normed = matmul_nt(grad_mixed, w_in)
    gain_one_grad, input_term = norm_back(hidden_in, scale_one, vectors[0], grad_normed)
    in_grad = grad_middle + input_term
    paired = (
        lax.all_gather(normed, "wt", axis=0, tiled=True),
        lax.all_gather(grad_mixed, "wt", axis=0, tiled=True),
        lax.all_gather(gated_out, "wt", axis=0, tiled=True),
        lax.all_gather(grad_branch, "wt", axis=0, tiled=True),
        lax.all_gather(normed_two, "wt", axis=0, tiled=True),
        lax.all_gather(grad_gate, "wt", axis=0, tiled=True),
        lax.all_gather(grad_up, "wt", axis=0, tiled=True),
        lax.all_gather(activated, "wt", axis=0, tiled=True),
        lax.all_gather(cotangent, "wt", axis=0, tiled=True),
    )
    pair_grads = weight_grads(paired)
    seq_count = lax.axis_size("seq")
    core_count = lax.axis_size("wt")
    owned_count = pair_grads.shape[0] // (seq_count * core_count)
    arranged = pair_grads.reshape(seq_count, core_count, owned_count, BS * BS)
    mine = lax.dynamic_index_in_dim(arranged, lax.axis_index("wt"), 1, keepdims=False).reshape(
        seq_count * owned_count, BS * BS
    )
    summed_flat = lax.psum_scatter(mine, "seq", scatter_dimension=0, tiled=True)
    vector_part = jnp.stack([gain_one_grad, gain_two_grad, tap_zero, tap_first, tap_second], axis=0)
    local_count = summed_flat.shape[0]
    summed = summed_flat.reshape(local_count, BS, BS)
    left_blocks = left_stat.reshape(local_count, BS, BS)
    right_blocks = right_stat.reshape(local_count, BS, BS)
    momentum_blocks = momentum.reshape(local_count, BS, BS)
    left_factor = left_root.reshape(local_count, BS, BS)
    right_factor = right_root.reshape(local_count, BS, BS)
    new_left = DECAY * left_blocks + (1.0 - DECAY) * jnp.einsum(
        "kij,klj->kil", summed, summed, precision=HIGHEST
    )
    new_right = DECAY * right_blocks + (1.0 - DECAY) * jnp.einsum(
        "kji,kjl->kil", summed, summed, precision=HIGHEST
    )
    new_momentum = MOMENT * momentum_blocks + summed
    precond = jnp.einsum("kij,kjl->kil", left_factor, new_momentum, precision=HIGHEST)
    precond = jnp.einsum("kij,kjl->kil", precond, right_factor, precision=HIGHEST)
    precond_flat = precond.reshape(local_count, BS * BS)
    square = jnp.sum(precond_flat * precond_flat, axis=1)
    in_end, out_end, gate_end, up_end = block_bounds()
    block_ids = lax.axis_index(("seq", "wt")) * local_count + jnp.arange(
        local_count, dtype=jnp.int32
    )
    kind_index = (
        (block_ids >= in_end).astype(jnp.int32)
        + (block_ids >= out_end).astype(jnp.int32)
        + (block_ids >= gate_end).astype(jnp.int32)
        + (block_ids >= up_end).astype(jnp.int32)
    )
    one_hot = (kind_index[:, None] == jnp.arange(5, dtype=jnp.int32)[None, :]).astype(jnp.float32)
    kind_part = jnp.sum(one_hot * square[:, None], axis=0)
    vector_grads, kind_sum = lax.psum((vector_part, kind_part), ("seq", "wt"))
    kind_total = jnp.array(
        [in_end, out_end - in_end, gate_end - out_end, up_end - gate_end, BLOCKS - up_end],
        jnp.float32,
    ) * (BS * BS)
    kind_scale = lax.rsqrt(kind_sum / kind_total + MEAN_EPS)
    block_scale = jnp.sum(one_hot * kind_scale[None, :], axis=1)
    new_weights = weights - RATE * block_scale[:, None] * precond_flat
    weight_copy = new_weights.astype(jnp.bfloat16)
    new_vector_sq = DECAY * vector_sq + (1.0 - DECAY) * vector_grads * vector_grads
    new_vectors = vectors - VEC_RATE * vector_grads * lax.rsqrt(new_vector_sq)
    flat_shape = (local_count, BS * BS)
    return (
        out_act,
        in_grad,
        new_weights,
        weight_copy,
        new_momentum.reshape(flat_shape),
        new_left.reshape(flat_shape),
        new_right.reshape(flat_shape),
        vector_grads,
        new_vector_sq,
        new_vectors,
    )


Z, Y, X = 4, 2, 2
CHIPS, CORES = Z * Y * X, 2
PLANE = Y * X
HALF = BS // 2
SWAP = [(0, 1), (1, 0)]


def chip(z, y, x):
    return (z * Y + y) * X + x


def plane_route(pairs):
    return [(chip(a, y, x), chip(b, y, x)) for a, b in pairs for y in range(Y) for x in range(X)]


ACROSS_X = [(i, i ^ 1) for i in range(CHIPS)]
ACROSS_Y = [(i, i ^ 2) for i in range(CHIPS)]


def send(block, route):
    return lax.ppermute(block, "seq", route)


def to_sibling(block):
    return lax.ppermute(block, "wt", SWAP)


def quad_bounds():
    return tuple(b // 4 for b in block_bounds())


def pick(place, options):
    out = options[0]
    for i, option in enumerate(options[1:], 1):
        out = jnp.where(place == i, option, out)
    return out


def take(array, index, axis):
    return lax.dynamic_index_in_dim(array, index, axis, keepdims=False)


QUAD = 4 * BS
LANES = 128
KINDS = 5
VMEM_LIMIT = 24 * 1024 * 1024
VMEM_MOST = 50 * 1024 * 1024
VMEM_ALL = 62 * 1024 * 1024


def busy(micros):
    return pl.CostEstimate(flops=0, bytes_accessed=int(micros * 3e6), transcendentals=0)


def lane_ids(rows):
    return lax.broadcasted_iota(jnp.int32, (rows, LANES), 1)


def strided(ref, part, start, count, stride):
    return ref[part, pl.ds(start, count, stride=stride), :]


def columns(flat_ref, cols_ref):
    for k in range(cols_ref.shape[0]):
        cols_ref[k] = flat_ref[:, pl.ds(k * LANES, LANES)]


def cols_to_wide(cols_ref, wide_ref, count):
    low = lane_ids(count) < BS
    for k in range(BS // 2):
        parts = [strided(cols_ref, k, b, count, 4) for b in range(4)]
        turned = [pltpu.roll(p, BS, 1) for p in parts]
        for t in range(2):
            a, b = 2 * t, 2 * t + 1
            even = jnp.where(low, parts[a], turned[b])
            odd = jnp.where(low, turned[a], parts[b])
            wide_ref[t, pl.ds(2 * k, count, stride=BS), :] = even
            wide_ref[t, pl.ds(2 * k + 1, count, stride=BS), :] = odd


def wide_to_cols(wide_ref, cols_ref, count):
    low = lane_ids(count) < BS
    for k in range(BS // 2):
        for t in range(2):
            even = strided(wide_ref, t, 2 * k, count, BS)
            odd = strided(wide_ref, t, 2 * k + 1, count, BS)
            a, b = 2 * t, 2 * t + 1
            cols_ref[k, pl.ds(a, count, stride=4), :] = jnp.where(
                low, even, pltpu.roll(odd, BS, 1)
            )
            cols_ref[k, pl.ds(b, count, stride=4), :] = jnp.where(
                low, pltpu.roll(even, BS, 1), odd
            )


def join(wide_ref, rows):
    return jnp.concatenate([wide_ref[0, rows, :], wide_ref[1, rows, :]], axis=1)


def cut(wide_ref, rows, value):
    wide_ref[0, rows, :] = value[:, :LANES].astype(wide_ref.dtype)
    wide_ref[1, rows, :] = value[:, LANES:].astype(wide_ref.dtype)


def cols_shape(flat):
    return (flat.shape[1] // LANES, flat.shape[0], LANES)


def kind_of(quad):
    kind = jnp.int32(0)
    for bound in quad_bounds():
        kind = kind + (quad >= bound).astype(jnp.int32)
    return kind


def is_row_kind(kind):
    return (kind == 1) | (kind == 4)


def split_weights_kernel(place_ref, flat_ref, kept_ref, sent_ref, cols_ref, col_ref, row_ref):
    count = flat_ref.shape[0] // 4
    core, first = place_ref[0], place_ref[1]
    group = lane_ids(count) // HALF
    low = group < 2
    columns(flat_ref, cols_ref)
    for k in range(BS // 2):
        parts = [strided(cols_ref, k, b, count, 4) for b in range(4)]
        rolls = [[p] + [pltpu.roll(p, s * HALF, 1) for s in (1, 2, 3)] for p in parts]
        for odd in range(2):
            r = 2 * k + odd
            for half in range(2):
                g = 2 * odd + half
                out = rolls[0][(0 - g) % 4]
                for b in range(1, 4):
                    out = jnp.where(group == b, rolls[b][(b - g) % 4], out)
                col_ref[half, pl.ds(r, count, stride=BS), :] = out
            for t in range(2):
                a, b = 2 * t, 2 * t + 1
                if odd:
                    out = jnp.where(low, rolls[a][2], parts[b])
                else:
                    out = jnp.where(low, parts[a], rolls[b][2])
                row_ref[r // HALF, pl.ds(t * HALF + r % HALF, count, stride=BS), :] = out

    def finish(q, carry):
        rows = pl.ds(pl.multiple_of(q * BS, BS), BS)
        by_row = is_row_kind(kind_of(first + q))
        for ref, half in ((kept_ref, core), (sent_ref, 1 - core)):
            value = jnp.where(by_row, row_ref[half, rows, :], col_ref[half, rows, :])
            ref[q] = value.astype(ref.dtype)
        return carry

    lax.fori_loop(0, count, finish, 0)


def whole(n):
    return [pl.BlockSpec(memory_space=pltpu.VMEM)] * n


SCALARS = pl.BlockSpec(memory_space=pltpu.SMEM)


def split_weights(core, first, weights):
    count = weights.shape[0] // 4
    quads = jax.ShapeDtypeStruct((count, BS, LANES), jnp.bfloat16)
    return pl.pallas_call(
        split_weights_kernel,
        out_shape=(quads, quads),
        in_specs=[SCALARS] + whole(1),
        out_specs=tuple(whole(2)),
        scratch_shapes=[pltpu.VMEM(cols_shape(weights), jnp.float32)]
        + [pltpu.VMEM((2, count * BS, LANES), jnp.float32)] * 2,
        compiler_params=pltpu.CompilerParams(vmem_limit_bytes=VMEM_LIMIT),
        cost_estimate=busy(8),
    )(jnp.stack([core, first]), weights)


def widen_kernel(momentum_ref, left_ref, right_ref, mom_ref, lw_ref, rw_ref, cols_ref, wide_ref):
    count = momentum_ref.shape[0] // 4
    sources = ((momentum_ref, mom_ref, MOMENT), (left_ref, lw_ref, 1.0), (right_ref, rw_ref, 1.0))
    for src, dst, scale in sources:
        columns(src, cols_ref)
        cols_to_wide(cols_ref, wide_ref, count)
        dst[...] = (scale * wide_ref[...]).astype(dst.dtype)


def widen(momentum, left_root, right_root):
    shape = (2, momentum.shape[0] // 4 * BS, LANES)
    return pl.pallas_call(
        widen_kernel,
        out_shape=(
            jax.ShapeDtypeStruct(shape, jnp.bfloat16),
            jax.ShapeDtypeStruct(shape, jnp.bfloat16),
            jax.ShapeDtypeStruct(shape, jnp.bfloat16),
        ),
        in_specs=whole(3),
        out_specs=tuple(whole(3)),
        scratch_shapes=[
            pltpu.VMEM(cols_shape(momentum), jnp.float32),
            pltpu.VMEM(shape, jnp.float32),
        ],
        compiler_params=pltpu.CompilerParams(vmem_limit_bytes=VMEM_LIMIT),
        cost_estimate=busy(11),
    )(momentum, left_root, right_root)


def diagonal(wide, mask):
    return jnp.where(mask, jnp.concatenate([wide] * 4, axis=0), jnp.zeros((), wide.dtype))


def diagonal_mask():
    rows = lax.broadcasted_iota(jnp.int32, (QUAD, QUAD), 0) // BS
    cols = lax.broadcasted_iota(jnp.int32, (QUAD, QUAD), 1) // BS
    return rows == cols


def wide_sum(kept, got, core, by_row):
    first = jnp.where(core == 0, kept, got)
    second = jnp.where(core == 0, got, kept)
    group = lane_ids(BS) // HALF
    tiles = []
    for t in range(2):
        pieces = (
            (first, 2 * t, 0),
            (second, 2 * t, 1),
            (first, 2 * t + 1, 2),
            (second, 2 * t + 1, 3),
        )
        out = None
        for value, source, target in pieces:
            shift = (target - source) * HALF % LANES
            moved = value if shift == 0 else pltpu.roll(value, shift, 1)
            out = moved if out is None else jnp.where(group == target, moved, out)
        rows = slice(t * HALF, (t + 1) * HALF)
        tiles.append(
            jnp.where(by_row, jnp.concatenate([first[rows], second[rows]], axis=0), out)
        )
    return jnp.concatenate(tiles, axis=1)


def step_kernel(
    place_ref, kept_ref, got_ref, mom_ref, lw_ref, rw_ref, flat_ref,
    new_mom_ref, precond_ref, wide_ref, kind_ref, cols_ref, sum_ref, step_ref,
):
    count = kept_ref.shape[0]
    core, first = place_ref[0], place_ref[1]
    mask = diagonal_mask()
    kind_ref[...] = jnp.zeros_like(kind_ref)

    def one(q, carry):
        rows = pl.ds(pl.multiple_of(q * BS, BS), BS)
        kind = kind_of(first + q)
        total = wide_sum(
            kept_ref[q].astype(jnp.float32), got_ref[q].astype(jnp.float32), core, is_row_kind(kind)
        )
        cut(sum_ref, rows, total)
        wide_ref[rows, :] = total.astype(jnp.bfloat16)
        moment = (join(mom_ref, rows).astype(jnp.float32) + total).astype(jnp.bfloat16)
        inner = jnp.dot(
            join(lw_ref, rows), diagonal(moment, mask), preferred_element_type=jnp.float32
        ).astype(jnp.bfloat16)
        step = jnp.dot(
            inner, diagonal(join(rw_ref, rows), mask), preferred_element_type=jnp.float32
        )
        cut(step_ref, rows, step)
        square = jnp.sum(step * step, axis=0, keepdims=True)
        kind_ref[pl.ds(kind, 1), :] += square[:, :LANES] + square[:, LANES:]
        return carry

    lax.fori_loop(0, count, one, 0, unroll=5)

    wide_to_cols(sum_ref, cols_ref, count)
    for k in range(cols_ref.shape[0]):
        lanes = pl.ds(k * LANES, LANES)
        new_mom_ref[:, lanes] = MOMENT * flat_ref[:, lanes] + cols_ref[k]
    wide_to_cols(step_ref, cols_ref, count)
    for k in range(cols_ref.shape[0]):
        precond_ref[:, pl.ds(k * LANES, LANES)] = cols_ref[k]


def step_blocks(core, first, kept, got, mom_wide, left_wide, right_wide, momentum):
    count = kept.shape[0]
    rows = count * BS
    flat = jax.ShapeDtypeStruct(momentum.shape, jnp.float32)
    return pl.pallas_call(
        step_kernel,
        out_shape=(
            flat,
            flat,
            jax.ShapeDtypeStruct((rows, QUAD), jnp.bfloat16),
            jax.ShapeDtypeStruct((8, LANES), jnp.float32),
        ),
        in_specs=[SCALARS] + whole(6),
        out_specs=tuple(whole(4)),
        scratch_shapes=[pltpu.VMEM(cols_shape(momentum), jnp.float32)]
        + [pltpu.VMEM((2, rows, LANES), jnp.float32)] * 2,
        compiler_params=pltpu.CompilerParams(vmem_limit_bytes=VMEM_LIMIT),
        cost_estimate=busy(13),
    )(jnp.stack([core, first]), kept, got, mom_wide, left_wide, right_wide, momentum)


def stat_kernel(turned, wide_ref, old_ref, new_ref, cols_ref, gram_ref):
    count = wide_ref.shape[0] // BS
    mask = diagonal_mask()

    def one(q, carry):
        rows = pl.ds(pl.multiple_of(q * BS, BS), BS)
        total = wide_ref[rows, :]
        if turned:
            gram = lax.dot_general(
                total, total, (((0,), (0,)), ((), ())), preferred_element_type=jnp.float32
            )
            gram = jnp.where(mask, gram, 0.0)
            gram = gram[:BS] + gram[BS : 2 * BS] + gram[2 * BS : 3 * BS] + gram[3 * BS :]
        else:
            gram = lax.dot_general(
                total, diagonal(total, mask), (((1,), (1,)), ((), ())),
                preferred_element_type=jnp.float32,
            )
        cut(gram_ref, rows, gram)
        return carry

    lax.fori_loop(0, count, one, 0, unroll=5)
    wide_to_cols(gram_ref, cols_ref, count)
    for k in range(cols_ref.shape[0]):
        lanes = pl.ds(k * LANES, LANES)
        new_ref[:, lanes] = DECAY * old_ref[:, lanes] + (1.0 - DECAY) * cols_ref[k]


def stat_blocks(wide, stat, turned):
    return pl.pallas_call(
        functools.partial(stat_kernel, turned),
        out_shape=jax.ShapeDtypeStruct(stat.shape, jnp.float32),
        in_specs=whole(2),
        out_specs=whole(1)[0],
        scratch_shapes=[
            pltpu.VMEM(cols_shape(stat), jnp.float32),
            pltpu.VMEM((2, wide.shape[0], LANES), jnp.float32),
        ],
        compiler_params=pltpu.CompilerParams(vmem_limit_bytes=VMEM_LIMIT),
        cost_estimate=busy(6),
    )(wide, stat)


TILE = 768
QUADS_WIDE = TILE // LANES
OUT_TILE = 256


def f32_dot(a, b, dims=((1,), (0,))):
    return lax.dot_general(a, b, (dims, ((), ())), preferred_element_type=jnp.float32)


def nt_dot(a, b):
    return f32_dot(a, b, ((1,), (1,)))


def col_tile(ref, rows, per_row, j, width=2):
    parts = [
        jnp.concatenate([ref[i * per_row + j + d] for i in range(rows)], axis=0)
        for d in range(width)
    ]
    return jnp.concatenate(parts, axis=1)


def col_rows(ref, first, rows, per_row):
    return jnp.concatenate(
        [
            jnp.concatenate([ref[(first + i) * per_row + j] for j in range(per_row)], axis=1)
            for i in range(rows)
        ],
        axis=0,
    )


def row_rows(ref, first, rows, per_row):
    return jnp.concatenate(
        [
            jnp.concatenate(
                [
                    ref[(first + i) * per_row + j, h * HALF : (h + 1) * HALF]
                    for j in range(per_row)
                    for h in range(2)
                ],
                axis=1,
            )
            for i in range(rows)
        ],
        axis=0,
    )


def row_tile(ref, rows, per_row, j):
    parts = [
        jnp.concatenate(
            [ref[i * per_row + j, h * HALF : (h + 1) * HALF] for i in range(rows)], axis=0
        )
        for h in range(2)
    ]
    return jnp.concatenate(parts, axis=1)


def put_col_tile(ref, value, rows, per_row, j, width=2):
    value = value.astype(ref.dtype)
    for i in range(rows):
        for d in range(width):
            ref[i * per_row + j + d] = value[i * BS : (i + 1) * BS, d * LANES : (d + 1) * LANES]


def put_row_rows(ref, value, first, rows, per_row):
    value = value.astype(ref.dtype)
    for i in range(rows):
        for j in range(per_row):
            for h in range(2):
                part = value[
                    i * HALF : (i + 1) * HALF, (2 * j + h) * LANES : (2 * j + h + 1) * LANES
                ]
                ref[(first + i) * per_row + j, h * HALF : (h + 1) * HALF] = part


def put_part(own_ref, other_ref, cols, value):
    rows = own_ref.shape[0]
    own_ref[:, cols] = value[:rows]
    other_ref[:, cols] = value[rows:]


def parts(rows):
    return [shape((rows // 2, D), jnp.float32)] * 2


def call(kernel, outs, ins, scratch=(), micros=0, any_in=(), any_out=(), limit=VMEM_MOST, aliases=None):
    def specs(count, far):
        return [
            pl.BlockSpec(memory_space=pltpu.HBM if i in far else pltpu.VMEM) for i in range(count)
        ]

    return pl.pallas_call(
        kernel,
        out_shape=tuple(jax.ShapeDtypeStruct(o.shape, o.dtype) for o in outs),
        in_specs=specs(len(ins), any_in),
        out_specs=tuple(specs(len(outs), any_out)),
        scratch_shapes=list(scratch),
        input_output_aliases=aliases or {},
        compiler_params=pltpu.CompilerParams(vmem_limit_bytes=limit),
        cost_estimate=busy(micros),
    )(*ins)


def shape(dims, dtype):
    return jax.ShapeDtypeStruct(dims, dtype)


IN_ROWS = D // BS
IN_COLS = 3 * D // 256
OUT_COLS = D // 256
FF_COLS = FF // 256
DOWN_ROWS = FF // BS
FF_HALF = FF // 2
D_HALF = D // 2


def fetch(quads_ref, first, count, into, sem):
    return pltpu.make_async_copy(quads_ref.at[pl.ds(first, count)], into, sem)


def mix_kernel(normed_ref, quads_ref, mixed_ref, w_ref, sems):
    step = 4 * IN_COLS
    copies = [
        fetch(quads_ref, g * step, step, w_ref.at[pl.ds(g * step, step)], sems.at[g])
        for g in range(IN_ROWS // 4)
    ]
    for c in copies:
        c.start()
    for c in copies:
        c.wait()

    def tile(t, carry):
        cols = pl.ds(pl.multiple_of(t * TILE, TILE), TILE)
        mixed_ref[:, cols] = f32_dot(
            normed_ref[...], col_tile(w_ref, IN_ROWS, IN_COLS, QUADS_WIDE * t, QUADS_WIDE)
        )
        return carry

    lax.fori_loop(0, IN_COLS // QUADS_WIDE, tile, 0)


def mix(normed, quads):
    rows = normed.shape[0]
    return call(
        mix_kernel,
        [shape((rows, 3 * D_HALF), jnp.float32)],
        [normed, quads],
        [
            pltpu.VMEM((IN_ROWS * IN_COLS, BS, LANES), jnp.bfloat16),
            pltpu.SemaphoreType.DMA((IN_ROWS // 4,)),
        ],
        micros=7,
        any_in=(1,),
    )[0]


def shift_down(value, halo, distance):
    moved = pltpu.roll(value, distance, 0)
    row = lax.broadcasted_iota(jnp.int32, value.shape, 0)
    out = jnp.where(row == 0, halo[2 - distance : 3 - distance], moved)
    if distance == 2:
        out = jnp.where(row == 1, halo[1:2], out)
    return out


def shift_up(value, distance):
    count = value.shape[0]
    moved = pltpu.roll(value, count - distance, 0)
    row = lax.broadcasted_iota(jnp.int32, value.shape, 0)
    return jnp.where(row < count - distance, moved, 0.0)


def conv_kernel(
    mixed_ref, halo_ref, keep_ref, taps_ref, quads_ref,
    conv_ref, gated_ref, own_ref, other_ref,
    w_ref, sem,
):
    first = 3 * IN_ROWS * OUT_COLS
    copy = fetch(quads_ref, first, IN_ROWS * OUT_COLS, w_ref, sem)
    copy.start()
    rows = mixed_ref.shape[0] // 2
    for s in range(2):
        at = pl.ds(s * rows, rows)
        driven = mixed_ref[at, :D_HALF] * mixed_ref[at, 2 * D_HALF :]
        halo = halo_ref[s]
        conv = (
            taps_ref[2:3] * driven
            + taps_ref[1:2] * keep_ref[at, 0:1] * shift_down(driven, halo, 1)
            + taps_ref[0:1] * keep_ref[at, 1:2] * shift_down(driven, halo, 2)
        )
        conv_ref[at, :] = conv
        gated_ref[at, :] = (mixed_ref[at, D_HALF : 2 * D_HALF] * conv).astype(jnp.bfloat16)
    copy.wait()
    for j in range(OUT_COLS):
        value = f32_dot(gated_ref[...], row_tile(w_ref, IN_ROWS, OUT_COLS, j))
        put_part(own_ref, other_ref, slice(j * OUT_TILE, (j + 1) * OUT_TILE), value)


def conv_forward(mixed, halos, keep, taps, quads):
    rows = mixed.shape[0]
    return call(
        conv_kernel,
        [
            shape((rows, D_HALF), jnp.float32),
            shape((rows, D_HALF), jnp.bfloat16),
        ]
        + parts(rows),
        [mixed, halos, keep, taps, quads],
        [
            pltpu.VMEM((IN_ROWS * OUT_COLS, BS, LANES), jnp.bfloat16),
            pltpu.SemaphoreType.DMA(()),
        ],
        micros=5,
        any_in=(4,),
    )


def join_rows(ref, mine_ref, theirs_ref):
    rows = mine_ref.shape[0]
    ref[:rows] = mine_ref[...]
    ref[rows:] = theirs_ref[...]


def ff_kernel(
    mine_ref, theirs_ref, cot_ref, quads_ref,
    act_ref, gg_ref, gu_ref,
    gate_ref, up_ref, down_ref, normed_ref, sems,
):
    _, out_end, gate_end, up_end = quad_bounds()
    per = IN_ROWS * FF_COLS
    copies = [
        fetch(quads_ref, first, per, ref, sems.at[n])
        for n, (first, ref) in enumerate(
            ((out_end, gate_ref), (gate_end, up_ref), (up_end, down_ref))
        )
    ]
    for c in copies:
        c.start()
    step = TILE // HALF
    join_rows(normed_ref, mine_ref, theirs_ref)

    def tile(t, wait):
        cols = pl.ds(pl.multiple_of(t * TILE, TILE), TILE)
        if wait:
            copies[0].wait()
        gate = f32_dot(
            normed_ref[...], col_tile(gate_ref, IN_ROWS, FF_COLS, QUADS_WIDE * t, QUADS_WIDE)
        )
        if wait:
            copies[1].wait()
        up = f32_dot(
            normed_ref[...], col_tile(up_ref, IN_ROWS, FF_COLS, QUADS_WIDE * t, QUADS_WIDE)
        )
        if wait:
            copies[2].wait()
        grad_act = nt_dot(cot_ref[...], row_rows(down_ref, step * t, step, OUT_COLS))
        sig = jax.nn.sigmoid(gate)
        silu = gate * sig
        act_ref[:, cols] = (silu * up).astype(jnp.bfloat16)
        gg_ref[:, cols] = (grad_act * up * sig * (1.0 + gate * (1.0 - sig))).astype(jnp.bfloat16)
        gu_ref[:, cols] = (grad_act * silu).astype(jnp.bfloat16)

    tile(0, True)

    def later(t, carry):
        tile(t, False)
        return carry

    lax.fori_loop(1, FF_HALF // TILE, later, 0)


def ff_pass(mine, theirs, cot, quads):
    rows = cot.shape[0]
    wide = shape((rows, FF_HALF), jnp.bfloat16)
    weights = pltpu.VMEM((IN_ROWS * FF_COLS, BS, LANES), jnp.bfloat16)
    return call(
        ff_kernel,
        [wide] * 3,
        [mine, theirs, cot, quads],
        [weights] * 3 + [pltpu.VMEM(cot.shape, cot.dtype), pltpu.SemaphoreType.DMA((3,))],
        micros=15,
        any_in=(3,),
    )


BACK_ROWS = 8


def ff_back_kernel(gg_ref, gu_ref, quads_ref, own_ref, other_ref, gate_ref, up_ref, sems):
    _, out_end, gate_end, _ = quad_bounds()
    step = BACK_ROWS * FF_COLS
    groups = IN_ROWS // BACK_ROWS
    copies = []
    for g in range(groups):
        at = pl.ds(g * step, step)
        copies.append(fetch(quads_ref, out_end + g * step, step, gate_ref.at[at], sems.at[0, g]))
        copies.append(fetch(quads_ref, gate_end + g * step, step, up_ref.at[at], sems.at[1, g]))
    for c in copies:
        c.start()
    for g in range(groups):
        copies[2 * g].wait()
        value = nt_dot(gg_ref[...], col_rows(gate_ref, BACK_ROWS * g, BACK_ROWS, FF_COLS))
        copies[2 * g + 1].wait()
        value = value + nt_dot(
            gu_ref[...], col_rows(up_ref, BACK_ROWS * g, BACK_ROWS, FF_COLS)
        )
        put_part(own_ref, other_ref, slice(g * BACK_ROWS * BS, (g + 1) * BACK_ROWS * BS), value)


def ff_back(gg, gu, quads):
    rows = gg.shape[0]
    weights = pltpu.VMEM((IN_ROWS * FF_COLS, BS, LANES), jnp.bfloat16)
    return call(
        ff_back_kernel,
        parts(rows),
        [gg, gu, quads],
        [weights, weights, pltpu.SemaphoreType.DMA((2, IN_ROWS // BACK_ROWS))],
        micros=11,
        any_in=(2,),
    )


def down_grad_kernel(
    normed_ref, act_ref, gg_ref, cot_ref, near_ref, head_ref, dgate_ref, ddown_ref, sem
):
    step = TILE // HALF
    behind = head_ref.shape[0]

    def tile(t, carry):
        cols = pl.ds(pl.multiple_of(t * TILE, TILE), TILE)
        put_row_rows(
            ddown_ref, f32_dot(act_ref[:, cols].T, cot_ref[...]), step * t, step, OUT_COLS
        )
        return carry

    lax.fori_loop(0, FF_HALF // TILE, tile, 0)
    move = pltpu.make_async_copy(
        ddown_ref.at[pl.ds(behind, PER_PLANE)], near_ref.at[pl.ds(PER_PLANE, PER_PLANE)], sem
    )
    move.start()
    head_ref[...] = ddown_ref[:behind]
    turned = normed_ref[:, : 2 * BS].T
    ahead = dgate_ref.shape[0] - FF_COLS
    first = f32_dot(turned[:BS], gg_ref[...]).astype(jnp.bfloat16)
    second = f32_dot(turned[BS:], gg_ref[:, : ahead * LANES]).astype(jnp.bfloat16)
    for j in range(FF_COLS):
        dgate_ref[j] = first[:, j * LANES : (j + 1) * LANES]
    for j in range(ahead):
        dgate_ref[FF_COLS + j] = second[:, j * LANES : (j + 1) * LANES]
    move.wait()


PER_PLANE = BLOCKS // 4 // Z


def down_grad(normed, act, gg, cot):
    return call(
        down_grad_kernel,
        [
            shape((2 * PER_PLANE, BS, LANES), jnp.bfloat16),
            shape((3 * PER_PLANE - quad_bounds()[3], BS, LANES), jnp.bfloat16),
            shape((PER_PLANE - quad_bounds()[1], BS, LANES), jnp.bfloat16),
        ],
        [normed, act, gg, cot],
        [
            pltpu.VMEM((DOWN_ROWS * OUT_COLS, BS, LANES), jnp.bfloat16),
            pltpu.SemaphoreType.DMA(()),
        ],
        micros=8,
        any_out=(0,),
    )


def ff_grads_kernel(
    normed_ref, gg_ref, gu_ref, ddown_ref, grads_ref, dgate_ref, dup_ref, turned_ref, sems
):
    _, out_end, _, up_end = quad_bounds()
    per = IN_ROWS * FF_COLS
    ahead = PER_PLANE - out_end
    behind = 3 * PER_PLANE - up_end
    pieces = (
        (ddown_ref, 2 * per - ahead, behind),
        (dgate_ref.at[pl.ds(ahead, per - ahead)], 0, per - ahead),
        (dup_ref, per - ahead, per),
    )
    moves = [
        pltpu.make_async_copy(src, grads_ref.at[pl.ds(first, count)], sems.at[n])
        for n, (src, first, count) in enumerate(pieces)
    ]
    moves[0].start()
    turned_ref[...] = normed_ref[...].T

    def weight_grad(grad_ref, out_ref):
        def tile(t, carry):
            cols = pl.ds(pl.multiple_of(t * TILE, TILE), TILE)
            put_col_tile(
                out_ref,
                f32_dot(turned_ref[...], grad_ref[:, cols]),
                IN_ROWS,
                FF_COLS,
                QUADS_WIDE * t,
                QUADS_WIDE,
            )
            return carry

        lax.fori_loop(0, FF_HALF // TILE, tile, 0)

    weight_grad(gg_ref, dgate_ref)
    moves[1].start()
    weight_grad(gu_ref, dup_ref)
    moves[2].start()
    for move in moves:
        move.wait()


def ff_grads(normed, gg, gu, ddown):
    rows = normed.shape[0]
    grads = pltpu.VMEM((IN_ROWS * FF_COLS, BS, LANES), jnp.bfloat16)
    return call(
        ff_grads_kernel,
        [shape((2 * PER_PLANE, BS, LANES), jnp.bfloat16)],
        [normed, gg, gu, ddown],
        [grads] * 2 + [pltpu.VMEM((D, rows), jnp.bfloat16), pltpu.SemaphoreType.DMA((3,))],
        micros=10,
        any_out=(0,),
    )[0]


def ff_out_kernel(act_ref, quads_ref, own_ref, other_ref, down_ref, sem):
    weights = fetch(quads_ref, quad_bounds()[3], DOWN_ROWS * OUT_COLS, down_ref, sem)
    weights.start()
    weights.wait()
    for j in range(OUT_COLS):
        value = f32_dot(act_ref[...], row_tile(down_ref, DOWN_ROWS, OUT_COLS, j))
        put_part(own_ref, other_ref, slice(j * OUT_TILE, (j + 1) * OUT_TILE), value)


def ff_out(act, quads):
    rows = act.shape[0]
    return call(
        ff_out_kernel,
        parts(rows),
        [act, quads],
        [
            pltpu.VMEM((IN_ROWS * FF_COLS, BS, LANES), jnp.bfloat16),
            pltpu.SemaphoreType.DMA(()),
        ],
        micros=6,
        any_in=(1,),
    )


def conv_back_kernel(
    mine_ref, theirs_ref, mixed_ref, conv_ref, gated_ref, halo_ref, keep_ref, taps_ref, quads_ref,
    dout_ref, gconv_ref, ggate_ref, heads_ref, tap_ref, w_ref, branch_ref, sem,
):
    join_rows(branch_ref, mine_ref, theirs_ref)
    first = 3 * IN_ROWS * OUT_COLS
    copy = fetch(quads_ref, first, IN_ROWS * OUT_COLS, w_ref, sem)
    copy.start()
    copy.wait()
    rows = mixed_ref.shape[0] // 2
    step = 2 * BS // HALF * 2
    grad = jnp.concatenate(
        [
            nt_dot(branch_ref[...], row_rows(w_ref, g * step, step, OUT_COLS))
            for g in range(IN_ROWS // step)
        ],
        axis=1,
    )
    ggate_ref[...] = (grad * conv_ref[...]).astype(jnp.bfloat16)
    gconv_ref[...] = grad * mixed_ref[:, D_HALF : 2 * D_HALF]
    taps = [jnp.zeros((1, D_HALF), jnp.float32)] * 3
    for s in range(2):
        at = pl.ds(s * rows, rows)
        driven = mixed_ref[at, :D_HALF] * mixed_ref[at, 2 * D_HALF :]
        halo = halo_ref[s]
        grad_conv = gconv_ref[at, :]
        one = keep_ref[at, 0:1] * grad_conv
        two = keep_ref[at, 1:2] * grad_conv
        terms = (two * shift_down(driven, halo, 2), one * shift_down(driven, halo, 1), grad_conv * driven)
        taps = [a + jnp.sum(b, axis=0, keepdims=True) for a, b in zip(taps, terms)]
        heads_ref[s, 0:1] = taps_ref[0:1] * two[0:1]
        heads_ref[s, 1:2] = taps_ref[1:2] * one[0:1] + taps_ref[0:1] * two[1:2]
    tap_ref[...] = jnp.concatenate(taps, axis=0)
    put_row_rows(dout_ref, f32_dot(gated_ref[...].T, branch_ref[...]), 0, IN_ROWS, OUT_COLS)


def conv_back(mine, theirs, mixed, conv, gated, halos, keep, taps, quads):
    rows = mixed.shape[0]
    return call(
        conv_back_kernel,
        [
            shape((IN_ROWS * OUT_COLS, BS, LANES), jnp.bfloat16),
            shape((rows, D_HALF), jnp.float32),
            shape((rows, D_HALF), jnp.bfloat16),
            shape((2, 2, D_HALF), jnp.float32),
            shape((3, D_HALF), jnp.float32),
        ],
        [mine, theirs, mixed, conv, gated, halos, keep, taps, quads],
        [
            pltpu.VMEM((IN_ROWS * OUT_COLS, BS, LANES), jnp.bfloat16),
            pltpu.VMEM((rows, D), jnp.bfloat16),
            pltpu.SemaphoreType.DMA(()),
        ],
        micros=7,
        any_in=(8,),
    )


def mix_back_kernel(
    place_ref, gconv_ref, ggate_ref, mixed_ref, normed_ref, tails_ref, keep_ref, taps_ref,
    dout_ref, dgate_ref, given_ref,
    grads_ref, grad_ref, first_ref, second_ref,
    din_ref, turned_ref, stage_ref, sems,
):
    z, far = place_ref[0], place_ref[1] ^ (PLANE - 1)
    count = PER_PLANE // PLANE
    half = count // 2
    corners = (first_ref, second_ref)
    last = z < Z // 2
    fetches = [
        pltpu.make_async_copy(
            given_ref.at[pl.ds(PER_PLANE + far * count + n * half, half)],
            stage_ref.at[n],
            sems.at[0, n],
        )
        for n in range(2)
    ]
    hands = [pltpu.make_async_copy(stage_ref.at[n], corners[n], sems.at[1, n]) for n in range(2)]

    @pl.when(last)
    def _():
        for c in fetches:
            c.start()

    moves = []
    at = IN_ROWS * IN_COLS
    for n, piece in enumerate((dout_ref, dgate_ref)):
        rows = piece.shape[0]
        moves.append(pltpu.make_async_copy(piece, grads_ref.at[pl.ds(at, rows)], sems.at[2, n]))
        at += rows
    for move in moves:
        move.start()
    turned_ref[...] = normed_ref[...].T
    rows = mixed_ref.shape[0] // 2
    for s in range(2):
        at = pl.ds(s * rows, rows)
        grad_conv = gconv_ref[at, :]
        one = keep_ref[at, 0:1] * grad_conv
        two = keep_ref[at, 1:2] * grad_conv
        grad = (
            taps_ref[2:3] * grad_conv
            + taps_ref[1:2] * shift_up(one, 1)
            + taps_ref[0:1] * shift_up(two, 2)
        )
        row = lax.broadcasted_iota(jnp.int32, grad.shape, 0)
        tail = tails_ref[s]
        grad = grad + jnp.where(
            row == rows - 2, tail[0:1], jnp.where(row == rows - 1, tail[1:2], 0.0)
        )
        grad_ref[at, :D_HALF] = (grad * mixed_ref[at, 2 * D_HALF :]).astype(jnp.bfloat16)
        grad_ref[at, D_HALF : 2 * D_HALF] = ggate_ref[at, :]
        grad_ref[at, 2 * D_HALF :] = (grad * mixed_ref[at, :D_HALF]).astype(jnp.bfloat16)

    @pl.when(last)
    def _():
        for c, d in zip(fetches, hands):
            c.wait()
            d.start()

    def tile(t, carry):
        cols = pl.ds(pl.multiple_of(t * TILE, TILE), TILE)
        put_col_tile(
            din_ref,
            f32_dot(turned_ref[...], grad_ref[:, cols]),
            IN_ROWS,
            IN_COLS,
            QUADS_WIDE * t,
            QUADS_WIDE,
        )
        return carry

    lax.fori_loop(0, IN_COLS // QUADS_WIDE, tile, 0)
    moves.append(
        pltpu.make_async_copy(din_ref, grads_ref.at[pl.ds(0, IN_ROWS * IN_COLS)], sems.at[3, 0])
    )
    moves[-1].start()

    @pl.when(last)
    def _():
        for d in hands:
            d.wait()

    for k in range(PLANE):

        @pl.when(jnp.logical_not(last) & (far == k))
        def _(k=k):
            copies = []
            for n, corner in enumerate(corners):
                low = k * count + n * half
                high = low + half
                start = 0
                for piece in (din_ref, dout_ref, dgate_ref):
                    stop = start + piece.shape[0]
                    a, b = max(low, start), min(high, stop)
                    if a < b:
                        copies.append(
                            pltpu.make_async_copy(
                                piece.at[pl.ds(a - start, b - a)],
                                corner.at[pl.ds(a - low, b - a)],
                                sems.at[4, len(copies)],
                            )
                        )
                    start = stop
            for c in copies:
                c.start()
            for c in copies:
                c.wait()

    for move in moves:
        move.wait()


def mix_back(place, gconv, ggate, mixed, normed, tails, keep, taps, dout, dgate, given):
    rows = mixed.shape[0]
    half = shape((PER_PLANE // PLANE // 2, BS, LANES), jnp.bfloat16)
    ins = [gconv, ggate, mixed, normed, tails, keep, taps, dout, dgate]
    hbm = pl.BlockSpec(memory_space=pltpu.HBM)
    return pl.pallas_call(
        mix_back_kernel,
        out_shape=(
            jax.ShapeDtypeStruct(given.shape, given.dtype),
            shape((rows, 3 * D_HALF), jnp.bfloat16),
            half,
            half,
        ),
        in_specs=[SCALARS] + whole(len(ins)) + [hbm],
        out_specs=(hbm, whole(1)[0], hbm, hbm),
        scratch_shapes=[
            pltpu.VMEM((IN_ROWS * IN_COLS, BS, LANES), jnp.bfloat16),
            pltpu.VMEM((D, rows), jnp.bfloat16),
            pltpu.VMEM((2,) + half.shape, jnp.bfloat16),
            pltpu.SemaphoreType.DMA((5, 4)),
        ],
        input_output_aliases={len(ins) + 1: 0},
        compiler_params=pltpu.CompilerParams(vmem_limit_bytes=VMEM_MOST),
        cost_estimate=busy(8),
    )(place, *ins, given)


def mix_rest_kernel(grad_ref, quads_ref, own_ref, other_ref, w_ref, sem):
    copy = fetch(quads_ref, 0, IN_ROWS * IN_COLS, w_ref, sem)
    copy.start()
    copy.wait()
    for g in range(IN_ROWS // BACK_ROWS):
        value = nt_dot(grad_ref[...], col_rows(w_ref, BACK_ROWS * g, BACK_ROWS, IN_COLS))
        put_part(own_ref, other_ref, slice(g * BACK_ROWS * BS, (g + 1) * BACK_ROWS * BS), value)


def mix_rest(grad, quads):
    rows = grad.shape[0]
    return call(
        mix_rest_kernel,
        parts(rows),
        [grad, quads],
        [
            pltpu.VMEM((IN_ROWS * IN_COLS, BS, LANES), jnp.bfloat16),
            pltpu.SemaphoreType.DMA(()),
        ],
        micros=5,
        any_in=(1,),
    )


def through(pairs, stage_ref, sems):
    ins = [
        pltpu.make_async_copy(src, stage_ref.at[n], sems.at[0, n])
        for n, (src, _) in enumerate(pairs)
    ]
    outs = [
        pltpu.make_async_copy(stage_ref.at[n], dst, sems.at[1, n])
        for n, (_, dst) in enumerate(pairs)
    ]
    for c in ins:
        c.start()
    for c, d in zip(ins, outs):
        c.wait()
        d.start()
    for d in outs:
        d.wait()


def halves_kernel(a_ref, b_ref, first_ref, second_ref, stage_ref, sems):
    through(((a_ref.at[0], first_ref), (b_ref.at[1], second_ref)), stage_ref, sems)


def halves_of(a, b):
    hbm = pl.BlockSpec(memory_space=pltpu.HBM)
    out = jax.ShapeDtypeStruct(a.shape[1:], a.dtype)
    return pl.pallas_call(
        halves_kernel,
        out_shape=(out, out),
        in_specs=[hbm, hbm],
        out_specs=(hbm, hbm),
        scratch_shapes=[
            pltpu.VMEM((2,) + out.shape, out.dtype),
            pltpu.SemaphoreType.DMA((2, 2)),
        ],
        compiler_params=pltpu.CompilerParams(vmem_limit_bytes=VMEM_ALL),
        cost_estimate=busy(2),
    )(a, b)


def place_kernel(places, place_ref, *refs):
    out_ref, stage_ref, sems = refs[-3:]
    plane, here, core = place_ref[0], place_ref[1], place_ref[2]
    pairs = []
    for src, (k, slot) in zip(refs, places):
        if slot is None:
            for s in range(2):
                pairs.append((src.at[s], out_ref.at[plane, here ^ k, s ^ core]))
        else:
            pairs.append((src, out_ref.at[plane, here ^ k, slot ^ core]))
    through(pairs, stage_ref, sems)


def put_plane(plane, here, core, pieces, out):
    hbm = pl.BlockSpec(memory_space=pltpu.HBM)
    places = tuple((piece[1], piece[2] if len(piece) == 3 else None) for piece in pieces)
    given = [piece[0] for piece in pieces]
    half = given[0].shape[-3:]
    count = sum(2 if slot is None else 1 for _, slot in places)
    full = jax.ShapeDtypeStruct((Z, PLANE, CORES) + half, given[0].dtype)
    aliases = {} if out is None else {len(given) + 1: 0}
    given += [] if out is None else [out]
    return pl.pallas_call(
        functools.partial(place_kernel, places),
        out_shape=full,
        in_specs=[SCALARS] + [hbm] * len(given),
        out_specs=hbm,
        scratch_shapes=[
            pltpu.VMEM((count,) + half, full.dtype),
            pltpu.SemaphoreType.DMA((2, count)),
        ],
        input_output_aliases=aliases,
        compiler_params=pltpu.CompilerParams(vmem_limit_bytes=VMEM_ALL),
        cost_estimate=busy(0.5 * count + 1),
    )(jnp.stack([plane, here, core]), *given)


PIECES = (
    ((0, 0), (1, 0), (1, 1)),
    ((1, 0), (1, 1), (0, 0)),
    ((1, 1), (1, 0), (0, 1)),
    ((0, 1), (1, 1), (1, 0)),
)


def pieces_kernel(wanted, place_ref, near_ref, far_ref, *refs):
    outs, (stage_ref, sems) = refs[:-2], refs[-2:]
    z, here = place_ref[0], place_ref[1]
    count = outs[0].shape[0]
    for plane, slots in enumerate(PIECES):

        @pl.when(z == plane)
        def _(slots=slots):
            pairs = []
            for (slot, k), dst in zip(wanted, outs):
                array, part = slots[slot]
                src = (near_ref, far_ref)[array]
                pairs.append((src.at[pl.ds(part * PER_PLANE + (here ^ k) * count, count)], dst))
            through(pairs, stage_ref, sems)


def pieces(wanted, z, here, near, far):
    hbm = pl.BlockSpec(memory_space=pltpu.HBM)
    out = jax.ShapeDtypeStruct((PER_PLANE // PLANE, BS, LANES), near.dtype)
    return pl.pallas_call(
        functools.partial(pieces_kernel, wanted),
        out_shape=(out,) * len(wanted),
        in_specs=[SCALARS, hbm, hbm],
        out_specs=(hbm,) * len(wanted),
        scratch_shapes=[
            pltpu.VMEM((len(wanted),) + out.shape, out.dtype),
            pltpu.SemaphoreType.DMA((2, len(wanted))),
        ],
        compiler_params=pltpu.CompilerParams(vmem_limit_bytes=VMEM_ALL),
        cost_estimate=busy(len(wanted) + 1),
    )(jnp.stack([z, here]), near, far)


def sums_kernel(count, parts, starts, lives, terms, scalars_ref, *refs):
    n = len(starts)
    sources, outs = refs[:n], refs[n : n + len(terms)]
    held_ref, made_ref, in_sems, out_sems = refs[n + len(terms) :]
    spans, at = [], 0
    for size in parts:
        spans.append((at, size))
        at += size

    def fetches(i):
        for c, (at, size) in enumerate(spans):
            yield pltpu.make_async_copy(
                sources[i].at[pl.ds(scalars_ref[starts[i]] + at, size)],
                held_ref.at[i, pl.ds(at, size)],
                in_sems.at[i, c],
            )

    copies = [list(fetches(i)) for i in range(n)]

    def each(c, act):
        for i in range(n):
            if lives[i] is None:
                act(copies[i][c])
            else:
                pl.when(scalars_ref[lives[i]] != 0)(functools.partial(act, copies[i][c]))

    for c in range(len(spans)):
        each(c, lambda copy: copy.start())
    stores = []
    for c, (at, size) in enumerate(spans):
        each(c, lambda copy: copy.wait())

        def one(q, carry):
            values = [held_ref[i, q].astype(jnp.float32) for i in range(n)]
            for k, row in enumerate(terms):
                made = None
                for i, weight in row:
                    term = values[i]
                    if weight is not None:
                        term = jnp.where(scalars_ref[weight] != 0, term, 0.0)
                    made = term if made is None else made + term
                made_ref[k, q] = made.astype(made_ref.dtype)
            return carry

        lax.fori_loop(at, at + size, one, 0, unroll=7)
        for k, out in enumerate(outs):
            span = pl.ds(at, size)
            stores.append(
                pltpu.make_async_copy(made_ref.at[k, span], out.at[span], out_sems.at[k, c])
            )
            stores[-1].start()
    for store in stores:
        store.wait()


def sums(count, sources, weights):
    scalars, starts, lives, terms = [], [], [], []

    def scalar(value):
        scalars.append(jnp.asarray(value, jnp.int32))
        return len(scalars) - 1

    for i, (_, first) in enumerate(sources):
        used = [row[i] for row in weights if not (isinstance(row[i], int) and row[i] == 0)]
        starts.append(scalar(first))
        if any(isinstance(w, int) for w in used):
            lives.append(None)
        else:
            lives.append(
                scalar(functools.reduce(jnp.maximum, [jnp.asarray(w, jnp.int32) for w in used]))
            )
    for row in weights:
        terms.append(
            [
                (i, None if isinstance(w, int) else scalar(w))
                for i, w in enumerate(row)
                if not (isinstance(w, int) and w == 0)
            ]
        )
    unit = count // 5
    parts = (unit, 2 * unit, 2 * unit)
    out = jax.ShapeDtypeStruct((count, BS, LANES), jnp.bfloat16)
    hbm = pl.BlockSpec(memory_space=pltpu.HBM)
    n, k = len(sources), len(weights)
    return pl.pallas_call(
        functools.partial(sums_kernel, count, parts, starts, lives, terms),
        out_shape=[out] * k,
        in_specs=[SCALARS] + [hbm] * n,
        out_specs=[hbm] * k,
        scratch_shapes=[
            pltpu.VMEM((n,) + out.shape, out.dtype),
            pltpu.VMEM((k,) + out.shape, out.dtype),
            pltpu.SemaphoreType.DMA((n, len(parts))),
            pltpu.SemaphoreType.DMA((k, len(parts))),
        ],
        compiler_params=pltpu.CompilerParams(vmem_limit_bytes=VMEM_ALL),
        cost_estimate=busy(0.35 * (n + k) + 1),
    )(jnp.stack(scalars), *[array.reshape(-1, BS, LANES) for array, _ in sources])


def mend_kernel(scalars_ref, one_ref, two_ref, a_ref, b_ref, x_ref, y_ref):
    later = jnp.where(pl.program_id(0) == 1, 1.0, 0.0)
    x = one_ref[...].astype(jnp.float32) + later * b_ref[...].astype(jnp.float32)
    y = two_ref[...].astype(jnp.float32) + (1.0 - later) * a_ref[...].astype(jnp.float32)
    x_ref[...] = x.astype(x_ref.dtype)
    y_ref[...] = y.astype(y_ref.dtype)


def mend(array, first, second, a, b):
    half = a.shape[0]
    block = (half, BS, LANES)
    out = jax.ShapeDtypeStruct((2 * half, BS, LANES), jnp.bfloat16)

    def at(n):
        return pl.BlockSpec(block, lambda step, ref: (ref[n] + step, 0, 0))

    fixed = pl.BlockSpec(block, lambda step, ref: (0, 0, 0))
    moving = pl.BlockSpec(block, lambda step, ref: (step, 0, 0))
    return pl.pallas_call(
        mend_kernel,
        grid_spec=pltpu.PrefetchScalarGridSpec(
            num_scalar_prefetch=1,
            grid=(2,),
            in_specs=[at(0), at(1), fixed, fixed],
            out_specs=[moving, moving],
        ),
        out_shape=[out, out],
        compiler_params=pltpu.CompilerParams(vmem_limit_bytes=VMEM_ALL),
        cost_estimate=busy(3),
    )(jnp.stack([first, second]).astype(jnp.int32), array, array, a, b)


UP = [(0, 1), (1, 2), (2, 3)]
DOWN = [(1, 0), (2, 1), (3, 2)]
SLOT_PLANES = ((0, 1, 2, 3), (1, 2, 0, 3), (2, 1, 3, 0), (3, 2, 1, 0))
INNER = [(1, 0), (2, 3), (0, 1), (3, 2)]


def reverse(pairs):
    return [(b, a) for a, b in pairs]


def together(*values):
    return lax.optimization_barrier(values)


def over_z(block, pairs):
    return send(block, plane_route(pairs))


def over_x(block):
    return send(block, ACROSS_X)


def over_y(block):
    return send(block, ACROSS_Y)


def gather_weights(own, z, here, core, beside):
    edge = (z == 0) | (z == Z - 1)
    up, down, x0, y0 = together(over_z(own, UP), over_z(own, DOWN), over_x(own), over_y(own))
    one = jnp.where(z < 2, down, up)
    first_x = over_x(one)
    f1 = over_y(first_x)
    up_two, down_two, x1, y1, beside = together(
        over_z(up, UP[1:]), over_z(down, DOWN[:2]), first_x, over_y(one), beside
    )
    two = pick(z, [down_two, up, down, up_two])
    ends, x2, y2, f0, f1 = together(
        over_z(jnp.where(z == 2, up_two, down_two), [UP[2], DOWN[0]]),
        over_x(two),
        over_y(two),
        over_x(y0),
        f1,
    )
    three = pick(z, [ends, down_two, up_two, ends])

    def put(slot, pieces, out):
        plane = pick(z, [jnp.int32(row[slot]) for row in SLOT_PLANES])
        return put_plane(plane, here, core, pieces, out)

    out = put(0, ((own, 0), (x0, 1), (y0, 2), (f0, 3)), None)
    out = put(1, ((one, 0), (x1, 1), (y1, 2), (f1, 3)), out)
    out = put(2, ((two, 0), (x2, 1), (y2, 2)), out)
    x3, y3, f2, out = together(
        over_x(three), over_y(three), over_z(jnp.where(edge, f0, f1), INNER), out
    )
    first, second = halves_of(y3, x3)
    fa, fb = over_x(first), over_y(second)
    out = put(2, ((f2, 3),), out)
    out = put(3, ((three, 0), (x3, 1), (y3, 2)), out)
    fa, fb, out = together(fa, fb, out)
    out = put(3, ((fa, 3, 0), (fb, 3, 1)), out)
    return out.reshape(-1, BS, LANES), beside


def reduce_grads(near, far, corners, z, here, core, meanwhile, operands):
    count = PER_PLANE // PLANE
    half = count // 2

    def flag(test):
        return test.astype(jnp.int32)

    edge = flag((z == 0) | (z == Z - 1))
    inner = 1 - edge
    after = flag(z >= 2)
    part_three = 1 - after
    part_one = z % 2
    part_two = 1 - part_one

    def at(part, k):
        return part * PER_PLANE + (here ^ k) * count

    def of_zero(k):
        return [(near, at(after, k)), (far, at(after, k))]

    def of_two(k):
        return [(near, at(part_two, k)), (far, at(part_two, k))]

    def of_one(k):
        return (far, at(part_one, k))

    got_a, got_b = together(over_x(corners[0]), over_y(corners[1]))
    x3, y3 = mend(near, at(part_three, 1) // half, at(part_three, 2) // half, got_a, got_b)
    x3, y3, far, operands = together(x3, y3, far, operands)
    (two_far,) = pieces(((2, 3),), z, here, near, far)
    two_x, two_y, one_y, zero_x = pieces(((2, 1), (2, 2), (1, 2), (0, 1)), z, here, near, far)
    got_x, got_y, got_z, two_x, two_y, one_y, zero_x = together(
        over_x(x3),
        over_y(y3),
        over_z(two_far, reverse(INNER)),
        over_x(two_x),
        over_y(two_y),
        one_y,
        zero_x,
    )
    f0, f1, three = sums(
        count,
        of_zero(3) + [of_one(3), (got_z, 0), (near, at(part_three, 0)), (got_x, 0), (got_y, 0)],
        [[edge, inner, 0, edge, 0, 0, 0], [0, 0, 1, inner, 0, 0, 0], [0, 0, 0, 0, 1, 1, 1]],
    )
    got_f0, got_f1, got_z, beside = together(
        over_x(f0),
        over_y(f1),
        over_z(three, [(3, 2), (0, 1)]),
        meanwhile(*operands),
    )
    x1, moved = sums(
        count,
        [of_one(1), (got_f1, 0), of_two(0)[1], (two_x, 0), (two_y, 0), (three, 0), (got_z, 0)],
        [[1, 1, 0, 0, 0, 0, 0], [0, 0, edge, edge, edge, inner, inner]],
    )
    x1, moved, got_f0, two_x, two_y = together(x1, moved, got_f0, two_x, two_y)
    (y0,) = sums(count, of_zero(2) + [(got_f0, 0)], [[edge, inner, 1]])
    (two,) = sums(count, [of_two(0)[0], (two_x, 0), (two_y, 0)], [[1, 1, 1]])
    got_x, got_y, got_up, got_down, y0, two = together(
        over_x(x1),
        over_y(one_y),
        over_z(moved, reverse(UP[1:])),
        over_z(moved, reverse(DOWN[:2])),
        y0,
        two,
    )
    low, high = flag(z == 1), flag(z == 2)
    up, down = sums(
        count,
        [of_one(0), (got_x, 0), (got_y, 0), (two, 0), (got_up, 0), (got_down, 0)],
        [
            [1 - low, 1 - low, 1 - low, low, 1, 0],
            [1 - high, 1 - high, 1 - high, high, 0, 1],
        ],
    )
    got = together(
        over_x(zero_x), over_y(y0), over_z(up, reverse(UP)), over_z(down, reverse(DOWN))
    )
    sources, rows = [], []
    for n, first in enumerate((core * half, (1 - core) * half)):
        base = at(after, 0) + first
        sources += [(near, base), (far, base)] + [(value, first) for value in got]
        row = [edge, inner, 1, 1, 1, 1]
        rows.append([0] * 6 * n + row + [0] * 6 * (1 - n))
    return *sums(half, sources, rows), beside


def phase(value, bits):
    a, b = bits
    got = [send(value, [(i, i ^ bit) for i in range(CHIPS)]) for bit in (a, b, a | b)]
    return got


def close(value, got):
    return (value + got[0]) + (got[1] + got[2])


def spread_sum(value, beside=(None, None)):
    beside = list(beside)
    for n, bits in enumerate(((1, 2), (4, 8))):
        got, beside[n] = together(phase(value, bits), beside[n])
        value = close(value, got)
    return value + to_sibling(value), beside


def shards(
    x_in,
    cotangent,
    seq_lengths,
    weights,
    momentum,
    left_stat,
    right_stat,
    left_root,
    right_root,
    vectors,
    vector_sq,
):
    core = lax.axis_index("wt").astype(jnp.int32)
    place = lax.axis_index("seq").astype(jnp.int32)
    z, here = place // PLANE, place % PLANE
    first_core = core == 0
    rows = x_in.shape[0]
    local_count = weights.shape[0]
    quad_count = local_count // 4
    first_quad = (place * CORES + core) * quad_count

    kept, sent = split_weights(core, first_quad, weights)
    quads, wide = gather_weights(
        jnp.stack([kept, to_sibling(sent)]), z, here, core, widen(momentum, left_root, right_root)
    )

    both_x = jnp.concatenate([x_in, to_sibling(x_in)], axis=0)
    both_cot = jnp.concatenate([cotangent, to_sibling(cotangent)], axis=0)
    starts = jnp.stack([place * CORES + core, place * CORES + 1 - core]) * rows
    places = (starts[:, None] + jnp.arange(rows, dtype=jnp.int32)[None, :]).reshape(-1)
    keep_one, keep_two = keep_masks(places, seq_lengths)
    lane = jnp.arange(LANES)[None, :]
    keep = jnp.where(lane == 0, keep_one, jnp.where(lane == 1, keep_two, 0.0))
    taps = take(vectors[2:].reshape(3, IN_ROWS, 2, HALF), core, 2).reshape(3, D_HALF)

    hidden_both = both_x.astype(jnp.float32)
    scale_both = rms_scale(hidden_both)
    normed = (hidden_both * scale_both * vectors[0]).astype(jnp.bfloat16)
    hidden_in, scale_one = hidden_both[:rows], scale_both[:rows]
    mixed = mix(normed, quads)
    ends = jnp.stack([mixed[rows - 2 : rows], mixed[-2:]])
    ends = ends[:, :, :D_HALF] * ends[:, :, 2 * D_HALF :]
    carried = send(jnp.where(first_core, ends[1], ends[0]), [(i, i + 1) for i in range(CHIPS - 1)])
    halos = jnp.stack(
        [jnp.where(first_core, carried, ends[1]), jnp.where(first_core, ends[0], carried)]
    )
    conv_out, gated_out, part, other = conv_forward(mixed, halos, keep, taps, quads)
    middle = hidden_in + part + to_sibling(other)
    scale_two = rms_scale(middle)
    own_two = (middle * scale_two * vectors[1]).astype(jnp.bfloat16)
    other_two = to_sibling(own_two)
    activated, grad_gate, grad_up = ff_pass(own_two, other_two, both_cot, quads)
    part, other = ff_back(grad_gate, grad_up, quads)
    normed_two = jnp.concatenate([own_two, other_two], axis=0)
    near_grads, grad_w_down, grad_w_gate = down_grad(normed_two, activated, grad_gate, both_cot)
    grad_normed_two = part + to_sibling(other)
    gain_two_grad, middle_term = norm_back(middle, scale_two, vectors[1], grad_normed_two)
    grad_middle = cotangent.astype(jnp.float32) + middle_term
    own_branch = grad_middle.astype(jnp.bfloat16)
    grad_w_out, grad_conv, grad_output, heads, tap_grads = conv_back(
        own_branch, to_sibling(own_branch), mixed, conv_out, gated_out, halos, keep, taps, quads
    )
    from_after = send(
        jnp.where(first_core, heads[0], heads[1]), [(i + 1, i) for i in range(CHIPS - 1)]
    )
    tails = jnp.stack(
        [jnp.where(first_core, heads[1], from_after), jnp.where(first_core, from_after, heads[0])]
    )
    near_grads, grad_mixed, *corners = mix_back(
        jnp.stack([z, here]), grad_conv, grad_output, mixed, normed, tails, keep, taps,
        grad_w_out, grad_w_gate, near_grads,
    )
    near_grads, grad_w_down = together(near_grads, grad_w_down)
    far_grads = ff_grads(normed_two, grad_gate, grad_up, grad_w_down)

    def meanwhile(activated, grad_mixed):
        part, other = ff_out(activated, quads)
        out_act = (middle + part + to_sibling(other)).astype(jnp.bfloat16)
        part, other = mix_rest(grad_mixed, quads)
        grad_normed = part + to_sibling(other)
        gain_one_grad, input_term = norm_back(hidden_in, scale_one, vectors[0], grad_normed)
        tap_part = jnp.where(
            jnp.arange(2).reshape(1, 1, 2, 1) == core, tap_grads.reshape(3, IN_ROWS, 1, HALF), 0.0
        ).reshape(3, D)
        vector_part = jnp.concatenate(
            [gain_one_grad[None], gain_two_grad[None], tap_part], axis=0
        )
        return out_act, grad_middle + input_term, vector_part

    kept, sent, (out_act, in_grad, vector_part) = reduce_grads(
        near_grads, far_grads, corners, z, here, core, meanwhile, (activated, grad_mixed)
    )
    got = to_sibling(sent)

    new_momentum, precond, sums, kind_part = step_blocks(
        core, first_quad, kept, got, *wide, momentum
    )
    vector_rows = vector_part.reshape(-1, LANES)
    summed, (new_left, new_right) = spread_sum(
        jnp.concatenate([vector_rows, kind_part], axis=0),
        (stat_blocks(sums, left_stat, False), stat_blocks(sums, right_stat, True)),
    )
    vector_grads = summed[: vector_rows.shape[0]].reshape(vectors.shape)
    new_vector_sq = DECAY * vector_sq + (1.0 - DECAY) * vector_grads * vector_grads
    new_vectors = vectors - VEC_RATE * vector_grads * lax.rsqrt(new_vector_sq)
    kind_sum = jnp.sum(summed[vector_rows.shape[0] :], axis=1)[:KINDS]
    in_end, out_end, gate_end, up_end = block_bounds()
    kind_total = jnp.array(
        [in_end, out_end - in_end, gate_end - out_end, up_end - gate_end, BLOCKS - up_end],
        jnp.float32,
    ) * (BS * BS)
    kind_scale = lax.rsqrt(kind_sum / kind_total + MEAN_EPS)
    block_kinds = kind_of(first_quad + jnp.arange(local_count, dtype=jnp.int32) // 4)
    one_hot = (block_kinds[:, None] == jnp.arange(KINDS)[None, :]).astype(jnp.float32)
    block_scale = jnp.sum(one_hot * kind_scale[None, :], axis=1)
    new_weights = weights - RATE * block_scale[:, None] * precond
    return (
        out_act,
        in_grad,
        new_weights,
        new_weights.astype(jnp.bfloat16),
        new_momentum,
        new_left,
        new_right,
        vector_grads,
        new_vector_sq,
        new_vectors,
    )


def solution(mesh):
    body = shards if (mesh.shape["seq"], mesh.shape["wt"]) == (CHIPS, CORES) else shards_any
    return jax.shard_map(
        body,
        mesh=mesh,
        in_specs=(
            P(("seq", "wt"), None),
            P(("seq", "wt"), None),
            P(),
            P(("seq", "wt"), None),
            P(("seq", "wt"), None),
            P(("seq", "wt"), None),
            P(("seq", "wt"), None),
            P(("seq", "wt"), None),
            P(("seq", "wt"), None),
            P(),
            P(),
        ),
        out_specs=(
            P(("seq", "wt"), None),
            P(("seq", "wt"), None),
            P(("seq", "wt"), None),
            P(("seq", "wt"), None),
            P(("seq", "wt"), None),
            P(("seq", "wt"), None),
            P(("seq", "wt"), None),
            P(),
            P(),
            P(),
        ),
        check_vma=False,
    )
```

```python
import functools

import jax
import jax.numpy as jnp
from jax import lax
from jax.experimental import pallas as pl
from jax.experimental.pallas import tpu as pltpu
from jax.sharding import PartitionSpec as P

D = 1024
FF = 4608
BS = 64
BLOCKS = 4480


NORM_EPS = 1e-05
MEAN_EPS = 1e-06
DECAY = 0.5
MOMENT = 0.9
RATE = 0.01
VEC_RATE = 0.25
HIGHEST = lax.Precision.HIGHEST


def from_behind(block, axis, distance):
    devices = range(lax.axis_size(axis))
    route = [(i - distance, i) for i in devices if i - distance in devices]
    return lax.ppermute(block, axis, route)


def unpack_blocks(blocks, row_count, col_count):
    return (
        blocks.reshape(row_count // BS, col_count // BS, BS, BS)
        .transpose(0, 2, 1, 3)
        .reshape(row_count, col_count)
    )


def pack_blocks(matrix):
    row_count, col_count = matrix.shape
    return (
        matrix.reshape(row_count // BS, BS, col_count // BS, BS)
        .transpose(0, 2, 1, 3)
        .reshape(-1, BS * BS)
    )


def block_bounds():
    per_block = BS * BS
    in_end = 3 * D * D // per_block
    out_end = in_end + D * D // per_block
    gate_end = out_end + D * FF // per_block
    up_end = gate_end + D * FF // per_block
    return (in_end, out_end, gate_end, up_end)


def matrices(blocks):
    in_end, out_end, gate_end, up_end = block_bounds()
    w_in = unpack_blocks(blocks[:in_end], D, 3 * D)
    w_out = unpack_blocks(blocks[in_end:out_end], D, D)
    w_gate = unpack_blocks(blocks[out_end:gate_end], D, FF)
    w_up = unpack_blocks(blocks[gate_end:up_end], D, FF)
    w_down = unpack_blocks(blocks[up_end:], FF, D)
    return (w_in, w_out, w_gate, w_up, w_down)


def matmul(left_side, right_side):
    return jnp.dot(left_side, right_side, preferred_element_type=jnp.float32)


def matmul_tn(left_side, right_side):
    return lax.dot_general(
        left_side, right_side, (((0,), (0,)), ((), ())), preferred_element_type=jnp.float32
    )


def matmul_nt(left_side, right_side):
    return lax.dot_general(
        left_side, right_side, (((1,), (1,)), ((), ())), preferred_element_type=jnp.float32
    )


def rms_scale(values):
    return lax.rsqrt(jnp.mean(values * values, axis=-1, keepdims=True) + NORM_EPS)


def norm_back(values, row_scale, norm_gain, grad_normed):
    gain_grad = jnp.sum(grad_normed * values * row_scale, axis=0)
    weighted = grad_normed * norm_gain
    grad_values = row_scale * weighted - values * row_scale**3 * jnp.mean(
        weighted * values, axis=-1, keepdims=True
    )
    return (gain_grad, grad_values)


def keep_masks(places, seq_lengths):
    ends = jnp.cumsum(seq_lengths)
    starts = jnp.max(jnp.where(ends[None, :] <= places[:, None], ends[None, :], 0), axis=1)
    keep_one = (places - 1 >= starts).astype(jnp.float32)[:, None]
    keep_two = (places - 2 >= starts).astype(jnp.float32)[:, None]
    return (keep_one, keep_two)


def weight_grads(operands):
    (
        normed,
        grad_mixed,
        gated_out,
        grad_branch,
        normed_two,
        grad_gate,
        grad_up,
        activated,
        cotangent,
    ) = operands
    return jnp.concatenate(
        [
            pack_blocks(matmul_tn(normed, grad_mixed)),
            pack_blocks(matmul_tn(gated_out, grad_branch)),
            pack_blocks(matmul_tn(normed_two, grad_gate)),
            pack_blocks(matmul_tn(normed_two, grad_up)),
            pack_blocks(matmul_tn(activated, cotangent)),
        ],
        axis=0,
    )


def shards_any(
    x_in,
    cotangent,
    seq_lengths,
    weights,
    momentum,
    left_stat,
    right_stat,
    left_root,
    right_root,
    vectors,
    vector_sq,
):
    gathered = lax.all_gather(weights.astype(jnp.bfloat16), ("seq", "wt"), axis=0, tiled=True)
    w_in, w_out, w_gate, w_up, w_down = matrices(gathered)
    row_count = x_in.shape[0]
    places = lax.axis_index(("seq", "wt")) * row_count + jnp.arange(row_count, dtype=jnp.int32)
    keep_one, keep_two = keep_masks(places, seq_lengths)
    hidden_in = x_in.astype(jnp.float32)
    scale_one = rms_scale(hidden_in)
    normed = (hidden_in * scale_one * vectors[0]).astype(jnp.bfloat16)
    mixed = matmul(normed, w_in)
    input_gate = mixed[:, :D]
    output_gate = mixed[:, D : 2 * D]
    values = mixed[:, 2 * D :]
    driven = input_gate * values
    carried = from_behind(driven[-2:], ("seq", "wt"), 1)
    extended = jnp.concatenate([carried, driven], axis=0)
    conv_out = (
        vectors[4] * driven
        + vectors[3] * keep_one * extended[1:-1]
        + vectors[2] * keep_two * extended[:-2]
    )
    gated_out = (output_gate * conv_out).astype(jnp.bfloat16)
    middle = hidden_in + matmul(gated_out, w_out)
    scale_two = rms_scale(middle)
    normed_two = (middle * scale_two * vectors[1]).astype(jnp.bfloat16)
    gate_ff = matmul(normed_two, w_gate)
    up_ff = matmul(normed_two, w_up)
    sigmoid_gate = jax.nn.sigmoid(gate_ff)
    silu_value = gate_ff * sigmoid_gate
    activated = (silu_value * up_ff).astype(jnp.bfloat16)
    out_act = (middle + matmul(activated, w_down)).astype(jnp.bfloat16)
    grad_act = matmul_nt(cotangent, w_down)
    grad_gate = (grad_act * up_ff * sigmoid_gate * (1.0 + gate_ff * (1.0 - sigmoid_gate))).astype(
        jnp.bfloat16
    )
    grad_up = (grad_act * silu_value).astype(jnp.bfloat16)
    grad_normed_two = matmul_nt(grad_gate, w_gate) + matmul_nt(grad_up, w_up)
    gain_two_grad, middle_term = norm_back(middle, scale_two, vectors[1], grad_normed_two)
    grad_middle = cotangent.astype(jnp.float32) + middle_term
    grad_branch = grad_middle.astype(jnp.bfloat16)
    grad_gated = matmul_nt(grad_branch, w_out)
    grad_output_gate = grad_gated * conv_out
    grad_conv = grad_gated * output_gate
    early_one = keep_one * grad_conv
    early_two = keep_two * grad_conv
    tap_zero = jnp.sum(early_two * extended[:-2], axis=0)
    tap_first = jnp.sum(early_one * extended[1:-1], axis=0)
    tap_second = jnp.sum(grad_conv * driven, axis=0)
    sent_back = jnp.stack(
        [vectors[2] * early_two[0], vectors[3] * early_one[0] + vectors[2] * early_two[1]], axis=0
    )
    from_after = from_behind(sent_back, ("seq", "wt"), -1)
    zero_rows = jnp.zeros((2, D), jnp.float32)
    grad_driven = vectors[4] * grad_conv
    grad_driven = grad_driven + vectors[3] * jnp.concatenate([early_one[1:], zero_rows[:1]], axis=0)
    grad_driven = grad_driven + vectors[2] * jnp.concatenate([early_two[2:], zero_rows], axis=0)
    grad_driven = grad_driven + jnp.concatenate(
        [jnp.zeros((row_count - 2, D), jnp.float32), from_after], axis=0
    )
    grad_mixed = jnp.concatenate(
        [grad_driven * values, grad_output_gate, grad_driven * input_gate], axis=1
    ).astype(jnp.bfloat16)
    grad_normed = matmul_nt(grad_mixed, w_in)
    gain_one_grad, input_term = norm_back(hidden_in, scale_one, vectors[0], grad_normed)
    in_grad = grad_middle + input_term
    paired = (
        lax.all_gather(normed, "wt", axis=0, tiled=True),
        lax.all_gather(grad_mixed, "wt", axis=0, tiled=True),
        lax.all_gather(gated_out, "wt", axis=0, tiled=True),
        lax.all_gather(grad_branch, "wt", axis=0, tiled=True),
        lax.all_gather(normed_two, "wt", axis=0, tiled=True),
        lax.all_gather(grad_gate, "wt", axis=0, tiled=True),
        lax.all_gather(grad_up, "wt", axis=0, tiled=True),
        lax.all_gather(activated, "wt", axis=0, tiled=True),
        lax.all_gather(cotangent, "wt", axis=0, tiled=True),
    )
    pair_grads = weight_grads(paired)
    seq_count = lax.axis_size("seq")
    core_count = lax.axis_size("wt")
    owned_count = pair_grads.shape[0] // (seq_count * core_count)
    arranged = pair_grads.reshape(seq_count, core_count, owned_count, BS * BS)
    mine = lax.dynamic_index_in_dim(arranged, lax.axis_index("wt"), 1, keepdims=False).reshape(
        seq_count * owned_count, BS * BS
    )
    summed_flat = lax.psum_scatter(mine, "seq", scatter_dimension=0, tiled=True)
    vector_part = jnp.stack([gain_one_grad, gain_two_grad, tap_zero, tap_first, tap_second], axis=0)
    local_count = summed_flat.shape[0]
    summed = summed_flat.reshape(local_count, BS, BS)
    left_blocks = left_stat.reshape(local_count, BS, BS)
    right_blocks = right_stat.reshape(local_count, BS, BS)
    momentum_blocks = momentum.reshape(local_count, BS, BS)
    left_factor = left_root.reshape(local_count, BS, BS)
    right_factor = right_root.reshape(local_count, BS, BS)
    new_left = DECAY * left_blocks + (1.0 - DECAY) * jnp.einsum(
        "kij,klj->kil", summed, summed, precision=HIGHEST
    )
    new_right = DECAY * right_blocks + (1.0 - DECAY) * jnp.einsum(
        "kji,kjl->kil", summed, summed, precision=HIGHEST
    )
    new_momentum = MOMENT * momentum_blocks + summed
    precond = jnp.einsum("kij,kjl->kil", left_factor, new_momentum, precision=HIGHEST)
    precond = jnp.einsum("kij,kjl->kil", precond, right_factor, precision=HIGHEST)
    precond_flat = precond.reshape(local_count, BS * BS)
    square = jnp.sum(precond_flat * precond_flat, axis=1)
    in_end, out_end, gate_end, up_end = block_bounds()
    block_ids = lax.axis_index(("seq", "wt")) * local_count + jnp.arange(
        local_count, dtype=jnp.int32
    )
    kind_index = (
        (block_ids >= in_end).astype(jnp.int32)
        + (block_ids >= out_end).astype(jnp.int32)
        + (block_ids >= gate_end).astype(jnp.int32)
        + (block_ids >= up_end).astype(jnp.int32)
    )
    one_hot = (kind_index[:, None] == jnp.arange(5, dtype=jnp.int32)[None, :]).astype(jnp.float32)
    kind_part = jnp.sum(one_hot * square[:, None], axis=0)
    vector_grads, kind_sum = lax.psum((vector_part, kind_part), ("seq", "wt"))
    kind_total = jnp.array(
        [in_end, out_end - in_end, gate_end - out_end, up_end - gate_end, BLOCKS - up_end],
        jnp.float32,
    ) * (BS * BS)
    kind_scale = lax.rsqrt(kind_sum / kind_total + MEAN_EPS)
    block_scale = jnp.sum(one_hot * kind_scale[None, :], axis=1)
    new_weights = weights - RATE * block_scale[:, None] * precond_flat
    weight_copy = new_weights.astype(jnp.bfloat16)
    new_vector_sq = DECAY * vector_sq + (1.0 - DECAY) * vector_grads * vector_grads
    new_vectors = vectors - VEC_RATE * vector_grads * lax.rsqrt(new_vector_sq)
    flat_shape = (local_count, BS * BS)
    return (
        out_act,
        in_grad,
        new_weights,
        weight_copy,
        new_momentum.reshape(flat_shape),
        new_left.reshape(flat_shape),
        new_right.reshape(flat_shape),
        vector_grads,
        new_vector_sq,
        new_vectors,
    )


Z, Y, X = 4, 2, 2
CHIPS, CORES = Z * Y * X, 2
PLANE = Y * X
HALF = BS // 2
SWAP = [(0, 1), (1, 0)]


def chip(z, y, x):
    return (z * Y + y) * X + x


def plane_route(pairs):
    return [(chip(a, y, x), chip(b, y, x)) for a, b in pairs for y in range(Y) for x in range(X)]


ACROSS_X = [(i, i ^ 1) for i in range(CHIPS)]
ACROSS_Y = [(i, i ^ 2) for i in range(CHIPS)]


def send(block, route):
    return lax.ppermute(block, "seq", route)


def to_sibling(block):
    return lax.ppermute(block, "wt", SWAP)


def quad_bounds():
    return tuple(b // 4 for b in block_bounds())


def pick(place, options):
    out = options[0]
    for i, option in enumerate(options[1:], 1):
        out = jnp.where(place == i, option, out)
    return out


def take(array, index, axis):
    return lax.dynamic_index_in_dim(array, index, axis, keepdims=False)


QUAD = 4 * BS
LANES = 128
KINDS = 5
VMEM_LIMIT = 24 * 1024 * 1024
VMEM_MOST = 50 * 1024 * 1024
VMEM_ALL = 62 * 1024 * 1024


def busy(micros):
    return pl.CostEstimate(flops=0, bytes_accessed=int(micros * 3e6), transcendentals=0)


def lane_ids(rows):
    return lax.broadcasted_iota(jnp.int32, (rows, LANES), 1)


def strided(ref, part, start, count, stride):
    return ref[part, pl.ds(start, count, stride=stride), :]


def each(count, body, unroll):
    def step(n, carry):
        body(n)
        return carry

    lax.fori_loop(0, count, step, 0, unroll=unroll)


def columns(flat_ref, cols_ref):
    for k in range(cols_ref.shape[0]):
        cols_ref[k] = flat_ref[:, pl.ds(k * LANES, LANES)]


def cols_to_wide(cols_ref, wide_ref, count):
    low = lane_ids(count) < BS
    for k in range(BS // 2):
        parts = [strided(cols_ref, k, b, count, 4) for b in range(4)]
        turned = [pltpu.roll(p, BS, 1) for p in parts]
        for t in range(2):
            a, b = 2 * t, 2 * t + 1
            even = jnp.where(low, parts[a], turned[b])
            odd = jnp.where(low, turned[a], parts[b])
            wide_ref[t, pl.ds(2 * k, count, stride=BS), :] = even
            wide_ref[t, pl.ds(2 * k + 1, count, stride=BS), :] = odd


def wide_to_cols(wide_ref, cols_ref, count):
    low = lane_ids(count) < BS
    for k in range(BS // 2):
        for t in range(2):
            even = strided(wide_ref, t, 2 * k, count, BS)
            odd = strided(wide_ref, t, 2 * k + 1, count, BS)
            a, b = 2 * t, 2 * t + 1
            cols_ref[k, pl.ds(a, count, stride=4), :] = jnp.where(
                low, even, pltpu.roll(odd, BS, 1)
            )
            cols_ref[k, pl.ds(b, count, stride=4), :] = jnp.where(
                low, pltpu.roll(even, BS, 1), odd
            )


def join(wide_ref, rows):
    return jnp.concatenate([wide_ref[0, rows, :], wide_ref[1, rows, :]], axis=1)


def cut(wide_ref, rows, value):
    wide_ref[0, rows, :] = value[:, :LANES].astype(wide_ref.dtype)
    wide_ref[1, rows, :] = value[:, LANES:].astype(wide_ref.dtype)


def cols_shape(flat):
    return (flat.shape[1] // LANES, flat.shape[0], LANES)


def kind_of(quad):
    kind = jnp.int32(0)
    for bound in quad_bounds():
        kind = kind + (quad >= bound).astype(jnp.int32)
    return kind


def is_row_kind(kind):
    return (kind == 1) | (kind == 4)


def split_weights_kernel(place_ref, flat_ref, kept_ref, sent_ref, cols_ref, col_ref, row_ref):
    count = flat_ref.shape[0] // 4
    core, first = place_ref[0], place_ref[1]
    group = lane_ids(count) // HALF
    low = group < 2
    columns(flat_ref, cols_ref)
    for k in range(BS // 2):
        parts = [strided(cols_ref, k, b, count, 4) for b in range(4)]
        rolls = [[p] + [pltpu.roll(p, s * HALF, 1) for s in (1, 2, 3)] for p in parts]
        for odd in range(2):
            r = 2 * k + odd
            for half in range(2):
                g = 2 * odd + half
                out = rolls[0][(0 - g) % 4]
                for b in range(1, 4):
                    out = jnp.where(group == b, rolls[b][(b - g) % 4], out)
                col_ref[half, pl.ds(r, count, stride=BS), :] = out
            for t in range(2):
                a, b = 2 * t, 2 * t + 1
                if odd:
                    out = jnp.where(low, rolls[a][2], parts[b])
                else:
                    out = jnp.where(low, parts[a], rolls[b][2])
                row_ref[r // HALF, pl.ds(t * HALF + r % HALF, count, stride=BS), :] = out

    def finish(q, carry):
        rows = pl.ds(pl.multiple_of(q * BS, BS), BS)
        by_row = is_row_kind(kind_of(first + q))
        for ref, half in ((kept_ref, core), (sent_ref, 1 - core)):
            value = jnp.where(by_row, row_ref[half, rows, :], col_ref[half, rows, :])
            ref[q] = value.astype(ref.dtype)
        return carry

    lax.fori_loop(0, count, finish, 0)


def whole(n):
    return [pl.BlockSpec(memory_space=pltpu.VMEM)] * n


SCALARS = pl.BlockSpec(memory_space=pltpu.SMEM)


def split_weights(core, first, weights):
    count = weights.shape[0] // 4
    quads = jax.ShapeDtypeStruct((count, BS, LANES), jnp.bfloat16)
    return pl.pallas_call(
        split_weights_kernel,
        out_shape=(quads, quads),
        in_specs=[SCALARS] + whole(1),
        out_specs=tuple(whole(2)),
        scratch_shapes=[pltpu.VMEM(cols_shape(weights), jnp.float32)]
        + [pltpu.VMEM((2, count * BS, LANES), jnp.float32)] * 2,
        compiler_params=pltpu.CompilerParams(vmem_limit_bytes=VMEM_LIMIT),
        cost_estimate=busy(8),
    )(jnp.stack([core, first]), weights)


def widen_kernel(momentum_ref, left_ref, right_ref, mom_ref, lw_ref, rw_ref, cols_ref, wide_ref):
    count = momentum_ref.shape[0] // 4
    sources = ((momentum_ref, mom_ref, MOMENT), (left_ref, lw_ref, 1.0), (right_ref, rw_ref, 1.0))
    for src, dst, scale in sources:
        columns(src, cols_ref)
        cols_to_wide(cols_ref, wide_ref, count)
        dst[...] = (scale * wide_ref[...]).astype(dst.dtype)


def widen(momentum, left_root, right_root):
    shape = (2, momentum.shape[0] // 4 * BS, LANES)
    return pl.pallas_call(
        widen_kernel,
        out_shape=(
            jax.ShapeDtypeStruct(shape, jnp.bfloat16),
            jax.ShapeDtypeStruct(shape, jnp.bfloat16),
            jax.ShapeDtypeStruct(shape, jnp.bfloat16),
        ),
        in_specs=whole(3),
        out_specs=tuple(whole(3)),
        scratch_shapes=[
            pltpu.VMEM(cols_shape(momentum), jnp.float32),
            pltpu.VMEM(shape, jnp.float32),
        ],
        compiler_params=pltpu.CompilerParams(vmem_limit_bytes=VMEM_LIMIT),
        cost_estimate=busy(11),
    )(momentum, left_root, right_root)


def diagonal(wide, mask):
    return jnp.where(mask, jnp.concatenate([wide] * 4, axis=0), jnp.zeros((), wide.dtype))


def diagonal_mask():
    rows = lax.broadcasted_iota(jnp.int32, (QUAD, QUAD), 0) // BS
    cols = lax.broadcasted_iota(jnp.int32, (QUAD, QUAD), 1) // BS
    return rows == cols


def wide_sum(kept, got, core, by_row):
    first = jnp.where(core == 0, kept, got)
    second = jnp.where(core == 0, got, kept)
    group = lane_ids(BS) // HALF
    tiles = []
    for t in range(2):
        pieces = (
            (first, 2 * t, 0),
            (second, 2 * t, 1),
            (first, 2 * t + 1, 2),
            (second, 2 * t + 1, 3),
        )
        out = None
        for value, source, target in pieces:
            shift = (target - source) * HALF % LANES
            moved = value if shift == 0 else pltpu.roll(value, shift, 1)
            out = moved if out is None else jnp.where(group == target, moved, out)
        rows = slice(t * HALF, (t + 1) * HALF)
        tiles.append(
            jnp.where(by_row, jnp.concatenate([first[rows], second[rows]], axis=0), out)
        )
    return jnp.concatenate(tiles, axis=1)


def step_kernel(
    place_ref, kept_ref, got_ref, mom_ref, lw_ref, rw_ref, flat_ref,
    new_mom_ref, precond_ref, wide_ref, kind_ref, cols_ref, sum_ref, step_ref,
):
    count = kept_ref.shape[0]
    core, first = place_ref[0], place_ref[1]
    mask = diagonal_mask()
    kind_ref[...] = jnp.zeros_like(kind_ref)

    def one(q, carry):
        rows = pl.ds(pl.multiple_of(q * BS, BS), BS)
        kind = kind_of(first + q)
        total = wide_sum(
            kept_ref[q].astype(jnp.float32), got_ref[q].astype(jnp.float32), core, is_row_kind(kind)
        )
        cut(sum_ref, rows, total)
        wide_ref[rows, :] = total.astype(jnp.bfloat16)
        moment = (join(mom_ref, rows).astype(jnp.float32) + total).astype(jnp.bfloat16)
        inner = jnp.dot(
            join(lw_ref, rows), diagonal(moment, mask), preferred_element_type=jnp.float32
        ).astype(jnp.bfloat16)
        step = jnp.dot(
            inner, diagonal(join(rw_ref, rows), mask), preferred_element_type=jnp.float32
        )
        cut(step_ref, rows, step)
        square = jnp.sum(step * step, axis=0, keepdims=True)
        kind_ref[pl.ds(kind, 1), :] += square[:, :LANES] + square[:, LANES:]
        return carry

    lax.fori_loop(0, count, one, 0, unroll=5)

    wide_to_cols(sum_ref, cols_ref, count)
    for k in range(cols_ref.shape[0]):
        lanes = pl.ds(k * LANES, LANES)
        new_mom_ref[:, lanes] = MOMENT * flat_ref[:, lanes] + cols_ref[k]
    wide_to_cols(step_ref, cols_ref, count)
    for k in range(cols_ref.shape[0]):
        precond_ref[:, pl.ds(k * LANES, LANES)] = cols_ref[k]


def step_blocks(core, first, kept, got, mom_wide, left_wide, right_wide, momentum):
    count = kept.shape[0]
    rows = count * BS
    flat = jax.ShapeDtypeStruct(momentum.shape, jnp.float32)
    return pl.pallas_call(
        step_kernel,
        out_shape=(
            flat,
            flat,
            jax.ShapeDtypeStruct((rows, QUAD), jnp.bfloat16),
            jax.ShapeDtypeStruct((8, LANES), jnp.float32),
        ),
        in_specs=[SCALARS] + whole(6),
        out_specs=tuple(whole(4)),
        scratch_shapes=[pltpu.VMEM(cols_shape(momentum), jnp.float32)]
        + [pltpu.VMEM((2, rows, LANES), jnp.float32)] * 2,
        compiler_params=pltpu.CompilerParams(vmem_limit_bytes=VMEM_LIMIT),
        cost_estimate=busy(13),
    )(jnp.stack([core, first]), kept, got, mom_wide, left_wide, right_wide, momentum)


def stat_kernel(turned, wide_ref, old_ref, new_ref, cols_ref, gram_ref):
    count = wide_ref.shape[0] // BS
    mask = diagonal_mask()

    def one(q, carry):
        rows = pl.ds(pl.multiple_of(q * BS, BS), BS)
        total = wide_ref[rows, :]
        if turned:
            gram = lax.dot_general(
                total, total, (((0,), (0,)), ((), ())), preferred_element_type=jnp.float32
            )
            gram = jnp.where(mask, gram, 0.0)
            gram = gram[:BS] + gram[BS : 2 * BS] + gram[2 * BS : 3 * BS] + gram[3 * BS :]
        else:
            gram = lax.dot_general(
                total, diagonal(total, mask), (((1,), (1,)), ((), ())),
                preferred_element_type=jnp.float32,
            )
        cut(gram_ref, rows, gram)
        return carry

    lax.fori_loop(0, count, one, 0, unroll=5)
    wide_to_cols(gram_ref, cols_ref, count)
    for k in range(cols_ref.shape[0]):
        lanes = pl.ds(k * LANES, LANES)
        new_ref[:, lanes] = DECAY * old_ref[:, lanes] + (1.0 - DECAY) * cols_ref[k]


def stat_blocks(wide, stat, turned):
    return pl.pallas_call(
        functools.partial(stat_kernel, turned),
        out_shape=jax.ShapeDtypeStruct(stat.shape, jnp.float32),
        in_specs=whole(2),
        out_specs=whole(1)[0],
        scratch_shapes=[
            pltpu.VMEM(cols_shape(stat), jnp.float32),
            pltpu.VMEM((2, wide.shape[0], LANES), jnp.float32),
        ],
        compiler_params=pltpu.CompilerParams(vmem_limit_bytes=VMEM_LIMIT),
        cost_estimate=busy(6),
    )(wide, stat)


TILE = 768
QUADS_WIDE = TILE // LANES
OUT_TILE = 256


def f32_dot(a, b, dims=((1,), (0,))):
    return lax.dot_general(a, b, (dims, ((), ())), preferred_element_type=jnp.float32)


def nt_dot(a, b):
    return f32_dot(a, b, ((1,), (1,)))


def col_tile(ref, rows, per_row, j, width=2):
    parts = [
        jnp.concatenate([ref[i * per_row + j + d] for i in range(rows)], axis=0)
        for d in range(width)
    ]
    return jnp.concatenate(parts, axis=1)


def col_rows(ref, first, rows, per_row):
    return jnp.concatenate(
        [
            jnp.concatenate([ref[(first + i) * per_row + j] for j in range(per_row)], axis=1)
            for i in range(rows)
        ],
        axis=0,
    )


def row_rows(ref, first, rows, per_row):
    return jnp.concatenate(
        [
            jnp.concatenate(
                [
                    ref[(first + i) * per_row + j, h * HALF : (h + 1) * HALF]
                    for j in range(per_row)
                    for h in range(2)
                ],
                axis=1,
            )
            for i in range(rows)
        ],
        axis=0,
    )


def row_tile(ref, rows, per_row, j):
    parts = [
        jnp.concatenate(
            [ref[i * per_row + j, h * HALF : (h + 1) * HALF] for i in range(rows)], axis=0
        )
        for h in range(2)
    ]
    return jnp.concatenate(parts, axis=1)


def put_col_tile(ref, value, rows, per_row, j, width=2):
    value = value.astype(ref.dtype)
    for i in range(rows):
        for d in range(width):
            ref[i * per_row + j + d] = value[i * BS : (i + 1) * BS, d * LANES : (d + 1) * LANES]


def put_row_rows(ref, value, first, rows, per_row):
    value = value.astype(ref.dtype)
    for i in range(rows):
        for j in range(per_row):
            for h in range(2):
                part = value[
                    i * HALF : (i + 1) * HALF, (2 * j + h) * LANES : (2 * j + h + 1) * LANES
                ]
                ref[(first + i) * per_row + j, h * HALF : (h + 1) * HALF] = part


def wide_at(n, width):
    at = n * width
    return pl.ds(at if isinstance(n, int) else pl.multiple_of(at, width), width)


def put_part(own_ref, other_ref, cols, value):
    rows = own_ref.shape[0]
    own_ref[:, cols] = value[:rows]
    other_ref[:, cols] = value[rows:].astype(other_ref.dtype)


def parts(rows):
    return [shape((rows // 2, D), jnp.float32), shape((rows // 2, D), jnp.bfloat16)]


def call(kernel, outs, ins, scratch=(), micros=0, any_in=(), any_out=(), limit=VMEM_MOST, aliases=None):
    def specs(count, far):
        return [
            pl.BlockSpec(memory_space=pltpu.HBM if i in far else pltpu.VMEM) for i in range(count)
        ]

    return pl.pallas_call(
        kernel,
        out_shape=tuple(jax.ShapeDtypeStruct(o.shape, o.dtype) for o in outs),
        in_specs=specs(len(ins), any_in),
        out_specs=tuple(specs(len(outs), any_out)),
        scratch_shapes=list(scratch),
        input_output_aliases=aliases or {},
        compiler_params=pltpu.CompilerParams(vmem_limit_bytes=limit),
        cost_estimate=busy(micros),
    )(*ins)


def shape(dims, dtype):
    return jax.ShapeDtypeStruct(dims, dtype)


IN_ROWS = D // BS
IN_COLS = 3 * D // 256
OUT_COLS = D // 256
FF_COLS = FF // 256
DOWN_ROWS = FF // BS
FF_HALF = FF // 2
D_HALF = D // 2


def fetch(quads_ref, first, count, into, sem):
    return pltpu.make_async_copy(quads_ref.at[pl.ds(first, count)], into, sem)


def mix_kernel(normed_ref, quads_ref, mixed_ref, w_ref, sems):
    step = 4 * IN_COLS
    copies = [
        fetch(quads_ref, g * step, step, w_ref.at[pl.ds(g * step, step)], sems.at[g])
        for g in range(IN_ROWS // 4)
    ]
    for c in copies:
        c.start()
    for c in copies:
        c.wait()

    def tile(t, carry):
        cols = pl.ds(pl.multiple_of(t * TILE, TILE), TILE)
        mixed_ref[:, cols] = f32_dot(
            normed_ref[...], col_tile(w_ref, IN_ROWS, IN_COLS, QUADS_WIDE * t, QUADS_WIDE)
        )
        return carry

    lax.fori_loop(0, IN_COLS // QUADS_WIDE, tile, 0)


def mix(normed, quads):
    rows = normed.shape[0]
    return call(
        mix_kernel,
        [shape((rows, 3 * D_HALF), jnp.float32)],
        [normed, quads],
        [
            pltpu.VMEM((IN_ROWS * IN_COLS, BS, LANES), jnp.bfloat16),
            pltpu.SemaphoreType.DMA((IN_ROWS // 4,)),
        ],
        micros=7,
        any_in=(1,),
    )[0]


def shift_down(value, halo, distance):
    moved = pltpu.roll(value, distance, 0)
    row = lax.broadcasted_iota(jnp.int32, value.shape, 0)
    out = jnp.where(row == 0, halo[2 - distance : 3 - distance], moved)
    if distance == 2:
        out = jnp.where(row == 1, halo[1:2], out)
    return out


def shift_up(value, distance):
    count = value.shape[0]
    moved = pltpu.roll(value, count - distance, 0)
    row = lax.broadcasted_iota(jnp.int32, value.shape, 0)
    return jnp.where(row < count - distance, moved, 0.0)


def conv_kernel(
    mixed_ref, halo_ref, keep_ref, taps_ref, quads_ref,
    conv_ref, gated_ref, own_ref, other_ref,
    w_ref, sem,
):
    first = 3 * IN_ROWS * OUT_COLS
    copy = fetch(quads_ref, first, IN_ROWS * OUT_COLS, w_ref, sem)
    copy.start()
    rows = mixed_ref.shape[0] // 2

    def segment(s):
        at = wide_at(s, rows)
        driven = mixed_ref[at, :D_HALF] * mixed_ref[at, 2 * D_HALF :]
        halo = halo_ref[s]
        conv = (
            taps_ref[2:3] * driven
            + taps_ref[1:2] * keep_ref[at, 0:1] * shift_down(driven, halo, 1)
            + taps_ref[0:1] * keep_ref[at, 1:2] * shift_down(driven, halo, 2)
        )
        conv_ref[at, :] = conv
        gated_ref[at, :] = (mixed_ref[at, D_HALF : 2 * D_HALF] * conv).astype(jnp.bfloat16)

    for s in range(2):
        segment(s)
    copy.wait()

    def tile(j):
        value = f32_dot(gated_ref[...], row_tile(w_ref, IN_ROWS, OUT_COLS, j))
        put_part(own_ref, other_ref, wide_at(j, OUT_TILE), value)

    for j in range(OUT_COLS):
        tile(j)


def conv_forward(mixed, halos, keep, taps, quads):
    rows = mixed.shape[0]
    return call(
        conv_kernel,
        [
            shape((rows, D_HALF), jnp.float32),
            shape((rows, D_HALF), jnp.bfloat16),
        ]
        + parts(rows),
        [mixed, halos, keep, taps, quads],
        [
            pltpu.VMEM((IN_ROWS * OUT_COLS, BS, LANES), jnp.bfloat16),
            pltpu.SemaphoreType.DMA(()),
        ],
        micros=5,
        any_in=(4,),
    )


def join_rows(ref, mine_ref, theirs_ref):
    rows = mine_ref.shape[0]
    ref[:rows] = mine_ref[...]
    ref[rows:] = theirs_ref[...]


BACK_ROWS = 8


def ff_kernel(
    mine_ref, theirs_ref, cot_ref, quads_ref,
    act_ref, gg_ref, gu_ref, own_ref, other_ref,
    gate_ref, up_ref, down_ref, normed_ref, sems,
):
    _, out_end, gate_end, up_end = quad_bounds()
    per = IN_ROWS * FF_COLS
    copies = [
        fetch(quads_ref, first, per, ref, sems.at[n])
        for n, (first, ref) in enumerate(
            ((out_end, gate_ref), (gate_end, up_ref), (up_end, down_ref))
        )
    ]
    for c in copies:
        c.start()
    step = TILE // HALF
    join_rows(normed_ref, mine_ref, theirs_ref)
    def tile(t, wait):
        cols = pl.ds(pl.multiple_of(t * TILE, TILE), TILE)
        if wait:
            copies[0].wait()
        gate = f32_dot(
            normed_ref[...], col_tile(gate_ref, IN_ROWS, FF_COLS, QUADS_WIDE * t, QUADS_WIDE)
        )
        if wait:
            copies[1].wait()
        up = f32_dot(
            normed_ref[...], col_tile(up_ref, IN_ROWS, FF_COLS, QUADS_WIDE * t, QUADS_WIDE)
        )
        if wait:
            copies[2].wait()
        grad_act = nt_dot(cot_ref[...], row_rows(down_ref, step * t, step, OUT_COLS))
        sig = jax.nn.sigmoid(gate)
        silu = gate * sig
        act_ref[:, cols] = (silu * up).astype(jnp.bfloat16)
        gg_ref[:, cols] = (grad_act * up * sig * (1.0 + gate * (1.0 - sig))).astype(jnp.bfloat16)
        gu_ref[:, cols] = (grad_act * silu).astype(jnp.bfloat16)

    tile(0, True)

    def later(t, carry):
        tile(t, False)
        return carry

    lax.fori_loop(1, FF_HALF // TILE, later, 0)

    def back(g, carry):
        value = nt_dot(gg_ref[...], col_rows(gate_ref, BACK_ROWS * g, BACK_ROWS, FF_COLS))
        value = value + nt_dot(
            gu_ref[...], col_rows(up_ref, BACK_ROWS * g, BACK_ROWS, FF_COLS)
        )
        wide = BACK_ROWS * BS
        put_part(own_ref, other_ref, pl.ds(pl.multiple_of(g * wide, wide), wide), value)
        return carry

    lax.fori_loop(0, IN_ROWS // BACK_ROWS, back, 0)


def ff_pass(mine, theirs, cot, quads):
    rows = cot.shape[0]
    wide = shape((rows, FF_HALF), jnp.bfloat16)
    weights = pltpu.VMEM((IN_ROWS * FF_COLS, BS, LANES), jnp.bfloat16)
    return call(
        ff_kernel,
        [wide] * 3 + parts(rows),
        [mine, theirs, cot, quads],
        [weights] * 3 + [pltpu.VMEM(cot.shape, cot.dtype), pltpu.SemaphoreType.DMA((3,))],
        micros=22,
        any_in=(3,),
    )


DOWN_FIRST = 2


def down_tiles(act_ref, cot_ref, out_ref, tiles):
    step = TILE // HALF
    for n, t in enumerate(tiles):
        cols = slice(t * TILE, (t + 1) * TILE)
        put_row_rows(
            out_ref, f32_dot(act_ref[:, cols].T, cot_ref[...]), step * n, step, OUT_COLS
        )


def down_first_kernel(act_ref, cot_ref, near_ref, head_ref, ddown_ref, sem):
    down_tiles(act_ref, cot_ref, ddown_ref, range(DOWN_FIRST))
    behind = head_ref.shape[0]
    count = ddown_ref.shape[0] - behind
    move = pltpu.make_async_copy(
        ddown_ref.at[pl.ds(behind, count)], near_ref.at[pl.ds(PER_PLANE, count)], sem
    )
    move.start()
    head_ref[...] = ddown_ref[:behind]
    move.wait()


def down_last_kernel(
    normed_ref, act_ref, gg_ref, cot_ref, given_ref, near_ref, dgate_ref, ddown_ref, sem
):
    down_tiles(act_ref, cot_ref, ddown_ref, range(DOWN_FIRST, FF_HALF // TILE))
    count = ddown_ref.shape[0]
    move = pltpu.make_async_copy(
        ddown_ref, near_ref.at[pl.ds(2 * PER_PLANE - count, count)], sem
    )
    move.start()
    turned = normed_ref[:, : 2 * BS].T
    ahead = dgate_ref.shape[0] - FF_COLS
    first = f32_dot(turned[:BS], gg_ref[...]).astype(jnp.bfloat16)
    second = f32_dot(turned[BS:], gg_ref[:, : ahead * LANES]).astype(jnp.bfloat16)
    for j in range(FF_COLS):
        dgate_ref[j] = first[:, j * LANES : (j + 1) * LANES]
    for j in range(ahead):
        dgate_ref[FF_COLS + j] = second[:, j * LANES : (j + 1) * LANES]
    move.wait()


PER_PLANE = BLOCKS // 4 // Z
DOWN_TILE = TILE // HALF * OUT_COLS


def down_first(act, cot):
    return call(
        down_first_kernel,
        [
            shape((2 * PER_PLANE, BS, LANES), jnp.bfloat16),
            shape((3 * PER_PLANE - quad_bounds()[3], BS, LANES), jnp.bfloat16),
        ],
        [act, cot],
        [
            pltpu.VMEM((DOWN_FIRST * DOWN_TILE, BS, LANES), jnp.bfloat16),
            pltpu.SemaphoreType.DMA(()),
        ],
        micros=5,
        any_out=(0,),
    )


def down_last(normed, act, gg, cot, given):
    rest = FF_HALF // TILE - DOWN_FIRST
    return call(
        down_last_kernel,
        [
            shape(given.shape, jnp.bfloat16),
            shape((PER_PLANE - quad_bounds()[1], BS, LANES), jnp.bfloat16),
        ],
        [normed, act, gg, cot, given],
        [
            pltpu.VMEM((rest * DOWN_TILE, BS, LANES), jnp.bfloat16),
            pltpu.SemaphoreType.DMA(()),
        ],
        micros=4,
        any_in=(4,),
        any_out=(0,),
        aliases={4: 0},
    )


def ff_grads_kernel(
    normed_ref, gg_ref, gu_ref, ddown_ref, grads_ref, dgate_ref, dup_ref, turned_ref, sems
):
    _, out_end, _, up_end = quad_bounds()
    per = IN_ROWS * FF_COLS
    ahead = PER_PLANE - out_end
    behind = 3 * PER_PLANE - up_end
    pieces = (
        (ddown_ref, 2 * per - ahead, behind),
        (dgate_ref.at[pl.ds(ahead, per - ahead)], 0, per - ahead),
        (dup_ref, per - ahead, per),
    )
    moves = [
        pltpu.make_async_copy(src, grads_ref.at[pl.ds(first, count)], sems.at[n])
        for n, (src, first, count) in enumerate(pieces)
    ]
    moves[0].start()
    turned_ref[...] = normed_ref[...].T

    def weight_grad(grad_ref, out_ref):
        def tile(t, carry):
            cols = pl.ds(pl.multiple_of(t * TILE, TILE), TILE)
            put_col_tile(
                out_ref,
                f32_dot(turned_ref[...], grad_ref[:, cols]),
                IN_ROWS,
                FF_COLS,
                QUADS_WIDE * t,
                QUADS_WIDE,
            )
            return carry

        lax.fori_loop(0, FF_HALF // TILE, tile, 0)

    weight_grad(gg_ref, dgate_ref)
    moves[1].start()
    weight_grad(gu_ref, dup_ref)
    moves[2].start()
    for move in moves:
        move.wait()


def ff_grads(normed, gg, gu, ddown):
    rows = normed.shape[0]
    grads = pltpu.VMEM((IN_ROWS * FF_COLS, BS, LANES), jnp.bfloat16)
    return call(
        ff_grads_kernel,
        [shape((2 * PER_PLANE, BS, LANES), jnp.bfloat16)],
        [normed, gg, gu, ddown],
        [grads] * 2 + [pltpu.VMEM((D, rows), jnp.bfloat16), pltpu.SemaphoreType.DMA((3,))],
        micros=10,
        any_out=(0,),
    )[0]


def ff_out_kernel(act_ref, quads_ref, own_ref, other_ref, down_ref, sem):
    weights = fetch(quads_ref, quad_bounds()[3], DOWN_ROWS * OUT_COLS, down_ref, sem)
    weights.start()
    weights.wait()

    def tile(j):
        value = f32_dot(act_ref[...], row_tile(down_ref, DOWN_ROWS, OUT_COLS, j))
        put_part(own_ref, other_ref, wide_at(j, OUT_TILE), value)

    for j in range(OUT_COLS):
        tile(j)


def ff_out(act, quads):
    rows = act.shape[0]
    return call(
        ff_out_kernel,
        parts(rows),
        [act, quads],
        [
            pltpu.VMEM((IN_ROWS * FF_COLS, BS, LANES), jnp.bfloat16),
            pltpu.SemaphoreType.DMA(()),
        ],
        micros=6,
        any_in=(1,),
    )


def conv_back_kernel(
    mine_ref, theirs_ref, mixed_ref, conv_ref, gated_ref, halo_ref, keep_ref, taps_ref, quads_ref,
    dout_ref, gconv_ref, ggate_ref, heads_ref, tap_ref, w_ref, branch_ref, sem,
):
    join_rows(branch_ref, mine_ref, theirs_ref)
    first = 3 * IN_ROWS * OUT_COLS
    copy = fetch(quads_ref, first, IN_ROWS * OUT_COLS, w_ref, sem)
    copy.start()
    copy.wait()
    rows = mixed_ref.shape[0] // 2
    step = 2 * BS // HALF * 2
    grad = jnp.concatenate(
        [
            nt_dot(branch_ref[...], row_rows(w_ref, g * step, step, OUT_COLS))
            for g in range(IN_ROWS // step)
        ],
        axis=1,
    )
    ggate_ref[...] = (grad * conv_ref[...]).astype(jnp.bfloat16)
    gconv_ref[...] = grad * mixed_ref[:, D_HALF : 2 * D_HALF]
    tap_ref[...] = jnp.zeros_like(tap_ref)

    def segment(s):
        at = wide_at(s, rows)
        driven = mixed_ref[at, :D_HALF] * mixed_ref[at, 2 * D_HALF :]
        halo = halo_ref[s]
        grad_conv = gconv_ref[at, :]
        one = keep_ref[at, 0:1] * grad_conv
        two = keep_ref[at, 1:2] * grad_conv
        terms = (two * shift_down(driven, halo, 2), one * shift_down(driven, halo, 1), grad_conv * driven)
        for n, term in enumerate(terms):
            tap_ref[n : n + 1] += jnp.sum(term, axis=0, keepdims=True)
        heads_ref[s, 0:1] = taps_ref[0:1] * two[0:1]
        heads_ref[s, 1:2] = taps_ref[1:2] * one[0:1] + taps_ref[0:1] * two[1:2]

    each(2, segment, 1)
    put_row_rows(dout_ref, f32_dot(gated_ref[...].T, branch_ref[...]), 0, IN_ROWS, OUT_COLS)


def conv_back(mine, theirs, mixed, conv, gated, halos, keep, taps, quads):
    rows = mixed.shape[0]
    return call(
        conv_back_kernel,
        [
            shape((IN_ROWS * OUT_COLS, BS, LANES), jnp.bfloat16),
            shape((rows, D_HALF), jnp.float32),
            shape((rows, D_HALF), jnp.bfloat16),
            shape((2, 2, D_HALF), jnp.float32),
            shape((3, D_HALF), jnp.float32),
        ],
        [mine, theirs, mixed, conv, gated, halos, keep, taps, quads],
        [
            pltpu.VMEM((IN_ROWS * OUT_COLS, BS, LANES), jnp.bfloat16),
            pltpu.VMEM((rows, D), jnp.bfloat16),
            pltpu.SemaphoreType.DMA(()),
        ],
        micros=7,
        any_in=(8,),
    )


def mix_back_kernel(
    place_ref, gconv_ref, ggate_ref, mixed_ref, normed_ref, tails_ref, keep_ref, taps_ref,
    dout_ref, dgate_ref, given_ref,
    grads_ref, grad_ref, first_ref, second_ref,
    din_ref, turned_ref, stage_ref, sems,
):
    z, far = place_ref[0], place_ref[1] ^ (PLANE - 1)
    count = PER_PLANE // PLANE
    half = count // 2
    corners = (first_ref, second_ref)
    last = z < Z // 2
    fetches = [
        pltpu.make_async_copy(
            given_ref.at[pl.ds(PER_PLANE + far * count + n * half, half)],
            stage_ref.at[n],
            sems.at[0, n],
        )
        for n in range(2)
    ]
    hands = [pltpu.make_async_copy(stage_ref.at[n], corners[n], sems.at[1, n]) for n in range(2)]

    @pl.when(last)
    def _():
        for c in fetches:
            c.start()

    moves = []
    at = IN_ROWS * IN_COLS
    for n, piece in enumerate((dout_ref, dgate_ref)):
        rows = piece.shape[0]
        moves.append(pltpu.make_async_copy(piece, grads_ref.at[pl.ds(at, rows)], sems.at[2, n]))
        at += rows
    for move in moves:
        move.start()
    turned_ref[...] = normed_ref[...].T
    rows = mixed_ref.shape[0] // 2

    def segment(s):
        at = wide_at(s, rows)
        grad_conv = gconv_ref[at, :]
        one = keep_ref[at, 0:1] * grad_conv
        two = keep_ref[at, 1:2] * grad_conv
        grad = (
            taps_ref[2:3] * grad_conv
            + taps_ref[1:2] * shift_up(one, 1)
            + taps_ref[0:1] * shift_up(two, 2)
        )
        row = lax.broadcasted_iota(jnp.int32, grad.shape, 0)
        tail = tails_ref[s]
        grad = grad + jnp.where(
            row == rows - 2, tail[0:1], jnp.where(row == rows - 1, tail[1:2], 0.0)
        )
        grad_ref[at, :D_HALF] = (grad * mixed_ref[at, 2 * D_HALF :]).astype(jnp.bfloat16)
        grad_ref[at, D_HALF : 2 * D_HALF] = ggate_ref[at, :]
        grad_ref[at, 2 * D_HALF :] = (grad * mixed_ref[at, :D_HALF]).astype(jnp.bfloat16)

    each(2, segment, 1)

    @pl.when(last)
    def _():
        for c, d in zip(fetches, hands):
            c.wait()
            d.start()

    def tile(t, carry):
        cols = pl.ds(pl.multiple_of(t * TILE, TILE), TILE)
        put_col_tile(
            din_ref,
            f32_dot(turned_ref[...], grad_ref[:, cols]),
            IN_ROWS,
            IN_COLS,
            QUADS_WIDE * t,
            QUADS_WIDE,
        )
        return carry

    lax.fori_loop(0, IN_COLS // QUADS_WIDE, tile, 0)
    moves.append(
        pltpu.make_async_copy(din_ref, grads_ref.at[pl.ds(0, IN_ROWS * IN_COLS)], sems.at[3, 0])
    )
    moves[-1].start()

    @pl.when(last)
    def _():
        for d in hands:
            d.wait()

    for k in range(PLANE):

        @pl.when(jnp.logical_not(last) & (far == k))
        def _(k=k):
            copies = []
            for n, corner in enumerate(corners):
                low = k * count + n * half
                high = low + half
                start = 0
                for piece in (din_ref, dout_ref, dgate_ref):
                    stop = start + piece.shape[0]
                    a, b = max(low, start), min(high, stop)
                    if a < b:
                        copies.append(
                            pltpu.make_async_copy(
                                piece.at[pl.ds(a - start, b - a)],
                                corner.at[pl.ds(a - low, b - a)],
                                sems.at[4, len(copies)],
                            )
                        )
                    start = stop
            for c in copies:
                c.start()
            for c in copies:
                c.wait()

    for move in moves:
        move.wait()


def mix_back(place, gconv, ggate, mixed, normed, tails, keep, taps, dout, dgate, given):
    rows = mixed.shape[0]
    half = shape((PER_PLANE // PLANE // 2, BS, LANES), jnp.bfloat16)
    ins = [gconv, ggate, mixed, normed, tails, keep, taps, dout, dgate]
    hbm = pl.BlockSpec(memory_space=pltpu.HBM)
    return pl.pallas_call(
        mix_back_kernel,
        out_shape=(
            jax.ShapeDtypeStruct(given.shape, given.dtype),
            shape((rows, 3 * D_HALF), jnp.bfloat16),
            half,
            half,
        ),
        in_specs=[SCALARS] + whole(len(ins)) + [hbm],
        out_specs=(hbm, whole(1)[0], hbm, hbm),
        scratch_shapes=[
            pltpu.VMEM((IN_ROWS * IN_COLS, BS, LANES), jnp.bfloat16),
            pltpu.VMEM((D, rows), jnp.bfloat16),
            pltpu.VMEM((2,) + half.shape, jnp.bfloat16),
            pltpu.SemaphoreType.DMA((5, 4)),
        ],
        input_output_aliases={len(ins) + 1: 0},
        compiler_params=pltpu.CompilerParams(vmem_limit_bytes=VMEM_MOST),
        cost_estimate=busy(8),
    )(place, *ins, given)


def mix_rest_kernel(grad_ref, quads_ref, own_ref, other_ref, w_ref, sem):
    copy = fetch(quads_ref, 0, IN_ROWS * IN_COLS, w_ref, sem)
    copy.start()
    copy.wait()

    def tile(g):
        value = nt_dot(grad_ref[...], col_rows(w_ref, BACK_ROWS * g, BACK_ROWS, IN_COLS))
        put_part(own_ref, other_ref, wide_at(g, BACK_ROWS * BS), value)

    for g in range(IN_ROWS // BACK_ROWS):
        tile(g)


def mix_rest(grad, quads):
    rows = grad.shape[0]
    return call(
        mix_rest_kernel,
        parts(rows),
        [grad, quads],
        [
            pltpu.VMEM((IN_ROWS * IN_COLS, BS, LANES), jnp.bfloat16),
            pltpu.SemaphoreType.DMA(()),
        ],
        micros=5,
        any_in=(1,),
    )


def through(pairs, stage_ref, sems):
    ins = [
        pltpu.make_async_copy(src, stage_ref.at[n], sems.at[0, n])
        for n, (src, _) in enumerate(pairs)
    ]
    outs = [
        pltpu.make_async_copy(stage_ref.at[n], dst, sems.at[1, n])
        for n, (_, dst) in enumerate(pairs)
    ]
    for c in ins:
        c.start()
    for c, d in zip(ins, outs):
        c.wait()
        d.start()
    for d in outs:
        d.wait()


def halves_kernel(a_ref, b_ref, first_ref, second_ref, stage_ref, sems):
    through(((a_ref.at[0], first_ref), (b_ref.at[1], second_ref)), stage_ref, sems)


def halves_of(a, b):
    hbm = pl.BlockSpec(memory_space=pltpu.HBM)
    out = jax.ShapeDtypeStruct(a.shape[1:], a.dtype)
    return pl.pallas_call(
        halves_kernel,
        out_shape=(out, out),
        in_specs=[hbm, hbm],
        out_specs=(hbm, hbm),
        scratch_shapes=[
            pltpu.VMEM((2,) + out.shape, out.dtype),
            pltpu.SemaphoreType.DMA((2, 2)),
        ],
        compiler_params=pltpu.CompilerParams(vmem_limit_bytes=VMEM_ALL),
        cost_estimate=busy(2),
    )(a, b)


def choose_kernel(tables, pairs_at, place_ref, *refs):
    count = len(refs) - 2 - len(tables)
    given, outs, (stage_ref, sems) = list(refs[:count]), refs[count:-2], refs[-2:]
    sources = []
    for pair in pairs_at:
        if pair:
            sources.append([given.pop(0), given.pop(0)])
        else:
            whole_ref = given.pop(0)
            sources.append([whole_ref.at[s] for s in range(CORES)])
    for plane in range(Z):

        @pl.when(place_ref[0] == plane)
        def _(plane=plane):
            pairs = []
            for table, out in zip(tables, outs):
                if table[plane] is not None:
                    for s in range(CORES):
                        pairs.append((sources[table[plane]][s], out.at[s]))
            through(pairs, stage_ref, sems)


def choose(z, sources, tables):
    pairs_at = tuple(isinstance(source, tuple) for source in sources)
    given = [part for s in sources for part in (s if isinstance(s, tuple) else (s,))]
    hbm = pl.BlockSpec(memory_space=pltpu.HBM)
    out = jax.ShapeDtypeStruct(sources[0].shape, sources[0].dtype)
    count = CORES * len(tables)
    return pl.pallas_call(
        functools.partial(choose_kernel, tables, pairs_at),
        out_shape=(out,) * len(tables),
        in_specs=[SCALARS] + [hbm] * len(given),
        out_specs=(hbm,) * len(tables),
        scratch_shapes=[
            pltpu.VMEM((count,) + out.shape[1:], out.dtype),
            pltpu.SemaphoreType.DMA((2, count)),
        ],
        compiler_params=pltpu.CompilerParams(vmem_limit_bytes=VMEM_ALL),
        cost_estimate=busy(2),
    )(z[None], *given)


def place_kernel(places, place_ref, *refs):
    out_ref, stage_ref, sems = refs[-3:]
    plane, here, core = place_ref[0], place_ref[1], place_ref[2]
    pairs = []
    for src, (k, slot) in zip(refs, places):
        if slot is None:
            for s in range(2):
                pairs.append((src.at[s], out_ref.at[plane, here ^ k, s ^ core]))
        else:
            pairs.append((src, out_ref.at[plane, here ^ k, slot ^ core]))
    through(pairs, stage_ref, sems)


def put_plane(plane, here, core, pieces, out):
    hbm = pl.BlockSpec(memory_space=pltpu.HBM)
    places = tuple((piece[1], piece[2] if len(piece) == 3 else None) for piece in pieces)
    given = [piece[0] for piece in pieces]
    half = given[0].shape[-3:]
    count = sum(2 if slot is None else 1 for _, slot in places)
    full = jax.ShapeDtypeStruct((Z, PLANE, CORES) + half, given[0].dtype)
    aliases = {} if out is None else {len(given) + 1: 0}
    given += [] if out is None else [out]
    return pl.pallas_call(
        functools.partial(place_kernel, places),
        out_shape=full,
        in_specs=[SCALARS] + [hbm] * len(given),
        out_specs=hbm,
        scratch_shapes=[
            pltpu.VMEM((count,) + half, full.dtype),
            pltpu.SemaphoreType.DMA((2, count)),
        ],
        input_output_aliases=aliases,
        compiler_params=pltpu.CompilerParams(vmem_limit_bytes=VMEM_ALL),
        cost_estimate=busy(0.5 * count + 1),
    )(jnp.stack([plane, here, core]), *given)


PIECES = (
    ((0, 0), (1, 0), (1, 1), (0, 1)),
    ((1, 0), (1, 1), (0, 0), (0, 1)),
    ((1, 1), (1, 0), (0, 1), (0, 0)),
    ((0, 1), (1, 1), (1, 0), (0, 0)),
)


def pieces_kernel(wanted, place_ref, near_ref, far_ref, *refs):
    outs, (stage_ref, sems) = refs[:-2], refs[-2:]
    z, here = place_ref[0], place_ref[1]
    count = outs[0].shape[0]
    for plane, slots in enumerate(PIECES):

        @pl.when(z == plane)
        def _(slots=slots):
            pairs = []
            for (slot, k), dst in zip(wanted, outs):
                array, part = slots[slot]
                src = (near_ref, far_ref)[array]
                pairs.append((src.at[pl.ds(part * PER_PLANE + (here ^ k) * count, count)], dst))
            through(pairs, stage_ref, sems)


def pieces(wanted, z, here, near, far):
    hbm = pl.BlockSpec(memory_space=pltpu.HBM)
    out = jax.ShapeDtypeStruct((PER_PLANE // PLANE, BS, LANES), near.dtype)
    return pl.pallas_call(
        functools.partial(pieces_kernel, wanted),
        out_shape=(out,) * len(wanted),
        in_specs=[SCALARS, hbm, hbm],
        out_specs=(hbm,) * len(wanted),
        scratch_shapes=[
            pltpu.VMEM((len(wanted),) + out.shape, out.dtype),
            pltpu.SemaphoreType.DMA((2, len(wanted))),
        ],
        compiler_params=pltpu.CompilerParams(vmem_limit_bytes=VMEM_ALL),
        cost_estimate=busy(len(wanted) + 1),
    )(jnp.stack([z, here]), near, far)


def sums_kernel(count, parts, starts, lives, terms, scalars_ref, *refs):
    n = len(starts)
    sources, outs = refs[:n], refs[n : n + len(terms)]
    held_ref, made_ref, in_sems, out_sems = refs[n + len(terms) :]
    spans, at = [], 0
    for size in parts:
        spans.append((at, size))
        at += size

    def fetches(i):
        for c, (at, size) in enumerate(spans):
            yield pltpu.make_async_copy(
                sources[i].at[pl.ds(scalars_ref[starts[i]] + at, size)],
                held_ref.at[i, pl.ds(at, size)],
                in_sems.at[i, c],
            )

    copies = [list(fetches(i)) for i in range(n)]

    def each(c, act):
        for i in range(n):
            if lives[i] is None:
                act(copies[i][c])
            else:
                pl.when(scalars_ref[lives[i]] != 0)(functools.partial(act, copies[i][c]))

    for c in range(len(spans)):
        each(c, lambda copy: copy.start())
    stores = []
    for c, (at, size) in enumerate(spans):
        each(c, lambda copy: copy.wait())

        def one(q, carry):
            values = [held_ref[i, q].astype(jnp.float32) for i in range(n)]
            for k, row in enumerate(terms):
                made = None
                for i, weight in row:
                    term = values[i]
                    if weight is not None:
                        term = jnp.where(scalars_ref[weight] != 0, term, 0.0)
                    made = term if made is None else made + term
                made_ref[k, q] = made.astype(made_ref.dtype)
            return carry

        lax.fori_loop(at, at + size, one, 0, unroll=7)
        for k, out in enumerate(outs):
            span = pl.ds(at, size)
            stores.append(
                pltpu.make_async_copy(made_ref.at[k, span], out.at[span], out_sems.at[k, c])
            )
            stores[-1].start()
    for store in stores:
        store.wait()


def sums(count, sources, weights):
    scalars, starts, lives, terms = [], [], [], []

    def scalar(value):
        scalars.append(jnp.asarray(value, jnp.int32))
        return len(scalars) - 1

    for i, (_, first) in enumerate(sources):
        used = [row[i] for row in weights if not (isinstance(row[i], int) and row[i] == 0)]
        starts.append(scalar(first))
        if any(isinstance(w, int) for w in used):
            lives.append(None)
        else:
            lives.append(
                scalar(functools.reduce(jnp.maximum, [jnp.asarray(w, jnp.int32) for w in used]))
            )
    for row in weights:
        terms.append(
            [
                (i, None if isinstance(w, int) else scalar(w))
                for i, w in enumerate(row)
                if not (isinstance(w, int) and w == 0)
            ]
        )
    unit = count // 5
    parts = (unit, 2 * unit, 2 * unit)
    out = jax.ShapeDtypeStruct((count, BS, LANES), jnp.bfloat16)
    hbm = pl.BlockSpec(memory_space=pltpu.HBM)
    n, k = len(sources), len(weights)
    return pl.pallas_call(
        functools.partial(sums_kernel, count, parts, starts, lives, terms),
        out_shape=[out] * k,
        in_specs=[SCALARS] + [hbm] * n,
        out_specs=[hbm] * k,
        scratch_shapes=[
            pltpu.VMEM((n,) + out.shape, out.dtype),
            pltpu.VMEM((k,) + out.shape, out.dtype),
            pltpu.SemaphoreType.DMA((n, len(parts))),
            pltpu.SemaphoreType.DMA((k, len(parts))),
        ],
        compiler_params=pltpu.CompilerParams(vmem_limit_bytes=VMEM_ALL),
        cost_estimate=busy(0.35 * (n + k) + 1),
    )(jnp.stack(scalars), *[array.reshape(-1, BS, LANES) for array, _ in sources])


def ready_kernel(place_ref, near_ref, far_ref, a_ref, b_ref, *refs):
    outs, (piece_ref, got_ref, sems) = refs[:-3], refs[-3:]
    z, here = place_ref[0], place_ref[1]
    half = a_ref.shape[0]
    count = 2 * half
    gots = [
        pltpu.make_async_copy(ref, got_ref.at[n], sems.at[2, n])
        for n, ref in enumerate((a_ref, b_ref))
    ]
    for c in gots:
        c.start()

    def mend(n, start):
        def one(q, carry):
            value = piece_ref[n, start + q].astype(jnp.float32)
            value = value + got_ref[1 - n, q].astype(jnp.float32)
            piece_ref[n, start + q] = value.astype(piece_ref.dtype)
            return carry

        lax.fori_loop(0, half, one, 0, unroll=7)

    for plane, slots in enumerate(PIECES):

        @pl.when(z == plane)
        def _(slots=slots):
            ins, stores = [], []
            for n, (slot, k) in enumerate(((3, 1), (3, 2), (2, 1), (2, 2), (2, 3))):
                array, part = slots[slot]
                src = (near_ref, far_ref)[array]
                at = pl.ds(part * PER_PLANE + (here ^ k) * count, count)
                ins.append(pltpu.make_async_copy(src.at[at], piece_ref.at[n], sems.at[0, n]))
                stores.append(pltpu.make_async_copy(piece_ref.at[n], outs[n], sems.at[1, n]))
            for c in ins:
                c.start()
            for c in gots:
                c.wait()
            for n in range(2):
                ins[n].wait()
                mend(n, half * (1 - n))
                stores[n].start()
            for n in range(2, len(ins)):
                ins[n].wait()
                stores[n].start()
            for c in stores:
                c.wait()


def ready(z, here, near, far, got):
    hbm = pl.BlockSpec(memory_space=pltpu.HBM)
    half = got[0].shape[0]
    out = jax.ShapeDtypeStruct((2 * half, BS, LANES), near.dtype)
    return pl.pallas_call(
        ready_kernel,
        out_shape=(out,) * 5,
        in_specs=[SCALARS] + [hbm] * 4,
        out_specs=(hbm,) * 5,
        scratch_shapes=[
            pltpu.VMEM((5,) + out.shape, out.dtype),
            pltpu.VMEM((2, half) + out.shape[1:], out.dtype),
            pltpu.SemaphoreType.DMA((3, 5)),
        ],
        compiler_params=pltpu.CompilerParams(vmem_limit_bytes=VMEM_ALL),
        cost_estimate=busy(6),
    )(jnp.stack([z, here]), near, far, *got)


UP = [(0, 1), (1, 2), (2, 3)]
DOWN = [(1, 0), (2, 1), (3, 2)]
SLOT_PLANES = ((0, 1, 2, 3), (1, 2, 0, 3), (2, 1, 3, 0), (3, 2, 1, 0))
INNER = [(1, 0), (2, 3), (0, 1), (3, 2)]


def reverse(pairs):
    return [(b, a) for a, b in pairs]


def together(*values):
    return lax.optimization_barrier(values)


def over_z(block, pairs):
    return send(block, plane_route(pairs))


def over_x(block):
    return send(block, ACROSS_X)


def over_y(block):
    return send(block, ACROSS_Y)


def gather_weights(own, z, here, core, beside):
    up, down, x0, y0 = together(over_z(own, UP), over_z(own, DOWN), over_x(own), over_y(own))
    (one,) = choose(z, (up, down), ((1, 1, 0, 0),))
    up_two, down_two, x1, y1, beside = together(
        over_z(up, UP[1:]), over_z(down, DOWN[:2]), over_x(one), over_y(one), beside
    )
    two, ends = choose(
        z, (up, down, up_two, down_two), ((3, 0, 1, 2), (None, 3, 2, None))
    )

    def corner(x, y):
        first, second = halves_of(y, x)
        return over_x(first), over_y(second)

    f0, f1 = corner(x0, y0), corner(x1, y1)
    ends, x2, y2, f0, f1 = together(over_z(ends, [UP[2], DOWN[0]]), over_x(two), over_y(two), f0, f1)
    three, lent = choose(
        z, (ends, up_two, down_two, f0, f1), ((0, 2, 1, 0), (3, 4, 4, 3))
    )

    def put(slot, pieces, out):
        plane = pick(z, [jnp.int32(row[slot]) for row in SLOT_PLANES])
        return put_plane(plane, here, core, pieces, out)

    out = put(0, ((own, 0), (x0, 1), (y0, 2), (f0[0], 3, 0), (f0[1], 3, 1)), None)
    out = put(1, ((one, 0), (x1, 1), (y1, 2), (f1[0], 3, 0), (f1[1], 3, 1)), out)
    out = put(2, ((two, 0), (x2, 1), (y2, 2)), out)
    x3, y3, f2, out = together(over_x(three), over_y(three), over_z(lent, INNER), out)
    fa, fb = corner(x3, y3)
    out = put(2, ((f2, 3),), out)
    out = put(3, ((three, 0), (x3, 1), (y3, 2)), out)
    fa, fb, out = together(fa, fb, out)
    out = put(3, ((fa, 3, 0), (fb, 3, 1)), out)
    return out.reshape(-1, BS, LANES), beside


def reduce_grads(near, far, corners, z, here, core, meanwhile, operands):
    count = PER_PLANE // PLANE
    half = count // 2

    def flag(test):
        return test.astype(jnp.int32)

    edge = flag((z == 0) | (z == Z - 1))
    inner = 1 - edge
    after = flag(z >= 2)
    part_three = 1 - after
    part_one = z % 2
    part_two = 1 - part_one

    def at(part, k):
        return part * PER_PLANE + (here ^ k) * count

    def of_zero(k):
        return [(near, at(after, k)), (far, at(after, k))]

    def of_two(k):
        return [(near, at(part_two, k)), (far, at(part_two, k))]

    def of_one(k):
        return (far, at(part_one, k))

    got_a, got_b = together(over_x(corners[0]), over_y(corners[1]))
    x3, y3, two_x, two_y, two_far = ready(z, here, near, far, (got_a, got_b))
    x3, y3, far, operands = together(x3, y3, far, operands)
    one_y, zero_x = pieces(((1, 2), (0, 1)), z, here, near, far)
    got_x, got_y, got_z, two_x, two_y, one_y, zero_x = together(
        over_x(x3),
        over_y(y3),
        over_z(two_far, reverse(INNER)),
        over_x(two_x),
        over_y(two_y),
        one_y,
        zero_x,
    )
    f0, f1, three = sums(
        count,
        of_zero(3) + [of_one(3), (got_z, 0), (near, at(part_three, 0)), (got_x, 0), (got_y, 0)],
        [[edge, inner, 0, edge, 0, 0, 0], [0, 0, 1, inner, 0, 0, 0], [0, 0, 0, 0, 1, 1, 1]],
    )
    got_f0, got_f1, got_z, beside = together(
        over_x(f0),
        over_y(f1),
        over_z(three, [(3, 2), (0, 1)]),
        meanwhile(*operands),
    )
    x1, moved = sums(
        count,
        [of_one(1), (got_f1, 0), of_two(0)[1], (two_x, 0), (two_y, 0), (three, 0), (got_z, 0)],
        [[1, 1, 0, 0, 0, 0, 0], [0, 0, edge, edge, edge, inner, inner]],
    )
    x1, moved, got_f0, two_x, two_y = together(x1, moved, got_f0, two_x, two_y)
    (y0,) = sums(count, of_zero(2) + [(got_f0, 0)], [[edge, inner, 1]])
    (two,) = sums(count, [of_two(0)[0], (two_x, 0), (two_y, 0)], [[1, 1, 1]])
    got_x, got_y, got_up, got_down, y0, two = together(
        over_x(x1),
        over_y(one_y),
        over_z(moved, reverse(UP[1:])),
        over_z(moved, reverse(DOWN[:2])),
        y0,
        two,
    )
    low, high = flag(z == 1), flag(z == 2)
    up, down = sums(
        count,
        [of_one(0), (got_x, 0), (got_y, 0), (two, 0), (got_up, 0), (got_down, 0)],
        [
            [1 - low, 1 - low, 1 - low, low, 1, 0],
            [1 - high, 1 - high, 1 - high, high, 0, 1],
        ],
    )
    got = together(
        over_x(zero_x), over_y(y0), over_z(up, reverse(UP)), over_z(down, reverse(DOWN))
    )
    sources, rows = [], []
    for n, first in enumerate((core * half, (1 - core) * half)):
        base = at(after, 0) + first
        sources += [(near, base), (far, base)] + [(value, first) for value in got]
        row = [edge, inner, 1, 1, 1, 1]
        rows.append([0] * 6 * n + row + [0] * 6 * (1 - n))
    return *sums(half, sources, rows), beside


def phase(value, bits):
    a, b = bits
    got = [send(value, [(i, i ^ bit) for i in range(CHIPS)]) for bit in (a, b, a | b)]
    return got


def close(value, got):
    return (value + got[0]) + (got[1] + got[2])


def spread_sum(value, beside=(None, None)):
    beside = list(beside)
    for n, bits in enumerate(((1, 2), (4, 8))):
        got, beside[n] = together(phase(value, bits), beside[n])
        value = close(value, got)
    return value + to_sibling(value), beside


def shards(
    x_in,
    cotangent,
    seq_lengths,
    weights,
    momentum,
    left_stat,
    right_stat,
    left_root,
    right_root,
    vectors,
    vector_sq,
):
    core = lax.axis_index("wt").astype(jnp.int32)
    place = lax.axis_index("seq").astype(jnp.int32)
    z, here = place // PLANE, place % PLANE
    first_core = core == 0
    rows = x_in.shape[0]
    local_count = weights.shape[0]
    quad_count = local_count // 4
    first_quad = (place * CORES + core) * quad_count

    kept, sent = split_weights(core, first_quad, weights)
    quads, wide = gather_weights(
        jnp.stack([kept, to_sibling(sent)]), z, here, core, widen(momentum, left_root, right_root)
    )

    both_x = jnp.concatenate([x_in, to_sibling(x_in)], axis=0)
    both_cot = jnp.concatenate([cotangent, to_sibling(cotangent)], axis=0)
    starts = jnp.stack([place * CORES + core, place * CORES + 1 - core]) * rows
    places = (starts[:, None] + jnp.arange(rows, dtype=jnp.int32)[None, :]).reshape(-1)
    keep_one, keep_two = keep_masks(places, seq_lengths)
    lane = jnp.arange(LANES)[None, :]
    keep = jnp.where(lane == 0, keep_one, jnp.where(lane == 1, keep_two, 0.0))
    taps = take(vectors[2:].reshape(3, IN_ROWS, 2, HALF), core, 2).reshape(3, D_HALF)

    hidden_both = both_x.astype(jnp.float32)
    scale_both = rms_scale(hidden_both)
    normed = (hidden_both * scale_both * vectors[0]).astype(jnp.bfloat16)
    hidden_in, scale_one = hidden_both[:rows], scale_both[:rows]
    mixed = mix(normed, quads)
    ends = jnp.stack([mixed[rows - 2 : rows], mixed[-2:]])
    ends = ends[:, :, :D_HALF] * ends[:, :, 2 * D_HALF :]
    carried = send(jnp.where(first_core, ends[1], ends[0]), [(i, i + 1) for i in range(CHIPS - 1)])
    halos = jnp.stack(
        [jnp.where(first_core, carried, ends[1]), jnp.where(first_core, ends[0], carried)]
    )
    conv_out, gated_out, part, other = conv_forward(mixed, halos, keep, taps, quads)
    middle = hidden_in + part + to_sibling(other)
    scale_two = rms_scale(middle)
    own_two = (middle * scale_two * vectors[1]).astype(jnp.bfloat16)
    other_two = to_sibling(own_two)
    activated, grad_gate, grad_up, part, other = ff_pass(own_two, other_two, both_cot, quads)
    near_grads, grad_w_down = down_first(activated, both_cot)
    grad_normed_two, grad_w_down = together(part + to_sibling(other), grad_w_down)
    gain_two_grad, middle_term = norm_back(middle, scale_two, vectors[1], grad_normed_two)
    grad_middle = cotangent.astype(jnp.float32) + middle_term
    own_branch = grad_middle.astype(jnp.bfloat16)
    grad_w_out, grad_conv, grad_output, heads, tap_grads = conv_back(
        own_branch, to_sibling(own_branch), mixed, conv_out, gated_out, halos, keep, taps, quads
    )
    from_after = send(
        jnp.where(first_core, heads[0], heads[1]), [(i + 1, i) for i in range(CHIPS - 1)]
    )
    tails = jnp.stack(
        [jnp.where(first_core, heads[1], from_after), jnp.where(first_core, from_after, heads[0])]
    )
    normed_two = jnp.concatenate([own_two, other_two], axis=0)
    near_grads, grad_w_gate = down_last(normed_two, activated, grad_gate, both_cot, near_grads)
    near_grads, grad_mixed, *corners = mix_back(
        jnp.stack([z, here]), grad_conv, grad_output, mixed, normed, tails, keep, taps,
        grad_w_out, grad_w_gate, near_grads,
    )
    near_grads, grad_w_down = together(near_grads, grad_w_down)
    far_grads = ff_grads(normed_two, grad_gate, grad_up, grad_w_down)

    def meanwhile(activated, grad_mixed):
        part, other = ff_out(activated, quads)
        out_act = (middle + part + to_sibling(other)).astype(jnp.bfloat16)
        part, other = mix_rest(grad_mixed, quads)
        grad_normed = part + to_sibling(other)
        gain_one_grad, input_term = norm_back(hidden_in, scale_one, vectors[0], grad_normed)
        tap_part = jnp.where(
            jnp.arange(2).reshape(1, 1, 2, 1) == core, tap_grads.reshape(3, IN_ROWS, 1, HALF), 0.0
        ).reshape(3, D)
        vector_part = jnp.concatenate(
            [gain_one_grad[None], gain_two_grad[None], tap_part], axis=0
        )
        return out_act, grad_middle + input_term, vector_part

    kept, sent, (out_act, in_grad, vector_part) = reduce_grads(
        near_grads, far_grads, corners, z, here, core, meanwhile, (activated, grad_mixed)
    )
    got = to_sibling(sent)

    new_momentum, precond, sums, kind_part = step_blocks(
        core, first_quad, kept, got, *wide, momentum
    )
    vector_rows = vector_part.reshape(-1, LANES)
    summed, (new_left, new_right) = spread_sum(
        jnp.concatenate([vector_rows, kind_part], axis=0),
        (stat_blocks(sums, left_stat, False), stat_blocks(sums, right_stat, True)),
    )
    vector_grads = summed[: vector_rows.shape[0]].reshape(vectors.shape)
    new_vector_sq = DECAY * vector_sq + (1.0 - DECAY) * vector_grads * vector_grads
    new_vectors = vectors - VEC_RATE * vector_grads * lax.rsqrt(new_vector_sq)
    kind_sum = jnp.sum(summed[vector_rows.shape[0] :], axis=1)[:KINDS]
    in_end, out_end, gate_end, up_end = block_bounds()
    kind_total = jnp.array(
        [in_end, out_end - in_end, gate_end - out_end, up_end - gate_end, BLOCKS - up_end],
        jnp.float32,
    ) * (BS * BS)
    kind_scale = lax.rsqrt(kind_sum / kind_total + MEAN_EPS)
    block_kinds = kind_of(first_quad + jnp.arange(local_count, dtype=jnp.int32) // 4)
    one_hot = (block_kinds[:, None] == jnp.arange(KINDS)[None, :]).astype(jnp.float32)
    block_scale = jnp.sum(one_hot * kind_scale[None, :], axis=1)
    new_weights = weights - RATE * block_scale[:, None] * precond
    return (
        out_act,
        in_grad,
        new_weights,
        new_weights.astype(jnp.bfloat16),
        new_momentum,
        new_left,
        new_right,
        vector_grads,
        new_vector_sq,
        new_vectors,
    )


def solution(mesh):
    body = shards if (mesh.shape["seq"], mesh.shape["wt"]) == (CHIPS, CORES) else shards_any
    return jax.shard_map(
        body,
        mesh=mesh,
        in_specs=(
            P(("seq", "wt"), None),
            P(("seq", "wt"), None),
            P(),
            P(("seq", "wt"), None),
            P(("seq", "wt"), None),
            P(("seq", "wt"), None),
            P(("seq", "wt"), None),
            P(("seq", "wt"), None),
            P(("seq", "wt"), None),
            P(),
            P(),
        ),
        out_specs=(
            P(("seq", "wt"), None),
            P(("seq", "wt"), None),
            P(("seq", "wt"), None),
            P(("seq", "wt"), None),
            P(("seq", "wt"), None),
            P(("seq", "wt"), None),
            P(("seq", "wt"), None),
            P(),
            P(),
            P(),
        ),
        check_vma=False,
    )
```
